512 devices in a mesh: dp: 32 (over x, y, core), tensor: 16 (over z).
Axes of the slice: x: 4, y: 4, z: 16, core: 2. Of those that a mesh axis runs over, the one named last changes fastest.
Arguments:
- gate_pre: bfloat16 [4096, 26624], P('dp', 'tensor'), may hold values from -6 to 6
- up_pre: bfloat16 [4096, 26624], P('dp', 'tensor'), may hold values from -6 to 6
- grad_rot: bfloat16 [4096, 26624], P('dp', 'tensor'), may hold values from -6 to 6
- grad_out: bfloat16 [4096, 8192], P('dp', 'tensor'), may hold values from -0.119628906 to 0.119628906
- latent_weight: bfloat16 [26624, 8192], P('dp', 'tensor'), may hold values from -0.0390625 to 0.0390625
- clip_codes: int32 [8192], P('tensor'), may hold values from 20 to 139
- bits: int32 [8192], P('tensor'), may hold values from 3 to 8
Outputs:
- grad_gate: bfloat16 [4096, 26624], P('dp', 'tensor')
- grad_up: bfloat16 [4096, 26624], P('dp', 'tensor')
- grad_weight: bfloat16 [26624, 8192], P('dp', 'tensor')
The draws below stay inside these ranges and needn't reach their ends.
All inputs are finite; a program needn't handle non-finite values.
Results may differ from the reference program's by a relative error of at most 0.014.
Values may be sent and summed in bfloat16 or wider, within the bound.
A program may use at most 64 MiB of HBM per device.

```python
import jax
import jax.numpy as jnp
from jax import lax

HAD = 1024
NBLK = 26
D = 8192
FF = 26624
TOKENS = 4096


def with_ends(entries, stream_key, least, largest):
    extent = entries.shape
    spot = [jax.random.randint(jax.random.fold_in(stream_key, axis), (), 0, extent[axis]) for axis in range(len(extent))]
    entries = entries.at[tuple(spot)].set(least)
    longest = extent.index(max(extent))
    spot[longest] = (spot[longest] + 1) % extent[longest]
    return entries.at[tuple(spot)].set(largest)


def level_of(key, shape, pieces, smallest, top_value):
    factor_of = 1.0
    for dim, shards_of in pieces:
        draws = jax.random.uniform(jax.random.fold_in(jax.random.fold_in(key, 6), dim), (shards_of,), jnp.float32, smallest / len(pieces), top_value / len(pieces))
        factor_of = factor_of * jnp.repeat(jnp.exp(draws), shape[dim] // shards_of).reshape((-1,) + (1,) * (len(shape) - 1 - dim))
    return factor_of


def scatter_about(stream_key, extent, width, most, cuts=(), held_as=jnp.bfloat16):
    level = level_of(stream_key, extent, cuts, -0.22, 0.18) if cuts else 1.0
    entries = jax.random.normal(stream_key, extent, jnp.float32) * width * level
    return jnp.minimum(jnp.maximum(entries, -most), most).astype(held_as)


def setup_inputs(seed: int = 0) -> dict:
    seeds = jax.random.split(jax.random.key(seed), 8)
    gate_pre = scatter_about(seeds[0], (TOKENS, FF), 1.0, 6.0, ((0, 32), (1, 16)))
    up_pre = scatter_about(seeds[1], (TOKENS, FF), 1.0, 6.0, ((0, 32), (1, 16)))
    grad_rot = scatter_about(seeds[2], (TOKENS, FF), 1.0, 6.0, ((0, 32), (1, 16)))
    grad_out = scatter_about(seeds[3], (TOKENS, D), 0.02, 0.119628906, ((0, 32), (1, 16)))
    latent_weight = scatter_about(seeds[4], (FF, D), FF ** -0.5, 0.0390625, ((0, 32), (1, 16)))
    clip_codes = with_ends(jax.random.randint(seeds[5], (D,), 20, 140), jax.random.fold_in(seeds[5], 1), 20, 139).astype(jnp.int32)
    bits = with_ends(jax.random.randint(seeds[6], (D,), 3, 9), jax.random.fold_in(seeds[6], 1), 3, 8).astype(jnp.int32)
    return {"gate_pre": gate_pre, "up_pre": up_pre, "grad_rot": grad_rot, "grad_out": grad_out, "latent_weight": latent_weight, "clip_codes": clip_codes, "bits": bits}


def sign_table(order):
    row_ids = jnp.arange(order, dtype=jnp.int32)[:, None]
    col_ids = jnp.arange(order, dtype=jnp.int32)[None, :]
    parity = jnp.zeros((order, order), jnp.int32)
    for position in range(order.bit_length() - 1):
        parity = parity + (jnp.right_shift(row_ids, position) & 1) * (jnp.right_shift(col_ids, position) & 1)
    signs = (1 - 2 * (parity % 2)).astype(jnp.float32)
    return signs / jnp.sqrt(jnp.float32(order))

def rotate(values):
    rows_count = values.shape[0]
    total_bits = HAD.bit_length() - 1
    outer = 2 ** (total_bits // 2)
    inner = HAD // outer
    shaped = values.reshape(rows_count, outer, inner, NBLK)
    first = jnp.einsum('tabk,ca->tcbk', shaped, sign_table(outer), precision=lax.Precision.HIGHEST)
    second = jnp.einsum('tcbk,db->tcdk', first, sign_table(inner), precision=lax.Precision.HIGHEST)
    return second.reshape(rows_count, HAD * NBLK)

def reference(gate_pre, up_pre, grad_rot, grad_out, latent_weight, clip_codes, bits):
    gate_vals = gate_pre.astype(jnp.float32)
    up_vals = up_pre.astype(jnp.float32)
    sigmoid_gate = jax.nn.sigmoid(gate_vals)
    hidden = (gate_vals * sigmoid_gate * up_vals).astype(jnp.bfloat16)
    rotated = rotate(hidden.astype(jnp.float32)).astype(jnp.bfloat16)
    levels = jnp.left_shift(jnp.int32(1), bits - 1) - 1
    clip_bound = clip_codes.astype(jnp.float32) * levels.astype(jnp.float32) / 65536.0
    row_groups = 16
    group_rows = HAD * NBLK // row_groups
    rotated_groups = rotated.T.reshape(row_groups, group_rows, TOKENS)
    weight_groups = latent_weight.reshape(row_groups, group_rows, D)

    def weight_block(pair):
        rows_rot, rows_weight = pair
        weight_sum = jnp.dot(rows_rot, grad_out, preferred_element_type=jnp.float32)
        inside = jnp.abs(rows_weight.astype(jnp.float32)) <= clip_bound[None, :]
        return jnp.where(inside, weight_sum, 0.0).astype(jnp.bfloat16)
    grad_weight = lax.map(weight_block, (rotated_groups, weight_groups)).reshape(HAD * NBLK, D)
    grad_hidden = rotate(grad_rot.astype(jnp.float32))
    grad_gate = (grad_hidden * up_vals * sigmoid_gate * (1.0 + gate_vals * (1.0 - sigmoid_gate))).astype(jnp.bfloat16)
    grad_up = (grad_hidden * gate_vals * sigmoid_gate).astype(jnp.bfloat16)
    return (grad_gate, grad_up, grad_weight)
```

```python
import jax
import jax.numpy as jnp
import numpy as np
from jax import lax
from jax.experimental import pallas as pl
from jax.experimental.pallas import tpu as pltpu
from jax.sharding import PartitionSpec as P

HAD = 1024
NBLK = 26
MESH = pl.DeviceIdType.MESH
BF = jnp.bfloat16
F32 = jnp.float32

ZN = 16
XY = 16
TOK = 128
UN = 1664
COL = 32
HALF = 896


def local_table():
    table = np.array([[1.0]])
    for _ in range(6):
        table = np.block([[table, table], [table, -table]])
    return np.kron(table / 8.0, np.eye(NBLK)).astype(jnp.bfloat16)


def hint(value, multiple):
    return pl.multiple_of(value, multiple)


CHUNKS = ((0, 896), (896, 384), (1280, 384))
PIECES = (
    ((0, 0, 0, 896, 0), (1, 1, 768, 128, 0)),
    ((2, 1, 896, 384, 128),),
    ((3, 1, 1280, 384, 512),),
)


def rotate16(src, dst, first, width):
    def tile(t, carry):
        lanes = pl.ds(hint(t * 128, 128), 128)
        vals = [src[j, :, lanes].astype(F32) for j in range(16)]
        for bit in range(4):
            step = 1 << bit
            for j in range(16):
                if not j & step:
                    low, high = vals[j], vals[j | step]
                    vals[j], vals[j | step] = low + high, low - high
        for j in range(16):
            dst[j, :, lanes] = (vals[j] * 0.25).astype(BF)
        return carry

    lax.fori_loop(first // 128, (first + width) // 128, tile, 0)


def kernel(
    gate, up, grot, gout, bound, latent_hbm, table_hbm, gg, gu, gw,
    acts, outs, part, send, other, own, got, turned, landed, hid, fin, fturn, fback,
    bt, table, latent, flipped, load_sem, ring_s, ring_r, f_s, f_r, fb_s, fb_r, b_s, b_r, e_s, e_r, g_s, g_r, z_s, z_r,
):
    i = lax.axis_index("dp")
    z = lax.axis_index("tensor")
    c = i % 2
    xy = i // 2
    x, y = xy // 4, xy % 4
    k_me = z // 2
    active = z % 2 == c

    def remote(src, dst, ssem, rsem, dp, zz):
        return pltpu.make_async_remote_copy(
            src_ref=src, dst_ref=dst, send_sem=ssem, recv_sem=rsem,
            device_id=(dp, zz), device_id_type=MESH,
        )

    load_table = pltpu.make_async_copy(table_hbm, table, load_sem.at[0])
    load_latent = pltpu.make_async_copy(latent_hbm, latent, load_sem.at[1])
    load_table.start()
    load_latent.start()

    barrier = pltpu.get_barrier_semaphore()

    def hail_z(off, carry):
        pl.semaphore_signal(barrier, inc=1, device_id=(i, (z + off) % ZN), device_id_type=MESH)
        return carry

    def hail_xy(off, carry):
        pl.semaphore_signal(barrier, inc=1, device_id=((i + off) % 32, z), device_id_type=MESH)
        return carry

    lax.fori_loop(1, ZN, hail_z, 0)
    lax.fori_loop(1, 32, hail_xy, 0)

    def make_hidden(t, carry):
        lanes = pl.ds(hint(t * 128, 128), 128)
        g = gate[:, lanes].astype(F32)
        u = up[:, lanes].astype(F32)
        hid[:, lanes] = (g * jax.nn.sigmoid(g) * u).astype(BF)
        return carry

    for t in range(4):
        lanes = slice(128 * t, 128 * (t + 1))
        bt[lanes, :] = gout[:, lanes].astype(F32).T.astype(BF)
    lax.fori_loop(0, UN // 128, make_hidden, 0)
    pl.semaphore_wait(barrier, ZN - 1 + 31)

    def f_copy(k):
        rows = pl.ds(hint(16 * k, 16), 16)
        return remote(grot.at[rows, :], fin.at[z], f_s.at[k], f_r.at[z], i, 2 * k + c)

    def f_start(j, carry):
        k = (k_me + 4 + j) % 8

        @pl.when(2 * k + c != z)
        def _():
            f_copy(k).start()

        return carry

    lax.fori_loop(0, 3, f_start, 0)

    def b_copy(off):
        peer = (xy + off) % XY
        return remote(
            bt.at[pl.ds(hint(COL * peer, COL), COL), :],
            outs.at[pl.ds(hint(COL * z, COL), COL), pl.ds(hint(TOK * xy, TOK), TOK)],
            b_s.at[off], b_r.at[xy], 2 * peer + c, z,
        )

    def b_start(off, carry):
        b_copy(off).start()
        return carry

    lax.fori_loop(1, XY, b_start, 0)
    outs[pl.ds(hint(COL * z, COL), COL), pl.ds(hint(TOK * xy, TOK), TOK)] = bt[
        pl.ds(hint(COL * xy, COL), COL), :
    ]

    @pl.when(active)
    def _():
        fin[z] = grot[pl.ds(hint(16 * k_me, 16), 16), :]

    load_table.wait()
    mine = pl.ds(hint(TOK * xy, TOK), TOK)

    def turn_hidden(t, carry):
        lanes = pl.ds(hint(t * 256, 256), 256)
        acts[mine, lanes] = jnp.dot(hid[...], table[:, lanes], preferred_element_type=F32).astype(BF)
        return carry

    lax.fori_loop(0, UN // 256, turn_hidden, 0)
    acts[mine, UN - 128 :] = jnp.dot(
        hid[...], table[:, UN - 128 :], preferred_element_type=F32
    ).astype(BF)

    place = (4 * x + (x + y) % 4, 4 * y + (x + y) % 4, z)

    def block_of(r, n):
        major, minor = n // 4, (n % 4 + 3 * (n // 4)) % 4
        return (4 * major + minor, 4 * minor + major, n)[r]

    def ring_copy(r, d, s, u):
        n = place[r]
        origin = (n + 16 - s) % 16 if d == 0 else (n + s) % 16
        peer = (n + 1) % 16 if d == 0 else (n + 15) % 16
        blk = block_of(r, origin)
        if r < 2:
            ref = acts.at[pl.ds(hint(TOK * blk + 64 * r + 32 * u, 32), 32), :]
            dp, zz = 2 * block_of(r, peer) + c, z
        else:
            ref = outs.at[pl.ds(hint(COL * blk + 16 * u, 16), 16), :]
            dp, zz = i, peer
        return remote(ref, ref, ring_s.at[r, d, s, u], ring_r.at[r, d, s, u], dp, zz)

    def ring_wait(r, d, s, u):
        n = place[r]
        origin = (n + 15 - s) % 16 if d == 0 else (n + s + 1) % 16
        blk = block_of(r, origin)
        if r < 2:
            ref = acts.at[pl.ds(hint(TOK * blk + 64 * r + 32 * u, 32), 32), :]
        else:
            ref = outs.at[pl.ds(hint(COL * blk + 16 * u, 16), 16), :]
        src = (n + 15) % 16 if d == 0 else (n + 1) % 16
        dp, zz = (2 * block_of(r, src) + c, z) if r < 2 else (i, src)
        remote(ref, ref, ring_s.at[r, d, s, u], ring_r.at[r, d, s, u], dp, zz).wait_recv()

    for u in range(2):
        for r in range(2):
            for d in range(2):
                ring_copy(r, d, 0, u).start()

    def b_wait(off, carry):
        src = (xy + off) % XY
        ref = outs.at[pl.ds(hint(COL * z, COL), COL), pl.ds(hint(TOK * src, TOK), TOK)]
        remote(ref, ref, b_s.at[off], b_r.at[src], 2 * src + c, z).wait_recv()
        return carry

    lax.fori_loop(1, XY, b_wait, 0)
    for u in range(2):
        for d in range(2):
            ring_copy(2, d, 0, u).start()

    def ring_step(s, carry):
        for u in range(2):
            for r in (2, 0, 1):
                for d in range(2):
                    ring_wait(r, d, s - 1, u)
                    ring_copy(r, d, s, u).start()
        return carry

    def ring_step_f(s, carry):
        f_start(s + 2, 0)
        return ring_step(s, carry)

    lax.fori_loop(1, 6, ring_step_f, 0)
    ring_step(6, 0)
    for u in range(2):
        for r in (2, 0, 1):
            for d in range(2):
                ring_wait(r, d, 6, u)
                if u == d:
                    ring_copy(r, d, 7, u).start()
    for r in (2, 0, 1):
        for d in range(2):
            ring_wait(r, d, 7, d)

    def fb_copy(dest):
        return remote(
            fturn.at[dest], fback.at[pl.ds(hint(16 * k_me, 16), 16), :],
            fb_s.at[dest], fb_r.at[k_me], i, dest,
        )

    @pl.when(active)
    def _():
        def f_wait(off, carry):
            src = (z + off) % ZN
            remote(fin.at[src], fin.at[src], f_s.at[0], f_r.at[src], i, src).wait_recv()
            return carry

        lax.fori_loop(1, ZN, f_wait, 0)
        rotate16(fin, fturn, 0, UN)

        def fb_start(off, carry):
            fb_copy((z + 7 + off) % ZN).start()
            return carry

        lax.fori_loop(1, 9, fb_start, 0)

        def fb_start2(off, carry):
            fb_copy((z + off) % ZN).start()
            return carry

        lax.fori_loop(1, 8, fb_start2, 0)
        fback[pl.ds(hint(16 * k_me, 16), 16), :] = fturn[z]

    def product(lanes, width):
        tile = jnp.dot(outs[...], acts[:, lanes], preferred_element_type=F32)
        tile = tile.reshape(ZN, COL, width)
        part[:, :, lanes] = tile
        send[:, :, lanes] = tile.astype(BF)

    def product_chunk(q):
        first, width = CHUNKS[q]

        def product_tile(t, carry):
            product(pl.ds(hint(first + t * 256, 128), 256), 256)
            return carry

        lax.fori_loop(0, width // 256, product_tile, 0)
        if width % 256:
            product(pl.ds(first + width - 128, 128), 128)

    def swap(q):
        lanes = pl.ds(*CHUNKS[q])
        return remote(
            send.at[:, pl.ds(hint(16 * (1 - c), 16), 16), lanes], other.at[:, :, lanes],
            e_s.at[q], e_r.at[q], 2 * xy + 1 - c, z,
        )

    def g_copy(q, dest):
        lanes = pl.ds(*CHUNKS[q])
        return remote(
            own.at[dest, :, lanes], got.at[z, :, lanes], g_s.at[q, dest], g_r.at[q, z], i, dest
        )

    def share(q):
        lanes = pl.ds(*CHUNKS[q])
        swap(q).wait_recv()

        def add_send(off, carry):
            j = (z + 8 + off) % ZN
            own[j, :, lanes] = (
                part[j, pl.ds(hint(16 * c, 16), 16), lanes] + other[j, :, lanes].astype(F32)
            ).astype(BF)

            @pl.when(j != z)
            def _():
                g_copy(q, j).start()

            return carry

        lax.fori_loop(0, ZN, add_send, 0)
        got[z, :, lanes] = own[z, :, lanes]

    product_chunk(0)
    swap(0).start()
    product_chunk(1)
    swap(1).start()
    share(0)
    product_chunk(2)
    swap(2).start()
    share(1)
    share(2)

    def fb_wait(k, carry):
        @pl.when(2 * k + c != z)
        def _():
            ref = fback.at[pl.ds(hint(16 * k, 16), 16), :]
            remote(ref, ref, fb_s.at[0], fb_r.at[k], i, 2 * k + c).wait_recv()

        return carry

    lax.fori_loop(0, 8, fb_wait, 0)

    def finish(lanes):
        gh = jnp.dot(fback[...], table[:, lanes], preferred_element_type=F32)
        g = gate[:, lanes].astype(F32)
        u = up[:, lanes].astype(F32)
        sg = jax.nn.sigmoid(g)
        gg[:, lanes] = (gh * u * sg * (1.0 + g * (1.0 - sg))).astype(BF)
        gu[:, lanes] = (gh * g * sg).astype(BF)

    def finish_tile(t, carry):
        finish(pl.ds(hint(t * 256, 256), 256))
        return carry

    lax.fori_loop(0, UN // 256, finish_tile, 0)
    finish(pl.ds(UN - 128, 128))

    def z_copy(piece, peer):
        p, core, first, width, at = piece
        return remote(
            turned.at[peer, :, pl.ds(first, width)],
            landed.at[pl.ds(hint(COL * xy + 16 * c, 16), 16), pl.ds(at, width)],
            z_s.at[p, peer], z_r.at[p, i], 2 * peer + core, z,
        )

    def g_wait_chunk(q):
        lanes = pl.ds(*CHUNKS[q])

        def g_wait(off, carry):
            src = (z + off) % ZN
            ref = got.at[src, :, lanes]
            remote(ref, ref, g_s.at[q, src], g_r.at[q, src], i, src).wait_recv()
            return carry

        lax.fori_loop(1, ZN, g_wait, 0)

    def z_send(piece):
        p, core, first, width, at = piece

        def z_start(off, carry):
            z_copy(piece, (xy + off) % XY).start()
            return carry

        lax.fori_loop(1, XY, z_start, 0)

        @pl.when(c == core)
        def _():
            landed[pl.ds(hint(COL * xy + 16 * c, 16), 16), at : at + width] = turned[
                xy, :, first : first + width
            ]

        @pl.when(c != core)
        def _():
            z_copy(piece, xy).start()

    def z_take(piece):
        p, core, first, width, at = piece

        @pl.when(c == core)
        def _():
            def z_wait(off, carry):
                src = (i + off) % 32
                ref = landed.at[pl.ds(hint(16 * src, 16), 16), pl.ds(at, width)]
                remote(ref, ref, z_s.at[p, 0], z_r.at[p, src], src, z).wait_recv()
                return carry

            lax.fori_loop(1, 32, z_wait, 0)

            def flip(t, carry):
                lanes = pl.ds(hint(t * 128, 128), 128)
                flipped[lanes, :] = landed[:, lanes].astype(F32).T
                return carry

            lax.fori_loop(at // 128, (at + width) // 128, flip, 0)

    for q in range(3):
        g_wait_chunk(q)
        rotate16(got, turned, *CHUNKS[q])
        for piece in PIECES[q]:
            z_send(piece)
        if q:
            for piece in PIECES[q - 1]:
                z_take(piece)
    for piece in PIECES[2]:
        z_take(piece)

    load_latent.wait()
    limit = bound[...]

    def mask(t, carry):
        rows = pl.ds(hint(t * 64, 64), 64)
        value = flipped[pl.ds(hint(t * 64 + 64 * c, 64), 64), :]
        inside = jnp.abs(latent[rows, :].astype(F32)) <= limit
        gw[rows, :] = jnp.where(inside, value, 0.0).astype(BF)
        return carry

    lax.fori_loop(0, 13, mask, 0)

    def ring_sent(s, carry):
        for r in range(3):
            for d in range(2):
                for u in range(2):
                    ring_copy(r, d, s, u).wait_send()
        return carry

    lax.fori_loop(0, 7, ring_sent, 0)
    for r in range(3):
        for d in range(2):
            ring_copy(r, d, 7, d).wait_send()

    def f_sent(k, carry):
        @pl.when(2 * k + c != z)
        def _():
            f_copy(k).wait_send()

        return carry

    lax.fori_loop(0, 8, f_sent, 0)

    def b_sent(off, carry):
        b_copy(off).wait_send()
        return carry

    lax.fori_loop(1, XY, b_sent, 0)

    @pl.when(active)
    def _():
        def fb_sent(off, carry):
            fb_copy((z + off) % ZN).wait_send()
            return carry

        lax.fori_loop(1, ZN, fb_sent, 0)

    def g_sent(off, carry):
        for q in range(3):
            g_copy(q, (z + off) % ZN).wait_send()
        return carry

    lax.fori_loop(1, ZN, g_sent, 0)

    def z_sent(off, carry):
        for pieces in PIECES:
            for piece in pieces:
                z_copy(piece, (xy + off) % XY).wait_send()
        return carry

    lax.fori_loop(1, XY, z_sent, 0)
    for q in range(3):
        swap(q).wait_send()
        for piece in PIECES[q]:

            @pl.when(c != piece[1])
            def _():
                z_copy(piece, xy).wait_send()


def local(gate_pre, up_pre, grad_rot, grad_out, latent_weight, clip_codes, bits):
    table = jnp.asarray(local_table())
    vmem = pl.BlockSpec(memory_space=pltpu.VMEM)
    dma = pltpu.SemaphoreType.DMA
    hbm = pl.BlockSpec(memory_space=pl.ANY)
    levels = jnp.left_shift(jnp.int32(1), bits - 1) - 1
    clip_bound = clip_codes.astype(F32) * levels.astype(F32) / 65536.0
    return pl.pallas_call(
        kernel,
        out_shape=(
            jax.ShapeDtypeStruct((TOK, UN), BF),
            jax.ShapeDtypeStruct((TOK, UN), BF),
            jax.ShapeDtypeStruct((832, 512), BF),
        ),
        in_specs=[vmem] * 5 + [hbm] * 2,
        out_specs=(vmem, vmem, vmem),
        scratch_shapes=[
            pltpu.VMEM((XY * TOK, UN), BF),
            pltpu.VMEM((512, XY * TOK), BF),
            pltpu.VMEM((ZN, COL, UN), F32),
            pltpu.VMEM((ZN, COL, UN), BF),
            pltpu.VMEM((ZN, 16, UN), BF),
            pltpu.VMEM((ZN, 16, UN), BF),
            pltpu.VMEM((ZN, 16, UN), BF),
            pltpu.VMEM((ZN, 16, UN), BF),
            pltpu.VMEM((512, HALF), BF),
            pltpu.VMEM((TOK, UN), BF),
            pltpu.VMEM((ZN, 16, UN), BF),
            pltpu.VMEM((ZN, 16, UN), BF),
            pltpu.VMEM((TOK, UN), BF),
            pltpu.VMEM((512, TOK), BF),
            pltpu.VMEM((UN, UN), BF),
            pltpu.VMEM((832, 512), BF),
            pltpu.VMEM((HALF, 512), F32),
            dma((2,)),
            dma((3, 2, 8, 2)), dma((3, 2, 8, 2)),
            dma((8,)), dma((ZN,)), dma((ZN,)), dma((8,)),
            dma((XY,)), dma((XY,)), dma((3,)), dma((3,)),
            dma((3, ZN)), dma((3, ZN)), dma((4, XY)), dma((4, 32)),
        ],
        compiler_params=pltpu.CompilerParams(
            collective_id=0, has_side_effects=True, vmem_limit_bytes=56 * 1024 * 1024
        ),
    )(gate_pre, up_pre, grad_rot, grad_out, clip_bound[None, :], latent_weight, table)


def solution(mesh):
    both = P("dp", "tensor")
    return jax.shard_map(
        local,
        mesh=mesh,
        in_specs=(both, both, both, both, both, P("tensor"), P("tensor")),
        out_specs=(both, both, both),
        check_vma=False,
    )
```

```python
import jax
import jax.numpy as jnp
import numpy as np
from jax import lax
from jax.experimental import pallas as pl
from jax.experimental.pallas import tpu as pltpu
from jax.sharding import PartitionSpec as P

HAD = 1024
NBLK = 26
MESH = pl.DeviceIdType.MESH
BF = jnp.bfloat16
F32 = jnp.float32

ZN = 16
XY = 16
TOK = 128
UN = 1664
COL = 32
HALF = 896


def local_table():
    table = np.array([[1.0]])
    for _ in range(6):
        table = np.block([[table, table], [table, -table]])
    return np.kron(table / 8.0, np.eye(NBLK)).astype(jnp.bfloat16)


def hint(value, multiple):
    return pl.multiple_of(value, multiple)


CHUNKS = ((0, 896), (896, 384), (1280, 384))
PIECES = (
    ((0, 0, 0, 896, 0), (1, 1, 768, 128, 0)),
    ((2, 1, 896, 384, 128),),
    ((3, 1, 1280, 384, 512),),
)


def rotate16(src, dst, first, width):
    def tile(t, carry):
        lanes = pl.ds(hint(t * 128, 128), 128)
        vals = [src[j, :, lanes].astype(F32) for j in range(16)]
        for bit in range(4):
            step = 1 << bit
            for j in range(16):
                if not j & step:
                    low, high = vals[j], vals[j | step]
                    vals[j], vals[j | step] = low + high, low - high
        for j in range(16):
            dst[j, :, lanes] = (vals[j] * 0.25).astype(BF)
        return carry

    lax.fori_loop(first // 128, (first + width) // 128, tile, 0)


def kernel(
    gate, up, grot, gout, table_hbm, gh_out, gw_out,
    acts, outs, part, send, other, own, got, turned, landed, hid, fin, fturn, fback,
    bt, table, load_sem, ring_s, ring_r, f_s, f_r, fb_s, fb_r, b_s, b_r, e_s, e_r, g_s, g_r, z_s, z_r,
):
    i = lax.axis_index("dp")
    z = lax.axis_index("tensor")
    c = i & 1
    xy = i >> 1
    x, y = xy >> 2, xy & 3
    k_me = z >> 1
    active = (z & 1) == c

    def remote(src, dst, ssem, rsem, dp, zz):
        return pltpu.make_async_remote_copy(
            src_ref=src, dst_ref=dst, send_sem=ssem, recv_sem=rsem,
            device_id=(dp, zz), device_id_type=MESH,
        )

    load_table = pltpu.make_async_copy(table_hbm, table, load_sem)
    load_table.start()

    def taken(ref, sem):
        remote(ref, ref, load_sem, sem, i, z ^ 1).wait_recv()

    def gone(ref, sem):
        remote(ref, ref, sem, load_sem, i, z ^ 1).wait_send()

    barrier = pltpu.get_barrier_semaphore()

    def hail_z(off, carry):
        pl.semaphore_signal(barrier, inc=1, device_id=(i, (z + off) & 15), device_id_type=MESH)
        return carry

    def hail_xy(off, carry):
        pl.semaphore_signal(barrier, inc=1, device_id=((i + off) & 31, z), device_id_type=MESH)
        return carry

    lax.fori_loop(1, ZN, hail_z, 0)
    lax.fori_loop(1, 32, hail_xy, 0)

    def make_hidden(t, carry):
        lanes = pl.ds(hint(t * 128, 128), 128)
        g = gate[:, lanes].astype(F32)
        u = up[:, lanes].astype(F32)
        hid[:, lanes] = (g * jax.nn.sigmoid(g) * u).astype(BF)
        return carry

    for t in range(4):
        lanes = slice(128 * t, 128 * (t + 1))
        bt[lanes, :] = gout[:, lanes].astype(F32).T.astype(BF)
    lax.fori_loop(0, UN // 128, make_hidden, 0)
    pl.semaphore_wait(barrier, ZN - 1 + 31)

    def f_copy(k):
        rows = pl.ds(hint(16 * k, 16), 16)
        return remote(grot.at[rows, :], fin.at[z], f_s, f_r, i, 2 * k + c)

    def f_start(j, carry):
        k = (k_me + 4 + j) & 7

        @pl.when(2 * k + c != z)
        def _():
            f_copy(k).start()

        return carry

    lax.fori_loop(0, 3, f_start, 0)

    def b_copy(off):
        peer = (xy + off) & 15
        return remote(
            bt.at[pl.ds(hint(COL * peer, COL), COL), :],
            outs.at[pl.ds(hint(COL * z, COL), COL), pl.ds(hint(TOK * xy, TOK), TOK)],
            b_s, b_r, 2 * peer + c, z,
        )

    def b_start(off, carry):
        b_copy(off).start()
        return carry

    lax.fori_loop(1, XY, b_start, 0)
    outs[pl.ds(hint(COL * z, COL), COL), pl.ds(hint(TOK * xy, TOK), TOK)] = bt[
        pl.ds(hint(COL * xy, COL), COL), :
    ]

    @pl.when(active)
    def _():
        fin[z] = grot[pl.ds(hint(16 * k_me, 16), 16), :]

    load_table.wait()
    mine = pl.ds(hint(TOK * xy, TOK), TOK)

    def turn_hidden(t, carry):
        lanes = pl.ds(hint(t * 256, 256), 256)
        acts[mine, lanes] = jnp.dot(hid[...], table[:, lanes], preferred_element_type=F32).astype(BF)
        return carry

    lax.fori_loop(0, UN // 256, turn_hidden, 0)
    acts[mine, UN - 128 :] = jnp.dot(
        hid[...], table[:, UN - 128 :], preferred_element_type=F32
    ).astype(BF)

    place = (4 * x + ((x + y) & 3), 4 * y + ((x + y) & 3), z)

    def block_of(r, n):
        if r == 2:
            return n
        major = n >> 2
        minor = (n + 3 * major) & 3
        return 4 * major + minor if r == 0 else 4 * minor + major

    def ring_peer(r, n):
        return (i, n) if r == 2 else (2 * block_of(r, n) + c, z)

    peers = [[ring_peer(r, (place[r] + hop) & 15) for hop in (1, 15)] for r in range(3)]

    def ring_copy(r, d, s, u):
        blk = block_of(r, (place[r] + 16 - s if d == 0 else place[r] + s) & 15)
        if r < 2:
            ref = acts.at[pl.ds(hint(TOK * blk + 64 * r + 32 * u, 32), 32), :]
        else:
            ref = outs.at[pl.ds(hint(COL * blk + 16 * u, 16), 16), :]
        return remote(ref, ref, ring_s.at[r], ring_r.at[r, d, s, u], *peers[r][d])

    def ring_wait(r, d, s, u):
        taken(acts.at[pl.ds(0, 32), :] if r < 2 else outs.at[pl.ds(0, 16), :], ring_r.at[r, d, s, u])

    for u in range(2):
        for r in range(2):
            for d in range(2):
                ring_copy(r, d, 0, u).start()

    taken(outs.at[pl.ds(0, COL), pl.ds(0, TOK * (XY - 1))], b_r)
    for u in range(2):
        for d in range(2):
            ring_copy(2, d, 0, u).start()

    def ring_step(s, carry):
        for u in range(2):
            for r in (2, 0, 1):
                for d in range(2):
                    ring_wait(r, d, s - 1, u)
                    ring_copy(r, d, s, u).start()
        return carry

    def ring_step_f(s, carry):
        f_start(s + 2, 0)
        return ring_step(s, carry)

    lax.fori_loop(1, 6, ring_step_f, 0)
    ring_step(6, 0)
    for u in range(2):
        for r in (2, 0, 1):
            for d in range(2):
                ring_wait(r, d, 6, u)
                if u == d:
                    ring_copy(r, d, 7, u).start()
    for r in (2, 0, 1):
        for d in range(2):
            ring_wait(r, d, 7, d)

    def fb_copy(dest):
        return remote(
            fturn.at[dest], fback.at[pl.ds(hint(16 * k_me, 16), 16), :],
            fb_s, fb_r, i, dest,
        )

    @pl.when(active)
    def _():
        taken(fin.at[pl.ds(0, ZN - 1)], f_r)
        rotate16(fin, fturn, 0, UN)

        def fb_start(off, carry):
            fb_copy((z + 7 + off) & 15).start()
            return carry

        lax.fori_loop(1, 9, fb_start, 0)

        def fb_start2(off, carry):
            fb_copy((z + off) & 15).start()
            return carry

        lax.fori_loop(1, 8, fb_start2, 0)
        fback[pl.ds(hint(16 * k_me, 16), 16), :] = fturn[z]

    def product(lanes, width):
        tile = jnp.dot(outs[...], acts[:, lanes], preferred_element_type=F32)
        tile = tile.reshape(ZN, COL, width)
        part[:, :, lanes] = tile
        send[:, :, lanes] = tile.astype(BF)

    def product_chunk(q):
        first, width = CHUNKS[q]

        def product_tile(t, carry):
            product(pl.ds(hint(first + t * 256, 128), 256), 256)
            return carry

        lax.fori_loop(0, width // 256, product_tile, 0)
        if width % 256:
            product(pl.ds(first + width - 128, 128), 128)

    def swap(q):
        lanes = pl.ds(*CHUNKS[q])
        return remote(
            send.at[:, pl.ds(hint(16 * (1 - c), 16), 16), lanes], other.at[:, :, lanes],
            e_s, e_r.at[q], i ^ 1, z,
        )

    def g_copy(q, dest):
        lanes = pl.ds(*CHUNKS[q])
        return remote(
            own.at[dest, :, lanes], got.at[z, :, lanes], g_s, g_r.at[q], i, dest
        )

    def share(q):
        lanes = pl.ds(*CHUNKS[q])
        taken(other.at[:, :, lanes], e_r.at[q])

        def add_send(off, carry):
            j = (z + 8 + off) & 15
            own[j, :, lanes] = (
                part[j, pl.ds(hint(16 * c, 16), 16), lanes] + other[j, :, lanes].astype(F32)
            ).astype(BF)

            @pl.when(j != z)
            def _():
                g_copy(q, j).start()

            return carry

        lax.fori_loop(0, ZN, add_send, 0)
        got[z, :, lanes] = own[z, :, lanes]

    product_chunk(0)
    swap(0).start()
    product_chunk(1)
    swap(1).start()
    share(0)
    product_chunk(2)
    swap(2).start()
    share(1)
    share(2)

    @pl.when(active)
    def _():
        taken(fback.at[pl.ds(0, TOK - 16), :], fb_r)

    @pl.when(jnp.logical_not(active))
    def _():
        taken(fback, fb_r)

    def finish(lanes):
        gh_out[:, lanes] = jnp.dot(fback[...], table[:, lanes], preferred_element_type=F32).astype(BF)

    def finish_tile(t, carry):
        finish(pl.ds(hint(t * 256, 256), 256))
        return carry

    lax.fori_loop(0, UN // 256, finish_tile, 0)
    finish(pl.ds(UN - 128, 128))

    def z_copy(piece, peer):
        p, core, first, width, at = piece
        return remote(
            turned.at[peer, :, pl.ds(first, width)],
            landed.at[pl.ds(hint(COL * xy + 16 * c, 16), 16), pl.ds(at, width)],
            z_s.at[p], z_r.at[p], 2 * peer + core, z,
        )

    def g_wait_chunk(q):
        lanes = pl.ds(*CHUNKS[q])

        taken(got.at[pl.ds(0, ZN - 1), :, lanes], g_r.at[q])

    def z_send(piece):
        p, core, first, width, at = piece

        def z_start(off, carry):
            z_copy(piece, (xy + off) & 15).start()
            return carry

        lax.fori_loop(1, XY, z_start, 0)

        @pl.when(c == core)
        def _():
            landed[pl.ds(hint(COL * xy + 16 * c, 16), 16), at : at + width] = turned[
                xy, :, first : first + width
            ]

        @pl.when(c != core)
        def _():
            z_copy(piece, xy).start()

    def z_take(piece):
        p, core, first, width, at = piece

        @pl.when(c == core)
        def _():
            taken(landed.at[pl.ds(0, 496), pl.ds(at, width)], z_r.at[p])

            def flip(t, carry):
                lanes = pl.ds(hint(t * 128, 128), 128)
                gw_out[lanes, :] = landed[:, lanes].astype(F32).T.astype(BF)
                return carry

            lax.fori_loop(at // 128, (at + width) // 128, flip, 0)

    for q in range(3):
        g_wait_chunk(q)
        rotate16(got, turned, *CHUNKS[q])
        for piece in PIECES[q]:
            z_send(piece)
        if q:
            for piece in PIECES[q - 1]:
                z_take(piece)
    for piece in PIECES[2]:
        z_take(piece)

    for r in range(2):
        gone(acts.at[pl.ds(0, 64 * 15), :], ring_s.at[r])
    gone(outs.at[pl.ds(0, COL * 15), :], ring_s.at[2])
    gone(outs.at[pl.ds(0, COL), pl.ds(0, TOK * (XY - 1))], b_s)

    @pl.when(active)
    def _():
        gone(grot.at[pl.ds(0, TOK - 16), :], f_s)
        gone(fturn.at[pl.ds(0, ZN - 1)], fb_s)

    @pl.when(jnp.logical_not(active))
    def _():
        gone(grot, f_s)

    gone(other, e_s)
    gone(own.at[pl.ds(0, ZN - 1)], g_s)
    for pieces in PIECES:
        for p, core, first, width, at in pieces:

            @pl.when(c == core)
            def _():
                gone(turned.at[pl.ds(0, XY - 1), :, pl.ds(first, width)], z_s.at[p])

            @pl.when(c != core)
            def _():
                gone(turned.at[:, :, pl.ds(first, width)], z_s.at[p])


def local(gate_pre, up_pre, grad_rot, grad_out, latent_weight, clip_codes, bits):
    table = jnp.asarray(local_table())
    vmem = pl.BlockSpec(memory_space=pltpu.VMEM)
    hbm = pl.BlockSpec(memory_space=pl.ANY)
    dma = pltpu.SemaphoreType.DMA
    grad_hidden, summed = pl.pallas_call(
        kernel,
        out_shape=(
            jax.ShapeDtypeStruct((TOK, UN), BF),
            jax.ShapeDtypeStruct((HALF, 512), BF),
        ),
        in_specs=[vmem] * 4 + [hbm],
        out_specs=(vmem, vmem),
        scratch_shapes=[
            pltpu.VMEM((XY * TOK, UN), BF),
            pltpu.VMEM((512, XY * TOK), BF),
            pltpu.VMEM((ZN, COL, UN), F32),
            pltpu.VMEM((ZN, COL, UN), BF),
            pltpu.VMEM((ZN, 16, UN), BF),
            pltpu.VMEM((ZN, 16, UN), BF),
            pltpu.VMEM((ZN, 16, UN), BF),
            pltpu.VMEM((ZN, 16, UN), BF),
            pltpu.VMEM((512, HALF), BF),
            pltpu.VMEM((TOK, UN), BF),
            pltpu.VMEM((ZN, 16, UN), BF),
            pltpu.VMEM((ZN, 16, UN), BF),
            pltpu.VMEM((TOK, UN), BF),
            pltpu.VMEM((512, TOK), BF),
            pltpu.VMEM((UN, UN), BF),
            dma(()), dma((3,)), dma((3, 2, 8, 2)),
            dma(()), dma(()), dma(()), dma(()),
            dma(()), dma(()), dma(()), dma((3,)),
            dma(()), dma((3,)), dma((4,)), dma((4,)),
        ],
        compiler_params=pltpu.CompilerParams(
            collective_id=0, has_side_effects=True, vmem_limit_bytes=56 * 1024 * 1024
        ),
    )(gate_pre, up_pre, grad_rot, grad_out, table)
    core = lax.axis_index("dp") & 1
    rows = jnp.where(core == 1, summed[HALF - 832 :], summed[:832])
    levels = jnp.left_shift(jnp.int32(1), bits - 1) - 1
    clip_bound = clip_codes.astype(F32) * levels.astype(F32) / 65536.0
    inside = jnp.abs(latent_weight.astype(F32)) <= clip_bound[None, :]
    grad_weight = jnp.where(inside, rows, jnp.zeros((), BF))
    gate_vals, up_vals = gate_pre.astype(F32), up_pre.astype(F32)
    gh = grad_hidden.astype(F32)
    sg = jax.nn.sigmoid(gate_vals)
    grad_gate = (gh * up_vals * sg * (1.0 + gate_vals * (1.0 - sg))).astype(BF)
    grad_up = (gh * gate_vals * sg).astype(BF)
    return grad_gate, grad_up, grad_weight


def solution(mesh):
    both = P("dp", "tensor")
    return jax.shard_map(
        local,
        mesh=mesh,
        in_specs=(both, both, both, both, both, P("tensor"), P("tensor")),
        out_specs=(both, both, both),
        check_vma=False,
    )
```

```python
import jax
import jax.numpy as jnp
import numpy as np
from jax import lax
from jax.experimental import pallas as pl
from jax.experimental.pallas import tpu as pltpu
from jax.sharding import PartitionSpec as P

HAD = 1024
NBLK = 26
MESH = pl.DeviceIdType.MESH
BF = jnp.bfloat16
F32 = jnp.float32

ZN = 16
XY = 16
TOK = 128
UN = 1664
COL = 32
HALF = 896


def local_table():
    table = np.array([[1.0]])
    for _ in range(6):
        table = np.block([[table, table], [table, -table]])
    return np.kron(table / 8.0, np.eye(NBLK)).astype(jnp.bfloat16)


def hint(value, multiple):
    return pl.multiple_of(value, multiple)


CHUNKS = ((0, 896), (896, 384), (1280, 384))
PIECES = (
    ((0, 0, 0, 896, 0), (1, 1, 768, 128, 0)),
    ((2, 1, 896, 384, 128),),
    ((3, 1, 1280, 384, 512),),
)


def far_first(t):
    half = (t + 1) >> 1
    return (8 + half * (1 - 2 * (t & 1))) & 15


def rotate16(src, dst, first, width):
    def tile(t, carry):
        lanes = pl.ds(hint(t * 128, 128), 128)
        vals = [src[j, :, lanes].astype(F32) for j in range(16)]
        for bit in range(4):
            step = 1 << bit
            for j in range(16):
                if not j & step:
                    low, high = vals[j], vals[j | step]
                    vals[j], vals[j | step] = low + high, low - high
        for j in range(16):
            dst[j, :, lanes] = (vals[j] * 0.25).astype(BF)
        return carry

    lax.fori_loop(first // 128, (first + width) // 128, tile, 0)


def kernel(
    gate, up, grot, gout, table_hbm, gh_out, gw_out,
    acts, outs, part, send, other, own, got, turned, landed, hid, fin, fturn, fback,
    bt, table, load_sem, ring_s, ring_r, f_s, f_r, fb_s, fb_r, b_s, b_r, e_s, e_r, g_s, g_r, z_s, z_r,
):
    i = lax.axis_index("dp")
    z = lax.axis_index("tensor")
    c = i & 1
    xy = i >> 1
    x, y = xy >> 2, xy & 3
    k_me = z >> 1
    active = (z & 1) == c

    def remote(src, dst, ssem, rsem, dp, zz):
        return pltpu.make_async_remote_copy(
            src_ref=src, dst_ref=dst, send_sem=ssem, recv_sem=rsem,
            device_id=(dp, zz), device_id_type=MESH,
        )

    load_table = pltpu.make_async_copy(table_hbm, table, load_sem)
    load_table.start()

    def taken(ref, sem):
        remote(ref, ref, load_sem, sem, i, z ^ 1).wait_recv()

    def gone(ref, sem):
        remote(ref, ref, sem, load_sem, i, z ^ 1).wait_send()

    barrier = pltpu.get_barrier_semaphore()

    def hail_z(off, carry):
        pl.semaphore_signal(barrier, inc=1, device_id=(i, (z + off) & 15), device_id_type=MESH)
        return carry

    def hail_xy(off, carry):
        pl.semaphore_signal(barrier, inc=1, device_id=((i + off) & 31, z), device_id_type=MESH)
        return carry

    lax.fori_loop(1, ZN, hail_z, 0)
    lax.fori_loop(1, 32, hail_xy, 0)

    for t in range(4):
        lanes = slice(128 * t, 128 * (t + 1))
        bt[lanes, :] = gout[:, lanes].astype(F32).T.astype(BF)
    pl.semaphore_wait(barrier, ZN - 1 + 31)

    def f_copy(k):
        rows = pl.ds(hint(16 * k, 16), 16)
        return remote(grot.at[rows, :], fin.at[z], f_s, f_r, i, 2 * k + c)

    def f_start(j, carry):
        half = (j + 1) >> 1
        k = (k_me + 4 + half * (1 - 2 * (j & 1))) & 7

        @pl.when(2 * k + c != z)
        def _():
            f_copy(k).start()

        return carry

    lax.fori_loop(0, 3, f_start, 0)

    def b_copy(off):
        peer = (xy + 7 * off) & 15
        return remote(
            bt.at[pl.ds(hint(COL * peer, COL), COL), :],
            outs.at[pl.ds(hint(COL * z, COL), COL), pl.ds(hint(TOK * xy, TOK), TOK)],
            b_s, b_r, 2 * peer + c, z,
        )

    def b_start(off, carry):
        b_copy(off).start()
        return carry

    lax.fori_loop(1, XY, b_start, 0)
    outs[pl.ds(hint(COL * z, COL), COL), pl.ds(hint(TOK * xy, TOK), TOK)] = bt[
        pl.ds(hint(COL * xy, COL), COL), :
    ]

    @pl.when(active)
    def _():
        fin[z] = grot[pl.ds(hint(16 * k_me, 16), 16), :]

    def make_hidden(t, carry):
        lanes = pl.ds(hint(t * 128, 128), 128)
        g = gate[:, lanes].astype(F32)
        u = up[:, lanes].astype(F32)
        hid[:, lanes] = (g * jax.nn.sigmoid(g) * u).astype(BF)
        return carry

    lax.fori_loop(0, UN // 128, make_hidden, 0)
    load_table.wait()
    mine = pl.ds(hint(TOK * xy, TOK), TOK)

    def turn_hidden(t, carry):
        lanes = pl.ds(hint(t * 256, 256), 256)
        acts[mine, lanes] = jnp.dot(hid[...], table[:, lanes], preferred_element_type=F32).astype(BF)
        return carry

    lax.fori_loop(0, UN // 256, turn_hidden, 0)
    acts[mine, UN - 128 :] = jnp.dot(
        hid[...], table[:, UN - 128 :], preferred_element_type=F32
    ).astype(BF)

    place = (4 * x + ((x + y) & 3), 4 * y + ((x + y) & 3), z)

    def block_of(r, n):
        if r == 2:
            return n
        major = n >> 2
        minor = (n + 3 * major) & 3
        return 4 * major + minor if r == 0 else 4 * minor + major

    def ring_peer(r, n):
        return (i, n) if r == 2 else (2 * block_of(r, n) + c, z)

    peers = [[ring_peer(r, (place[r] + hop) & 15) for hop in (1, 15)] for r in range(3)]

    def ring_copy(r, d, s, u):
        blk = block_of(r, (place[r] + 16 - s if d == 0 else place[r] + s) & 15)
        if r < 2:
            ref = acts.at[pl.ds(hint(TOK * blk + 64 * r + 32 * u, 32), 32), :]
        else:
            ref = outs.at[pl.ds(hint(COL * blk + 16 * u, 16), 16), :]
        return remote(ref, ref, ring_s.at[r], ring_r.at[r, d, s, u], *peers[r][d])

    def ring_wait(r, d, s, u):
        taken(acts.at[pl.ds(0, 32), :] if r < 2 else outs.at[pl.ds(0, 16), :], ring_r.at[r, d, s, u])

    for u in range(2):
        for r in range(2):
            for d in range(2):
                ring_copy(r, d, 0, u).start()

    taken(outs.at[pl.ds(0, COL), pl.ds(0, TOK * (XY - 1))], b_r)
    for u in range(2):
        for d in range(2):
            ring_copy(2, d, 0, u).start()

    def ring_step(s, carry):
        for u in range(2):
            for r in (2, 0, 1):
                for d in range(2):
                    ring_wait(r, d, s - 1, u)
                    ring_copy(r, d, s, u).start()
        return carry

    def ring_step_f(s, carry):
        f_start(s + 2, 0)
        return ring_step(s, carry)

    lax.fori_loop(1, 6, ring_step_f, 0)
    ring_step(6, 0)
    for u in range(2):
        for r in (2, 0, 1):
            for d in range(2):
                ring_wait(r, d, 6, u)
                if u == d:
                    ring_copy(r, d, 7, u).start()
    for r in (2, 0, 1):
        for d in range(2):
            ring_wait(r, d, 7, d)

    def fb_copy(dest):
        return remote(
            fturn.at[dest], fback.at[pl.ds(hint(16 * k_me, 16), 16), :],
            fb_s, fb_r, i, dest,
        )

    @pl.when(active)
    def _():
        taken(fin.at[pl.ds(0, ZN - 1)], f_r)
        rotate16(fin, fturn, 0, UN)

        def fb_start(t, carry):
            fb_copy((z + far_first(t)) & 15).start()
            return carry

        lax.fori_loop(0, ZN - 1, fb_start, 0)
        fback[pl.ds(hint(16 * k_me, 16), 16), :] = fturn[z]

    def product(lanes, width):
        tile = jnp.dot(outs[...], acts[:, lanes], preferred_element_type=F32)
        tile = tile.reshape(ZN, COL, width)
        part[:, :, lanes] = tile
        send[:, :, lanes] = tile.astype(BF)

    def product_chunk(q):
        first, width = CHUNKS[q]

        def product_tile(t, carry):
            product(pl.ds(hint(first + t * 256, 128), 256), 256)
            return carry

        lax.fori_loop(0, width // 256, product_tile, 0)
        if width % 256:
            product(pl.ds(first + width - 128, 128), 128)

    def swap(q):
        lanes = pl.ds(*CHUNKS[q])
        return remote(
            send.at[:, pl.ds(hint(16 * (1 - c), 16), 16), lanes], other.at[:, :, lanes],
            e_s, e_r.at[q], i ^ 1, z,
        )

    def g_copy(q, dest):
        lanes = pl.ds(*CHUNKS[q])
        return remote(
            own.at[dest, :, lanes], got.at[z, :, lanes], g_s, g_r.at[q], i, dest
        )

    def share(q):
        lanes = pl.ds(*CHUNKS[q])
        taken(other.at[:, :, lanes], e_r.at[q])

        def add_send(t, carry):
            j = (z + far_first(t)) & 15
            own[j, :, lanes] = (
                part[j, pl.ds(hint(16 * c, 16), 16), lanes] + other[j, :, lanes].astype(F32)
            ).astype(BF)

            @pl.when(t < ZN - 1)
            def _():
                g_copy(q, j).start()

            return carry

        lax.fori_loop(0, ZN, add_send, 0)
        got[z, :, lanes] = own[z, :, lanes]

    product_chunk(0)
    swap(0).start()
    product_chunk(1)
    swap(1).start()
    share(0)
    product_chunk(2)
    swap(2).start()
    share(1)
    share(2)

    @pl.when(active)
    def _():
        taken(fback.at[pl.ds(0, TOK - 16), :], fb_r)

    @pl.when(jnp.logical_not(active))
    def _():
        taken(fback, fb_r)

    def finish(lanes):
        gh_out[:, lanes] = jnp.dot(fback[...], table[:, lanes], preferred_element_type=F32).astype(BF)

    def finish_tile(t, carry):
        finish(pl.ds(hint(t * 256, 256), 256))
        return carry

    lax.fori_loop(0, UN // 256, finish_tile, 0)
    finish(pl.ds(UN - 128, 128))

    def z_copy(piece, peer):
        p, core, first, width, at = piece
        return remote(
            turned.at[peer, :, pl.ds(first, width)],
            landed.at[pl.ds(hint(COL * xy + 16 * c, 16), 16), pl.ds(at, width)],
            z_s.at[p], z_r.at[p], 2 * peer + core, z,
        )

    def g_wait_chunk(q):
        lanes = pl.ds(*CHUNKS[q])

        taken(got.at[pl.ds(0, ZN - 1), :, lanes], g_r.at[q])

    def z_send(piece):
        p, core, first, width, at = piece

        def z_start(off, carry):
            z_copy(piece, (xy + 7 * off) & 15).start()
            return carry

        lax.fori_loop(1, XY, z_start, 0)

        @pl.when(c == core)
        def _():
            landed[pl.ds(hint(COL * xy + 16 * c, 16), 16), at : at + width] = turned[
                xy, :, first : first + width
            ]

        @pl.when(c != core)
        def _():
            z_copy(piece, xy).start()

    def z_take(piece):
        p, core, first, width, at = piece

        @pl.when(c == core)
        def _():
            taken(landed.at[pl.ds(0, 496), pl.ds(at, width)], z_r.at[p])

            def flip(t, carry):
                lanes = pl.ds(hint(t * 128, 128), 128)
                gw_out[lanes, :] = landed[:, lanes].astype(F32).T.astype(BF)
                return carry

            lax.fori_loop(at // 128, (at + width) // 128, flip, 0)

    for q in range(3):
        g_wait_chunk(q)
        rotate16(got, turned, *CHUNKS[q])
        for piece in PIECES[q]:
            z_send(piece)
        if q:
            for piece in PIECES[q - 1]:
                z_take(piece)
    for piece in PIECES[2]:
        z_take(piece)

    for r in range(2):
        gone(acts.at[pl.ds(0, 64 * 15), :], ring_s.at[r])
    gone(outs.at[pl.ds(0, COL * 15), :], ring_s.at[2])
    gone(outs.at[pl.ds(0, COL), pl.ds(0, TOK * (XY - 1))], b_s)

    @pl.when(active)
    def _():
        gone(grot.at[pl.ds(0, TOK - 16), :], f_s)
        gone(fturn.at[pl.ds(0, ZN - 1)], fb_s)

    @pl.when(jnp.logical_not(active))
    def _():
        gone(grot, f_s)

    gone(other, e_s)
    gone(own.at[pl.ds(0, ZN - 1)], g_s)
    for pieces in PIECES:
        for p, core, first, width, at in pieces:

            @pl.when(c == core)
            def _():
                gone(turned.at[pl.ds(0, XY - 1), :, pl.ds(first, width)], z_s.at[p])

            @pl.when(c != core)
            def _():
                gone(turned.at[:, :, pl.ds(first, width)], z_s.at[p])


def local(gate_pre, up_pre, grad_rot, grad_out, latent_weight, clip_codes, bits):
    table = jnp.asarray(local_table())
    vmem = pl.BlockSpec(memory_space=pltpu.VMEM)
    hbm = pl.BlockSpec(memory_space=pl.ANY)
    dma = pltpu.SemaphoreType.DMA
    grad_hidden, summed = pl.pallas_call(
        kernel,
        out_shape=(
            jax.ShapeDtypeStruct((TOK, UN), BF),
            jax.ShapeDtypeStruct((HALF, 512), BF),
        ),
        in_specs=[vmem] * 4 + [hbm],
        out_specs=(vmem, vmem),
        scratch_shapes=[
            pltpu.VMEM((XY * TOK, UN), BF),
            pltpu.VMEM((512, XY * TOK), BF),
            pltpu.VMEM((ZN, COL, UN), F32),
            pltpu.VMEM((ZN, COL, UN), BF),
            pltpu.VMEM((ZN, 16, UN), BF),
            pltpu.VMEM((ZN, 16, UN), BF),
            pltpu.VMEM((ZN, 16, UN), BF),
            pltpu.VMEM((ZN, 16, UN), BF),
            pltpu.VMEM((512, HALF), BF),
            pltpu.VMEM((TOK, UN), BF),
            pltpu.VMEM((ZN, 16, UN), BF),
            pltpu.VMEM((ZN, 16, UN), BF),
            pltpu.VMEM((TOK, UN), BF),
            pltpu.VMEM((512, TOK), BF),
            pltpu.VMEM((UN, UN), BF),
            dma(()), dma((3,)), dma((3, 2, 8, 2)),
            dma(()), dma(()), dma(()), dma(()),
            dma(()), dma(()), dma(()), dma((3,)),
            dma(()), dma((3,)), dma((4,)), dma((4,)),
        ],
        compiler_params=pltpu.CompilerParams(
            collective_id=0, has_side_effects=True, vmem_limit_bytes=56 * 1024 * 1024
        ),
    )(gate_pre, up_pre, grad_rot, grad_out, table)
    core = lax.axis_index("dp") & 1
    rows = jnp.where(core == 1, summed[HALF - 832 :], summed[:832])
    levels = jnp.left_shift(jnp.int32(1), bits - 1) - 1
    clip_bound = clip_codes.astype(F32) * levels.astype(F32) / 65536.0
    inside = jnp.abs(latent_weight.astype(F32)) <= clip_bound[None, :]
    grad_weight = jnp.where(inside, rows, jnp.zeros((), BF))
    gate_vals, up_vals = gate_pre.astype(F32), up_pre.astype(F32)
    gh = grad_hidden.astype(F32)
    sg = jax.nn.sigmoid(gate_vals)
    grad_gate = (gh * up_vals * sg * (1.0 + gate_vals * (1.0 - sg))).astype(BF)
    grad_up = (gh * gate_vals * sg).astype(BF)
    return grad_gate, grad_up, grad_weight


def solution(mesh):
    both = P("dp", "tensor")
    return jax.shard_map(
        local,
        mesh=mesh,
        in_specs=(both, both, both, both, both, P("tensor"), P("tensor")),
        out_specs=(both, both, both),
        check_vma=False,
    )
```

```python
import jax
import jax.numpy as jnp
import numpy as np
from jax import lax
from jax.experimental import pallas as pl
from jax.experimental.pallas import tpu as pltpu
from jax.sharding import PartitionSpec as P

HAD = 1024
NBLK = 26
MESH = pl.DeviceIdType.MESH
BF = jnp.bfloat16
F32 = jnp.float32

ZN = 16
XY = 16
TOK = 128
UN = 1664
COL = 32
HALF = 896


def local_table():
    table = np.array([[1.0]])
    for _ in range(6):
        table = np.block([[table, table], [table, -table]])
    return np.kron(table / 8.0, np.eye(NBLK)).astype(jnp.bfloat16)


def hint(value, multiple):
    return pl.multiple_of(value, multiple)


CHUNKS = ((0, 896), (896, 384), (1280, 384))
PASSES = ((0, 896), (896, 768))
PIECES = (
    ((0, 0, 0, 896, 0), (1, 1, 768, 128, 0)),
    ((2, 1, 896, 384, 128),),
    ((3, 1, 1280, 384, 512),),
)


def far_first(t):
    half = (t + 1) >> 1
    return (8 + half * (1 - 2 * (t & 1))) & 15


def rotate16(src, dst, first, width):
    def tile(t, carry):
        lanes = pl.ds(hint(t * 128, 128), 128)
        vals = [src[j, :, lanes].astype(F32) for j in range(16)]
        for bit in range(4):
            step = 1 << bit
            for j in range(16):
                if not j & step:
                    low, high = vals[j], vals[j | step]
                    vals[j], vals[j | step] = low + high, low - high
        for j in range(16):
            dst[j, :, lanes] = (vals[j] * 0.25).astype(BF)
        return carry

    lax.fori_loop(first // 128, (first + width) // 128, tile, 0)


def kernel(
    gate, up, grot, gout, table_hbm, gh_out, gw_out,
    acts, outs, part, send, other, own, got, turned, landed, hid, fin, fturn, fback,
    bt, table, load_sem, ring_s, ring_r, ring_rz, f_s, f_r, fb_s, fb_r, b_s, b_r, e_s, e_r, g_s, g_r, z_s, z_r,
):
    i = lax.axis_index("dp")
    z = lax.axis_index("tensor")
    c = i & 1
    xy = i >> 1
    x, y = xy >> 2, xy & 3
    k_me = z >> 1
    active = (z & 1) == c

    def remote(src, dst, ssem, rsem, dp, zz):
        return pltpu.make_async_remote_copy(
            src_ref=src, dst_ref=dst, send_sem=ssem, recv_sem=rsem,
            device_id=(dp, zz), device_id_type=MESH,
        )

    load_table = pltpu.make_async_copy(table_hbm, table, load_sem)
    load_table.start()

    def taken(ref, sem):
        remote(ref, ref, load_sem, sem, i, z ^ 1).wait_recv()

    def gone(ref, sem):
        remote(ref, ref, sem, load_sem, i, z ^ 1).wait_send()

    barrier = pltpu.get_barrier_semaphore()

    def hail_z(off, carry):
        pl.semaphore_signal(barrier, inc=1, device_id=(i, (z + off) & 15), device_id_type=MESH)
        return carry

    def hail_xy(off, carry):
        pl.semaphore_signal(barrier, inc=1, device_id=((i + off) & 31, z), device_id_type=MESH)
        return carry

    lax.fori_loop(1, ZN, hail_z, 0)
    lax.fori_loop(1, 32, hail_xy, 0)

    for t in range(4):
        lanes = slice(128 * t, 128 * (t + 1))
        bt[lanes, :] = gout[:, lanes].astype(F32).T.astype(BF)
    pl.semaphore_wait(barrier, ZN - 1 + 31)

    def f_copy(k):
        rows = pl.ds(hint(16 * k, 16), 16)
        return remote(grot.at[rows, :], fin.at[z], f_s, f_r, i, 2 * k + c)

    def f_start(j, carry):
        half = (j + 1) >> 1
        k = (k_me + 4 + half * (1 - 2 * (j & 1))) & 7

        @pl.when(2 * k + c != z)
        def _():
            f_copy(k).start()

        return carry

    lax.fori_loop(0, 3, f_start, 0)

    def b_copy(off):
        peer = (xy + 7 * off) & 15
        return remote(
            bt.at[pl.ds(hint(COL * peer, COL), COL), :],
            outs.at[pl.ds(hint(COL * z, COL), COL), pl.ds(hint(TOK * xy, TOK), TOK)],
            b_s, b_r, 2 * peer + c, z,
        )

    def b_start(off, carry):
        b_copy(off).start()
        return carry

    lax.fori_loop(1, XY, b_start, 0)
    outs[pl.ds(hint(COL * z, COL), COL), pl.ds(hint(TOK * xy, TOK), TOK)] = bt[
        pl.ds(hint(COL * xy, COL), COL), :
    ]

    @pl.when(active)
    def _():
        fin[z] = grot[pl.ds(hint(16 * k_me, 16), 16), :]

    def make_hidden(t, carry):
        lanes = pl.ds(hint(t * 128, 128), 128)
        g = gate[:, lanes].astype(F32)
        u = up[:, lanes].astype(F32)
        hid[:, lanes] = (g * jax.nn.sigmoid(g) * u).astype(BF)
        return carry

    lax.fori_loop(0, UN // 128, make_hidden, 0)
    load_table.wait()
    mine = pl.ds(hint(TOK * xy, TOK), TOK)


    def turn(lanes):
        acts[mine, lanes] = jnp.dot(hid[...], table[:, lanes], preferred_element_type=F32).astype(BF)

    def turn_pass(q):
        first, width = PASSES[q]

        def turn_tile(t, carry):
            turn(pl.ds(hint(first + t * 256, 128), 256))
            return carry

        lax.fori_loop(0, width // 256, turn_tile, 0)
        if width % 256:
            turn(pl.ds(first + width - 128, 128))

    turn_pass(0)

    place = (4 * x + ((x + y) & 3), 4 * y + ((x + y) & 3), z)

    def block_of(r, n):
        if r == 2:
            return n
        major = n >> 2
        minor = (n + 3 * major) & 3
        return 4 * major + minor if r == 0 else 4 * minor + major

    def ring_peer(r, n):
        return (i, n) if r == 2 else (2 * block_of(r, n) + c, z)

    peers = [[ring_peer(r, (place[r] + hop) & 15) for hop in (1, 15)] for r in range(3)]

    def ring_copy(q, r, d, s, u):
        blk = block_of(r, (place[r] + 16 - s if d == 0 else place[r] + s) & 15)
        if r < 2:
            ref = acts.at[pl.ds(hint(TOK * blk + 64 * r + 32 * u, 32), 32), pl.ds(*PASSES[q])]
            sem = ring_r.at[q, r, d, s, u]
        else:
            ref = outs.at[pl.ds(hint(COL * blk + 16 * u, 16), 16), :]
            sem = ring_rz.at[d, s, u]
        return remote(ref, ref, ring_s.at[r], sem, *peers[r][d])

    def ring_wait(q, r, d, s, u):
        if r < 2:
            taken(acts.at[pl.ds(0, 32), pl.ds(*PASSES[q])], ring_r.at[q, r, d, s, u])
        else:
            taken(outs.at[pl.ds(0, 16), :], ring_rz.at[d, s, u])

    def ring_step(q, rings, s):
        for u in range(2):
            for r in rings:
                for d in range(2):
                    ring_wait(q, r, d, s - 1, u)
                    ring_copy(q, r, d, s, u).start()

    def ring_last(q, rings):
        for u in range(2):
            for r in rings:
                for d in range(2):
                    ring_wait(q, r, d, 6, u)
                    if u == d:
                        ring_copy(q, r, d, 7, u).start()

    def ring_end(q, rings):
        for r in rings:
            for d in range(2):
                ring_wait(q, r, d, 7, d)

    for u in range(2):
        for r in range(2):
            for d in range(2):
                ring_copy(0, r, d, 0, u).start()

    taken(outs.at[pl.ds(0, COL), pl.ds(0, TOK * (XY - 1))], b_r)
    for u in range(2):
        for d in range(2):
            ring_copy(0, 2, d, 0, u).start()
    turn_pass(1)

    def ring_steps(h, carry):
        ring_step(0, (2, 0, 1), 2 * h + 1)
        f_start(h + 3, 0)
        ring_step(0, (2, 0, 1), 2 * h + 2)
        return carry

    lax.fori_loop(0, 3, ring_steps, 0)
    ring_last(0, (2, 0, 1))
    lax.fori_loop(6, 8, f_start, 0)
    for u in range(2):
        for r in range(2):
            for d in range(2):
                ring_copy(1, r, d, 0, u).start()
    ring_end(0, (2, 0, 1))

    def fb_copy(dest):
        return remote(
            fturn.at[dest], fback.at[pl.ds(hint(16 * k_me, 16), 16), :],
            fb_s, fb_r, i, dest,
        )

    def turn_back():
        @pl.when(active)
        def _():
            taken(fin.at[pl.ds(0, ZN - 1)], f_r)
            rotate16(fin, fturn, 0, UN)
            fback[pl.ds(hint(16 * k_me, 16), 16), :] = fturn[z]

    def send_back(first, last):
        @pl.when(active)
        def _():
            def fb_start(t, carry):
                fb_copy((z + far_first(t)) & 15).start()
                return carry

            lax.fori_loop(first, last, fb_start, 0)

    def product(lanes, width):
        tile = jnp.dot(outs[...], acts[:, lanes], preferred_element_type=F32)
        tile = tile.reshape(ZN, COL, width)
        part[:, :, lanes] = tile
        send[:, :, lanes] = tile.astype(BF)

    def product_chunk(q):
        first, width = CHUNKS[q]

        def product_tile(t, carry):
            product(pl.ds(hint(first + t * 256, 128), 256), 256)
            return carry

        lax.fori_loop(0, width // 256, product_tile, 0)
        if width % 256:
            product(pl.ds(first + width - 128, 128), 128)

    def swap(q):
        lanes = pl.ds(*CHUNKS[q])
        return remote(
            send.at[:, pl.ds(hint(16 * (1 - c), 16), 16), lanes], other.at[:, :, lanes],
            e_s, e_r.at[q], i ^ 1, z,
        )

    def g_copy(q, dest):
        lanes = pl.ds(*CHUNKS[q])
        return remote(
            own.at[dest, :, lanes], got.at[z, :, lanes], g_s, g_r.at[q], i, dest
        )

    def share(q, begin=0, end=ZN):
        lanes = pl.ds(*CHUNKS[q])
        if begin == 0:
            taken(other.at[:, :, lanes], e_r.at[q])

        def add_send(t, carry):
            j = (z + far_first(t)) & 15
            own[j, :, lanes] = (
                part[j, pl.ds(hint(16 * c, 16), 16), lanes] + other[j, :, lanes].astype(F32)
            ).astype(BF)

            @pl.when(t < ZN - 1)
            def _():
                g_copy(q, j).start()

            return carry

        lax.fori_loop(begin, end, add_send, 0)
        if end == ZN:
            got[z, :, lanes] = own[z, :, lanes]

    ring_step(1, (0, 1), 1)
    product_chunk(0)
    swap(0).start()
    ring_step(1, (0, 1), 2)
    turn_back()
    send_back(0, 4)
    ring_step(1, (0, 1), 3)
    share(0, 0, 5)
    ring_step(1, (0, 1), 4)
    share(0, 5, 9)
    send_back(4, 7)
    ring_step(1, (0, 1), 5)
    share(0, 9, 13)
    send_back(7, 10)
    ring_step(1, (0, 1), 6)
    share(0, 13, ZN)
    send_back(10, 13)
    ring_last(1, (0, 1))
    send_back(13, 15)
    ring_end(1, (0, 1))
    product_chunk(1)
    swap(1).start()
    product_chunk(2)
    swap(2).start()
    share(1)
    share(2)

    @pl.when(active)
    def _():
        taken(fback.at[pl.ds(0, TOK - 16), :], fb_r)

    @pl.when(jnp.logical_not(active))
    def _():
        taken(fback, fb_r)

    def finish(lanes):
        gh_out[:, lanes] = jnp.dot(fback[...], table[:, lanes], preferred_element_type=F32).astype(BF)

    def finish_tile(t, carry):
        finish(pl.ds(hint(t * 256, 256), 256))
        return carry

    lax.fori_loop(0, UN // 256, finish_tile, 0)
    finish(pl.ds(UN - 128, 128))

    def z_copy(piece, peer):
        p, core, first, width, at = piece
        return remote(
            turned.at[peer, :, pl.ds(first, width)],
            landed.at[pl.ds(hint(COL * xy + 16 * c, 16), 16), pl.ds(at, width)],
            z_s.at[p], z_r.at[p], 2 * peer + core, z,
        )

    def g_wait_chunk(q):
        lanes = pl.ds(*CHUNKS[q])

        taken(got.at[pl.ds(0, ZN - 1), :, lanes], g_r.at[q])

    def z_send(piece):
        p, core, first, width, at = piece

        def z_start(off, carry):
            z_copy(piece, (xy + 7 * off) & 15).start()
            return carry

        lax.fori_loop(1, XY, z_start, 0)

        @pl.when(c == core)
        def _():
            landed[pl.ds(hint(COL * xy + 16 * c, 16), 16), at : at + width] = turned[
                xy, :, first : first + width
            ]

        @pl.when(c != core)
        def _():
            z_copy(piece, xy).start()

    def z_take(piece):
        p, core, first, width, at = piece

        @pl.when(c == core)
        def _():
            taken(landed.at[pl.ds(0, 496), pl.ds(at, width)], z_r.at[p])

            def flip(t, carry):
                lanes = pl.ds(hint(t * 128, 128), 128)
                gw_out[lanes, :] = landed[:, lanes].astype(F32).T.astype(BF)
                return carry

            lax.fori_loop(at // 128, (at + width) // 128, flip, 0)

    for q in range(3):
        g_wait_chunk(q)
        rotate16(got, turned, *CHUNKS[q])
        for piece in PIECES[q]:
            z_send(piece)
        if q:
            for piece in PIECES[q - 1]:
                z_take(piece)
    for piece in PIECES[2]:
        z_take(piece)

    for r in range(2):
        gone(acts.at[pl.ds(0, 64 * 15), :], ring_s.at[r])
    gone(outs.at[pl.ds(0, COL * 15), :], ring_s.at[2])
    gone(outs.at[pl.ds(0, COL), pl.ds(0, TOK * (XY - 1))], b_s)

    @pl.when(active)
    def _():
        gone(grot.at[pl.ds(0, TOK - 16), :], f_s)
        gone(fturn.at[pl.ds(0, ZN - 1)], fb_s)

    @pl.when(jnp.logical_not(active))
    def _():
        gone(grot, f_s)

    gone(other, e_s)
    gone(own.at[pl.ds(0, ZN - 1)], g_s)
    for pieces in PIECES:
        for p, core, first, width, at in pieces:

            @pl.when(c == core)
            def _():
                gone(turned.at[pl.ds(0, XY - 1), :, pl.ds(first, width)], z_s.at[p])

            @pl.when(c != core)
            def _():
                gone(turned.at[:, :, pl.ds(first, width)], z_s.at[p])


def local(gate_pre, up_pre, grad_rot, grad_out, latent_weight, clip_codes, bits):
    table = jnp.asarray(local_table())
    vmem = pl.BlockSpec(memory_space=pltpu.VMEM)
    hbm = pl.BlockSpec(memory_space=pl.ANY)
    dma = pltpu.SemaphoreType.DMA
    grad_hidden, summed = pl.pallas_call(
        kernel,
        out_shape=(
            jax.ShapeDtypeStruct((TOK, UN), BF),
            jax.ShapeDtypeStruct((HALF, 512), BF),
        ),
        in_specs=[vmem] * 4 + [hbm],
        out_specs=(vmem, vmem),
        scratch_shapes=[
            pltpu.VMEM((XY * TOK, UN), BF),
            pltpu.VMEM((512, XY * TOK), BF),
            pltpu.VMEM((ZN, COL, UN), F32),
            pltpu.VMEM((ZN, COL, UN), BF),
            pltpu.VMEM((ZN, 16, UN), BF),
            pltpu.VMEM((ZN, 16, UN), BF),
            pltpu.VMEM((ZN, 16, UN), BF),
            pltpu.VMEM((ZN, 16, UN), BF),
            pltpu.VMEM((512, HALF), BF),
            pltpu.VMEM((TOK, UN), BF),
            pltpu.VMEM((ZN, 16, UN), BF),
            pltpu.VMEM((ZN, 16, UN), BF),
            pltpu.VMEM((TOK, UN), BF),
            pltpu.VMEM((512, TOK), BF),
            pltpu.VMEM((UN, UN), BF),
            dma(()), dma((3,)), dma((2, 2, 2, 8, 2)), dma((2, 8, 2)),
            dma(()), dma(()), dma(()), dma(()),
            dma(()), dma(()), dma(()), dma((3,)),
            dma(()), dma((3,)), dma((4,)), dma((4,)),
        ],
        compiler_params=pltpu.CompilerParams(
            collective_id=0, has_side_effects=True, vmem_limit_bytes=56 * 1024 * 1024
        ),
    )(gate_pre, up_pre, grad_rot, grad_out, table)
    core = lax.axis_index("dp") & 1
    rows = jnp.where(core == 1, summed[HALF - 832 :], summed[:832])
    levels = jnp.left_shift(jnp.int32(1), bits - 1) - 1
    clip_bound = clip_codes.astype(F32) * levels.astype(F32) / 65536.0
    inside = jnp.abs(latent_weight.astype(F32)) <= clip_bound[None, :]
    grad_weight = jnp.where(inside, rows, jnp.zeros((), BF))
    gate_vals, up_vals = gate_pre.astype(F32), up_pre.astype(F32)
    gh = grad_hidden.astype(F32)
    sg = jax.nn.sigmoid(gate_vals)
    grad_gate = (gh * up_vals * sg * (1.0 + gate_vals * (1.0 - sg))).astype(BF)
    grad_up = (gh * gate_vals * sg).astype(BF)
    return grad_gate, grad_up, grad_weight


def solution(mesh):
    both = P("dp", "tensor")
    return jax.shard_map(
        local,
        mesh=mesh,
        in_specs=(both, both, both, both, both, P("tensor"), P("tensor")),
        out_specs=(both, both, both),
        check_vma=False,
    )
```

```python
import jax
import jax.numpy as jnp
import numpy as np
from jax import lax
from jax.experimental import pallas as pl
from jax.experimental.pallas import tpu as pltpu
from jax.sharding import PartitionSpec as P

HAD = 1024
NBLK = 26
MESH = pl.DeviceIdType.MESH
BF = jnp.bfloat16
F32 = jnp.float32

ZN = 16
XY = 16
TOK = 128
UN = 1664
COL = 32
HALF = 896


def local_table():
    table = np.array([[1.0]])
    for _ in range(6):
        table = np.block([[table, table], [table, -table]])
    return np.kron(table / 8.0, np.eye(NBLK)).astype(jnp.bfloat16)


def hint(value, multiple):
    return pl.multiple_of(value, multiple)


CHUNKS = ((0, 896), (896, 384), (1280, 384))
PIECES = (
    ((0, 0, 0, 896, 0), (1, 1, 768, 128, 0)),
    ((2, 1, 896, 384, 128),),
    ((3, 1, 1280, 384, 512),),
)


def far_first(t):
    half = (t + 1) >> 1
    return (8 + half * (1 - 2 * (t & 1))) & 15


def rotate16(src, dst, first, width):
    def tile(t, carry):
        lanes = pl.ds(hint(t * 128, 128), 128)
        vals = [src[j, :, lanes].astype(F32) for j in range(16)]
        for bit in range(4):
            step = 1 << bit
            for j in range(16):
                if not j & step:
                    low, high = vals[j], vals[j | step]
                    vals[j], vals[j | step] = low + high, low - high
        for j in range(16):
            dst[j, :, lanes] = (vals[j] * 0.25).astype(BF)
        return carry

    lax.fori_loop(first // 128, (first + width) // 128, tile, 0)


def kernel(
    gate, up, grot, gout, table_hbm, gh_out, gw_out,
    acts, outs, part, send, other, own, got, turned, landed, hid, fin, fturn, fback,
    bt, table, load_sem, ring_s, ring_r, f_s, f_r, fb_s, fb_r, b_s, b_r, e_s, e_r, g_s, g_r, z_s, z_r,
):
    i = lax.axis_index("dp")
    z = lax.axis_index("tensor")
    c = i & 1
    xy = i >> 1
    x, y = xy >> 2, xy & 3
    k_me = z >> 1
    active = (z & 1) == c
    sign = 1 - 2 * c

    def remote(src, dst, ssem, rsem, dp, zz):
        return pltpu.make_async_remote_copy(
            src_ref=src, dst_ref=dst, send_sem=ssem, recv_sem=rsem,
            device_id=(dp, zz), device_id_type=MESH,
        )

    load_table = pltpu.make_async_copy(table_hbm, table, load_sem)
    load_table.start()

    def taken(ref, sem):
        remote(ref, ref, load_sem, sem, i, z ^ 1).wait_recv()

    def gone(ref, sem):
        remote(ref, ref, sem, load_sem, i, z ^ 1).wait_send()

    barrier = pltpu.get_barrier_semaphore()

    def hail_z(off, carry):
        pl.semaphore_signal(barrier, inc=1, device_id=(i, (z + off) & 15), device_id_type=MESH)
        return carry

    def hail_xy(off, carry):
        pl.semaphore_signal(barrier, inc=1, device_id=((i + off) & 31, z), device_id_type=MESH)
        return carry

    lax.fori_loop(1, ZN, hail_z, 0)
    lax.fori_loop(1, 32, hail_xy, 0)

    pl.semaphore_wait(barrier, ZN - 1 + 31)

    def f_copy(k):
        rows = pl.ds(hint(16 * k, 16), 16)
        return remote(grot.at[rows, :], fin.at[z], f_s, f_r, i, 2 * k + c)

    def f_start(j, carry):
        half = (j + 1) >> 1
        k = (k_me + 4 + sign * half * (1 - 2 * (j & 1))) & 7

        @pl.when(2 * k + c != z)
        def _():
            f_copy(k).start()

        return carry

    lax.fori_loop(0, 4, f_start, 0)

    for t in range(4):
        lanes = slice(128 * t, 128 * (t + 1))
        bt[lanes, :] = gout[:, lanes].astype(F32).T.astype(BF)

    def b_copy(off):
        peer = (xy + 7 * off) & 15
        return remote(
            bt.at[pl.ds(hint(COL * peer, COL), COL), :],
            outs.at[pl.ds(hint(COL * z, COL), COL), pl.ds(hint(TOK * xy, TOK), TOK)],
            b_s, b_r, 2 * peer + c, z,
        )

    def b_start(off, carry):
        b_copy(off).start()
        return carry

    lax.fori_loop(1, XY, b_start, 0)
    outs[pl.ds(hint(COL * z, COL), COL), pl.ds(hint(TOK * xy, TOK), TOK)] = bt[
        pl.ds(hint(COL * xy, COL), COL), :
    ]

    @pl.when(active)
    def _():
        fin[z] = grot[pl.ds(hint(16 * k_me, 16), 16), :]

    def make_hidden(t, carry):
        lanes = pl.ds(hint(t * 128, 128), 128)
        g = gate[:, lanes].astype(F32)
        u = up[:, lanes].astype(F32)
        hid[:, lanes] = (g * jax.nn.sigmoid(g) * u).astype(BF)
        return carry

    lax.fori_loop(0, UN // 128, make_hidden, 0)
    load_table.wait()
    mine = pl.ds(hint(TOK * xy, TOK), TOK)

    def turn_hidden(t, carry):
        lanes = pl.ds(hint(t * 256, 256), 256)
        acts[mine, lanes] = jnp.dot(hid[...], table[:, lanes], preferred_element_type=F32).astype(BF)
        return carry

    lax.fori_loop(0, UN // 256, turn_hidden, 0)
    acts[mine, UN - 128 :] = jnp.dot(
        hid[...], table[:, UN - 128 :], preferred_element_type=F32
    ).astype(BF)

    place = (4 * x + ((x + y) & 3), 4 * y + ((x + y) & 3), z)

    def block_of(r, n):
        if r == 2:
            return n
        major = n >> 2
        minor = (n + 3 * major) & 3
        return 4 * major + minor if r == 0 else 4 * minor + major

    def ring_peer(r, n):
        return (i, n) if r == 2 else (2 * block_of(r, n) + c, z)

    peers = [[ring_peer(r, (place[r] + hop) & 15) for hop in (sign, -sign)] for r in range(3)]

    def ring_copy(r, d, s, u):
        blk = block_of(r, (place[r] - (1 - 2 * d) * sign * s) & 15)
        if r < 2:
            ref = acts.at[pl.ds(hint(TOK * blk + 64 * r + 32 * u, 32), 32), :]
        else:
            ref = outs.at[pl.ds(hint(COL * blk + 16 * u, 16), 16), :]
        return remote(ref, ref, ring_s.at[r], ring_r.at[r, d, s, u], *peers[r][d])

    def ring_wait(r, d, s, u):
        taken(acts.at[pl.ds(0, 32), :] if r < 2 else outs.at[pl.ds(0, 16), :], ring_r.at[r, d, s, u])

    for u in range(2):
        for r in range(2):
            for d in range(2):
                ring_copy(r, d, 0, u).start()

    taken(outs.at[pl.ds(0, COL), pl.ds(0, TOK * (XY - 1))], b_r)
    for u in range(2):
        for d in range(2):
            ring_copy(2, d, 0, u).start()

    def ring_step(s, carry):
        for u in range(2):
            for r in (2, 0, 1):
                for d in range(2):
                    ring_wait(r, d, s - 1, u)
                    ring_copy(r, d, s, u).start()
        return carry

    def ring_step_f(s, carry):
        f_start(s + 3, 0)
        return ring_step(s, carry)

    def fb_copy(dest):
        return remote(
            fturn.at[dest], fback.at[pl.ds(hint(16 * k_me, 16), 16), :],
            fb_s, fb_r, i, dest,
        )

    def turn_back():
        @pl.when(active)
        def _():
            taken(fin.at[pl.ds(0, ZN - 1)], f_r)
            rotate16(fin, fturn, 0, UN)
            fback[pl.ds(hint(16 * k_me, 16), 16), :] = fturn[z]

    def send_back(first, last):
        @pl.when(active)
        def _():
            def fb_start(t, carry):
                fb_copy((z + sign * far_first(t)) & 15).start()
                return carry

            lax.fori_loop(first, last, fb_start, 0)

    lax.fori_loop(1, 5, ring_step_f, 0)
    lax.fori_loop(5, 7, ring_step, 0)
    turn_back()
    for u in range(2):
        for r in (2, 0, 1):
            for d in range(2):
                ring_wait(r, d, 6, u)
                if u == d:
                    ring_copy(r, d, 7, u).start()
    send_back(0, 4)
    for r in (2, 0, 1):
        for d in range(2):
            ring_wait(r, d, 7, d)

    def product(lanes, width):
        tile = jnp.dot(outs[...], acts[:, lanes], preferred_element_type=F32)
        tile = tile.reshape(ZN, COL, width)
        part[:, :, lanes] = tile
        send[:, :, lanes] = tile.astype(BF)

    def product_chunk(q):
        first, width = CHUNKS[q]

        def product_tile(t, carry):
            product(pl.ds(hint(first + t * 256, 128), 256), 256)
            return carry

        lax.fori_loop(0, width // 256, product_tile, 0)
        if width % 256:
            product(pl.ds(first + width - 128, 128), 128)

    def swap(q):
        lanes = pl.ds(*CHUNKS[q])
        return remote(
            send.at[:, pl.ds(hint(16 * (1 - c), 16), 16), lanes], other.at[:, :, lanes],
            e_s, e_r.at[q], i ^ 1, z,
        )

    def g_copy(q, dest):
        lanes = pl.ds(*CHUNKS[q])
        return remote(
            own.at[dest, :, lanes], got.at[z, :, lanes], g_s, g_r.at[q], i, dest
        )

    def share(q):
        lanes = pl.ds(*CHUNKS[q])
        taken(other.at[:, :, lanes], e_r.at[q])

        def add_send(t, carry):
            j = (z + sign * far_first(t)) & 15
            own[j, :, lanes] = (
                part[j, pl.ds(hint(16 * c, 16), 16), lanes] + other[j, :, lanes].astype(F32)
            ).astype(BF)

            @pl.when(t < ZN - 1)
            def _():
                g_copy(q, j).start()

            return carry

        lax.fori_loop(0, ZN, add_send, 0)
        got[z, :, lanes] = own[z, :, lanes]

    product_chunk(0)
    swap(0).start()
    send_back(4, 7)
    product_chunk(1)
    swap(1).start()
    send_back(7, 10)
    product_chunk(2)
    swap(2).start()
    share(0)
    send_back(10, 12)
    share(1)
    send_back(12, 15)
    share(2)

    @pl.when(active)
    def _():
        taken(fback.at[pl.ds(0, TOK - 16), :], fb_r)

    @pl.when(jnp.logical_not(active))
    def _():
        taken(fback, fb_r)

    def finish(lanes):
        gh_out[:, lanes] = jnp.dot(fback[...], table[:, lanes], preferred_element_type=F32).astype(BF)

    def finish_tile(t, carry):
        finish(pl.ds(hint(t * 256, 256), 256))
        return carry

    lax.fori_loop(0, UN // 256, finish_tile, 0)
    finish(pl.ds(UN - 128, 128))

    def z_copy(piece, peer):
        p, core, first, width, at = piece
        return remote(
            turned.at[peer, :, pl.ds(first, width)],
            landed.at[pl.ds(hint(COL * xy + 16 * c, 16), 16), pl.ds(at, width)],
            z_s.at[p], z_r.at[p], 2 * peer + core, z,
        )

    def g_wait_chunk(q):
        lanes = pl.ds(*CHUNKS[q])

        taken(got.at[pl.ds(0, ZN - 1), :, lanes], g_r.at[q])

    def z_send(piece):
        p, core, first, width, at = piece

        def z_start(off, carry):
            z_copy(piece, (xy + 7 * off) & 15).start()
            return carry

        lax.fori_loop(1, XY, z_start, 0)

        @pl.when(c == core)
        def _():
            landed[pl.ds(hint(COL * xy + 16 * c, 16), 16), at : at + width] = turned[
                xy, :, first : first + width
            ]

        @pl.when(c != core)
        def _():
            z_copy(piece, xy).start()

    def z_take(piece):
        p, core, first, width, at = piece

        @pl.when(c == core)
        def _():
            taken(landed.at[pl.ds(0, 496), pl.ds(at, width)], z_r.at[p])

            def flip(t, carry):
                lanes = pl.ds(hint(t * 128, 128), 128)
                gw_out[lanes, :] = landed[:, lanes].astype(F32).T.astype(BF)
                return carry

            lax.fori_loop(at // 128, (at + width) // 128, flip, 0)

    for q in range(3):
        g_wait_chunk(q)
        rotate16(got, turned, *CHUNKS[q])
        for piece in PIECES[q]:
            z_send(piece)
        if q:
            for piece in PIECES[q - 1]:
                z_take(piece)
    for piece in PIECES[2]:
        z_take(piece)

    for r in range(2):
        gone(acts.at[pl.ds(0, 64 * 15), :], ring_s.at[r])
    gone(outs.at[pl.ds(0, COL * 15), :], ring_s.at[2])
    gone(outs.at[pl.ds(0, COL), pl.ds(0, TOK * (XY - 1))], b_s)

    @pl.when(active)
    def _():
        gone(grot.at[pl.ds(0, TOK - 16), :], f_s)
        gone(fturn.at[pl.ds(0, ZN - 1)], fb_s)

    @pl.when(jnp.logical_not(active))
    def _():
        gone(grot, f_s)

    gone(other, e_s)
    gone(own.at[pl.ds(0, ZN - 1)], g_s)
    for pieces in PIECES:
        for p, core, first, width, at in pieces:

            @pl.when(c == core)
            def _():
                gone(turned.at[pl.ds(0, XY - 1), :, pl.ds(first, width)], z_s.at[p])

            @pl.when(c != core)
            def _():
                gone(turned.at[:, :, pl.ds(first, width)], z_s.at[p])


def local(gate_pre, up_pre, grad_rot, grad_out, latent_weight, clip_codes, bits):
    table = jnp.asarray(local_table())
    vmem = pl.BlockSpec(memory_space=pltpu.VMEM)
    hbm = pl.BlockSpec(memory_space=pl.ANY)
    dma = pltpu.SemaphoreType.DMA
    grad_hidden, summed = pl.pallas_call(
        kernel,
        out_shape=(
            jax.ShapeDtypeStruct((TOK, UN), BF),
            jax.ShapeDtypeStruct((HALF, 512), BF),
        ),
        in_specs=[vmem] * 4 + [hbm],
        out_specs=(vmem, vmem),
        scratch_shapes=[
            pltpu.VMEM((XY * TOK, UN), BF),
            pltpu.VMEM((512, XY * TOK), BF),
            pltpu.VMEM((ZN, COL, UN), F32),
            pltpu.VMEM((ZN, COL, UN), BF),
            pltpu.VMEM((ZN, 16, UN), BF),
            pltpu.VMEM((ZN, 16, UN), BF),
            pltpu.VMEM((ZN, 16, UN), BF),
            pltpu.VMEM((ZN, 16, UN), BF),
            pltpu.VMEM((512, HALF), BF),
            pltpu.VMEM((TOK, UN), BF),
            pltpu.VMEM((ZN, 16, UN), BF),
            pltpu.VMEM((ZN, 16, UN), BF),
            pltpu.VMEM((TOK, UN), BF),
            pltpu.VMEM((512, TOK), BF),
            pltpu.VMEM((UN, UN), BF),
            dma(()), dma((3,)), dma((3, 2, 8, 2)),
            dma(()), dma(()), dma(()), dma(()),
            dma(()), dma(()), dma(()), dma((3,)),
            dma(()), dma((3,)), dma((4,)), dma((4,)),
        ],
        compiler_params=pltpu.CompilerParams(
            collective_id=0, has_side_effects=True, vmem_limit_bytes=56 * 1024 * 1024
        ),
    )(gate_pre, up_pre, grad_rot, grad_out, table)
    core = lax.axis_index("dp") & 1
    rows = jnp.where(core == 1, summed[HALF - 832 :], summed[:832])
    levels = jnp.left_shift(jnp.int32(1), bits - 1) - 1
    clip_bound = clip_codes.astype(F32) * levels.astype(F32) / 65536.0
    inside = jnp.abs(latent_weight.astype(F32)) <= clip_bound[None, :]
    grad_weight = jnp.where(inside, rows, jnp.zeros((), BF))
    gate_vals, up_vals = gate_pre.astype(F32), up_pre.astype(F32)
    gh = grad_hidden.astype(F32)
    sg = jax.nn.sigmoid(gate_vals)
    grad_gate = (gh * up_vals * sg * (1.0 + gate_vals * (1.0 - sg))).astype(BF)
    grad_up = (gh * gate_vals * sg).astype(BF)
    return grad_gate, grad_up, grad_weight


def solution(mesh):
    both = P("dp", "tensor")
    return jax.shard_map(
        local,
        mesh=mesh,
        in_specs=(both, both, both, both, both, P("tensor"), P("tensor")),
        out_specs=(both, both, both),
        check_vma=False,
    )
```

```python
import jax
import jax.numpy as jnp
import numpy as np
from jax import lax
from jax.experimental import pallas as pl
from jax.experimental.pallas import tpu as pltpu
from jax.sharding import PartitionSpec as P

HAD = 1024
NBLK = 26
MESH = pl.DeviceIdType.MESH
BF = jnp.bfloat16
F32 = jnp.float32

ZN = 16
XY = 16
TOK = 128
UN = 1664
COL = 32
HALF = 896


def local_table():
    table = np.array([[1.0]])
    for _ in range(6):
        table = np.block([[table, table], [table, -table]])
    return np.kron(table / 8.0, np.eye(NBLK)).astype(jnp.bfloat16)


def hint(value, multiple):
    return pl.multiple_of(value, multiple)


CHUNKS = ((0, 896), (896, 384), (1280, 384))
PIECES = (
    ((0, 0, 0, 896, 0), (1, 1, 768, 128, 0)),
    ((2, 1, 896, 384, 128),),
    ((3, 1, 1280, 384, 512),),
)


def far_first(t):
    half = (t + 1) >> 1
    return (8 + half * (1 - 2 * (t & 1))) & 15


def rotate16(src, dst, first, width):
    def tile(t, carry):
        lanes = pl.ds(hint(t * 128, 128), 128)
        vals = [src[j, :, lanes].astype(F32) for j in range(16)]
        for bit in range(4):
            step = 1 << bit
            for j in range(16):
                if not j & step:
                    low, high = vals[j], vals[j | step]
                    vals[j], vals[j | step] = low + high, low - high
        for j in range(16):
            dst[j, :, lanes] = (vals[j] * 0.25).astype(BF)
        return carry

    lax.fori_loop(first // 128, (first + width) // 128, tile, 0)


def kernel(
    gate, up, grot, gout, table_hbm, gh_out, gw_out,
    acts, outs, part, send, other, own, got, turned, landed, hid, fin, fturn, fback,
    bt, table, load_sem, a_s, a_r, ring_s, ring_r, f_s, f_r, fb_s, fb_r, b_s, b_r, e_s, e_r, g_s, g_r, z_s, z_r,
):
    i = lax.axis_index("dp")
    z = lax.axis_index("tensor")
    c = i & 1
    xy = i >> 1
    x, y = xy >> 2, xy & 3
    k_me = z >> 1
    active = (z & 1) == c

    def remote(src, dst, ssem, rsem, dp, zz):
        return pltpu.make_async_remote_copy(
            src_ref=src, dst_ref=dst, send_sem=ssem, recv_sem=rsem,
            device_id=(dp, zz), device_id_type=MESH,
        )

    load_table = pltpu.make_async_copy(table_hbm, table, load_sem)
    load_table.start()

    def taken(ref, sem):
        remote(ref, ref, load_sem, sem, i, z ^ 1).wait_recv()

    def gone(ref, sem):
        remote(ref, ref, sem, load_sem, i, z ^ 1).wait_send()

    barrier = pltpu.get_barrier_semaphore()

    def hail_z(off, carry):
        pl.semaphore_signal(barrier, inc=1, device_id=(i, (z + off) & 15), device_id_type=MESH)
        return carry

    def hail_xy(off, carry):
        pl.semaphore_signal(barrier, inc=1, device_id=((i + off) & 31, z), device_id_type=MESH)
        return carry

    lax.fori_loop(1, ZN, hail_z, 0)
    lax.fori_loop(1, 32, hail_xy, 0)

    for t in range(4):
        lanes = slice(128 * t, 128 * (t + 1))
        bt[lanes, :] = gout[:, lanes].astype(F32).T.astype(BF)
    pl.semaphore_wait(barrier, ZN - 1 + 31)

    def f_copy(k):
        rows = pl.ds(hint(16 * k, 16), 16)
        return remote(grot.at[rows, :], fin.at[z], f_s, f_r, i, 2 * k + c)

    def f_start(j, carry):
        half = (j + 1) >> 1
        k = (k_me + 4 + half * (1 - 2 * (j & 1))) & 7

        @pl.when(2 * k + c != z)
        def _():
            f_copy(k).start()

        return carry

    lax.fori_loop(0, 3, f_start, 0)

    def b_copy(off):
        peer = (xy + 7 * off) & 15
        return remote(
            bt.at[pl.ds(hint(COL * peer, COL), COL), :],
            outs.at[pl.ds(hint(COL * z, COL), COL), pl.ds(hint(TOK * xy, TOK), TOK)],
            b_s, b_r, 2 * peer + c, z,
        )

    def b_start(off, carry):
        b_copy(off).start()
        return carry

    lax.fori_loop(1, XY, b_start, 0)
    outs[pl.ds(hint(COL * z, COL), COL), pl.ds(hint(TOK * xy, TOK), TOK)] = bt[
        pl.ds(hint(COL * xy, COL), COL), :
    ]

    @pl.when(active)
    def _():
        fin[z] = grot[pl.ds(hint(16 * k_me, 16), 16), :]

    def make_hidden(t, carry):
        lanes = pl.ds(hint(t * 128, 128), 128)
        g = gate[:, lanes].astype(F32)
        u = up[:, lanes].astype(F32)
        hid[:, lanes] = (g * jax.nn.sigmoid(g) * u).astype(BF)
        return carry

    lax.fori_loop(0, UN // 128, make_hidden, 0)
    load_table.wait()
    mine = pl.ds(hint(TOK * xy, TOK), TOK)

    def turn_hidden(t, carry):
        lanes = pl.ds(hint(t * 256, 256), 256)
        acts[mine, lanes] = jnp.dot(hid[...], table[:, lanes], preferred_element_type=F32).astype(BF)
        return carry

    lax.fori_loop(0, UN // 256, turn_hidden, 0)
    acts[mine, UN - 128 :] = jnp.dot(
        hid[...], table[:, UN - 128 :], preferred_element_type=F32
    ).astype(BF)

    COLS = (0, -1, 1, 2)

    def chip(h, p, q):
        return 4 * (p & 3) + (q & 3) if h == 0 else 4 * (q & 3) + (p & 3)

    def spot(h):
        return (x, y) if h == 0 else (y, x)

    def a_rows(h, blk, part):
        if part is None:
            return acts.at[pl.ds(hint(TOK * blk + 64 * h, 64), 64), :]
        return acts.at[pl.ds(hint(TOK * blk + 64 * h + 32 * part, 32), 32), :]

    def a_send(h, first_axis, blk, part, d, sem):
        p, q = spot(h)
        hop = 1 - 2 * d
        peer = chip(h, p + hop, q) if first_axis else chip(h, p, q + hop)
        ref = a_rows(h, blk, part)
        remote(ref, ref, a_s.at[h], a_r.at[h, sem, d], 2 * peer + c, z).start()

    def a_take(h, rows, d, sem):
        taken(acts.at[pl.ds(0, rows), :], a_r.at[h, sem, d])

    def first_near(h, d):
        a_send(h, True, chip(h, *spot(h)), None, d, 0)

    def first_far(h, d):
        p, q = spot(h)
        a_send(h, True, chip(h, p - 1 + 2 * d, q), d, d, 1)

    def second_near(h, j, d):
        p, q = spot(h)
        a_send(h, False, chip(h, p + COLS[j], q), None, d, 2 + j)

    def second_far(h, j, d):
        p, q = spot(h)
        a_send(h, False, chip(h, p + COLS[j], q - 1 + 2 * d), d, d, 6 + j)

    both = [(h, d) for d in range(2) for h in range(2)]
    for h, d in both:
        first_near(h, d)
    for h, d in both:
        second_near(h, 0, d)

    def ring_copy(d, s, u):
        origin = (z + 16 - s if d == 0 else z + s) & 15
        ref = outs.at[pl.ds(hint(COL * origin + 16 * u, 16), 16), :]
        peer = (z + 1 if d == 0 else z + 15) & 15
        return remote(ref, ref, ring_s, ring_r.at[d, s, u], i, peer)

    def ring_wait(d, s, u):
        taken(outs.at[pl.ds(0, 16), :], ring_r.at[d, s, u])

    def ring_step(s):
        for u in range(2):
            for d in range(2):
                ring_wait(d, s - 1, u)
                if s < 7 or u == d:
                    ring_copy(d, s, u).start()

    taken(outs.at[pl.ds(0, COL), pl.ds(0, TOK * (XY - 1))], b_r)
    for u in range(2):
        for d in range(2):
            ring_copy(d, 0, u).start()

    f_start(3, 0)
    ring_step(1)
    for h, d in both:
        a_take(h, 64, d, 0)
        first_far(h, d)
    for h, d in both:
        second_near(h, 1, d)
    f_start(4, 0)
    ring_step(2)
    for h, d in both:
        a_take(h, 64, d, 2)
        second_far(h, 0, d)
    for h, d in both:
        second_near(h, 2, d)
    f_start(5, 0)
    ring_step(3)
    for h, d in both:
        a_take(h, 32, d, 1)
    for h, d in both:
        second_near(h, 3, d)
    f_start(6, 0)
    ring_step(4)
    for j in range(1, 4):
        for h, d in both:
            a_take(h, 64, d, 2 + j)
            second_far(h, j, d)
        if j == 1:
            f_start(7, 0)
        ring_step(4 + j)
    for d in range(2):
        ring_wait(d, 7, d)
    for j in range(4):
        for h, d in both:
            a_take(h, 32, d, 6 + j)

    def fb_copy(dest):
        return remote(
            fturn.at[dest], fback.at[pl.ds(hint(16 * k_me, 16), 16), :],
            fb_s, fb_r, i, dest,
        )

    @pl.when(active)
    def _():
        taken(fin.at[pl.ds(0, ZN - 1)], f_r)
        rotate16(fin, fturn, 0, UN)

        def fb_start(t, carry):
            fb_copy((z + far_first(t)) & 15).start()
            return carry

        lax.fori_loop(0, ZN - 1, fb_start, 0)
        fback[pl.ds(hint(16 * k_me, 16), 16), :] = fturn[z]

    def product(lanes, width):
        tile = jnp.dot(outs[...], acts[:, lanes], preferred_element_type=F32)
        tile = tile.reshape(ZN, COL, width)
        part[:, :, lanes] = tile
        send[:, :, lanes] = tile.astype(BF)

    def product_chunk(q):
        first, width = CHUNKS[q]

        def product_tile(t, carry):
            product(pl.ds(hint(first + t * 256, 128), 256), 256)
            return carry

        lax.fori_loop(0, width // 256, product_tile, 0)
        if width % 256:
            product(pl.ds(first + width - 128, 128), 128)

    def swap(q):
        lanes = pl.ds(*CHUNKS[q])
        return remote(
            send.at[:, pl.ds(hint(16 * (1 - c), 16), 16), lanes], other.at[:, :, lanes],
            e_s, e_r.at[q], i ^ 1, z,
        )

    def g_copy(q, dest):
        lanes = pl.ds(*CHUNKS[q])
        return remote(
            own.at[dest, :, lanes], got.at[z, :, lanes], g_s, g_r.at[q], i, dest
        )

    def share(q):
        lanes = pl.ds(*CHUNKS[q])
        taken(other.at[:, :, lanes], e_r.at[q])

        def add_send(t, carry):
            j = (z + far_first(t)) & 15
            own[j, :, lanes] = (
                part[j, pl.ds(hint(16 * c, 16), 16), lanes] + other[j, :, lanes].astype(F32)
            ).astype(BF)

            @pl.when(t < ZN - 1)
            def _():
                g_copy(q, j).start()

            return carry

        lax.fori_loop(0, ZN, add_send, 0)
        got[z, :, lanes] = own[z, :, lanes]

    product_chunk(0)
    swap(0).start()
    product_chunk(1)
    swap(1).start()
    share(0)
    product_chunk(2)
    swap(2).start()
    share(1)
    share(2)

    @pl.when(active)
    def _():
        taken(fback.at[pl.ds(0, TOK - 16), :], fb_r)

    @pl.when(jnp.logical_not(active))
    def _():
        taken(fback, fb_r)

    def finish(lanes):
        gh_out[:, lanes] = jnp.dot(fback[...], table[:, lanes], preferred_element_type=F32).astype(BF)

    def finish_tile(t, carry):
        finish(pl.ds(hint(t * 256, 256), 256))
        return carry

    lax.fori_loop(0, UN // 256, finish_tile, 0)
    finish(pl.ds(UN - 128, 128))

    def z_copy(piece, peer):
        p, core, first, width, at = piece
        return remote(
            turned.at[peer, :, pl.ds(first, width)],
            landed.at[pl.ds(hint(COL * xy + 16 * c, 16), 16), pl.ds(at, width)],
            z_s.at[p], z_r.at[p], 2 * peer + core, z,
        )

    def g_wait_chunk(q):
        lanes = pl.ds(*CHUNKS[q])

        taken(got.at[pl.ds(0, ZN - 1), :, lanes], g_r.at[q])

    def z_send(piece):
        p, core, first, width, at = piece

        def z_start(off, carry):
            z_copy(piece, (xy + 7 * off) & 15).start()
            return carry

        lax.fori_loop(1, XY, z_start, 0)

        @pl.when(c == core)
        def _():
            landed[pl.ds(hint(COL * xy + 16 * c, 16), 16), at : at + width] = turned[
                xy, :, first : first + width
            ]

        @pl.when(c != core)
        def _():
            z_copy(piece, xy).start()

    def z_take(piece):
        p, core, first, width, at = piece

        @pl.when(c == core)
        def _():
            taken(landed.at[pl.ds(0, 496), pl.ds(at, width)], z_r.at[p])

            def flip(t, carry):
                lanes = pl.ds(hint(t * 128, 128), 128)
                gw_out[lanes, :] = landed[:, lanes].astype(F32).T.astype(BF)
                return carry

            lax.fori_loop(at // 128, (at + width) // 128, flip, 0)

    for q in range(3):
        g_wait_chunk(q)
        rotate16(got, turned, *CHUNKS[q])
        for piece in PIECES[q]:
            z_send(piece)
        if q:
            for piece in PIECES[q - 1]:
                z_take(piece)
    for piece in PIECES[2]:
        z_take(piece)

    for h in range(2):
        gone(acts.at[pl.ds(0, 64 * 15), :], a_s.at[h])
    gone(outs.at[pl.ds(0, COL * 15), :], ring_s)
    gone(outs.at[pl.ds(0, COL), pl.ds(0, TOK * (XY - 1))], b_s)

    @pl.when(active)
    def _():
        gone(grot.at[pl.ds(0, TOK - 16), :], f_s)
        gone(fturn.at[pl.ds(0, ZN - 1)], fb_s)

    @pl.when(jnp.logical_not(active))
    def _():
        gone(grot, f_s)

    gone(other, e_s)
    gone(own.at[pl.ds(0, ZN - 1)], g_s)
    for pieces in PIECES:
        for p, core, first, width, at in pieces:

            @pl.when(c == core)
            def _():
                gone(turned.at[pl.ds(0, XY - 1), :, pl.ds(first, width)], z_s.at[p])

            @pl.when(c != core)
            def _():
                gone(turned.at[:, :, pl.ds(first, width)], z_s.at[p])


def local(gate_pre, up_pre, grad_rot, grad_out, latent_weight, clip_codes, bits):
    table = jnp.asarray(local_table())
    vmem = pl.BlockSpec(memory_space=pltpu.VMEM)
    hbm = pl.BlockSpec(memory_space=pl.ANY)
    dma = pltpu.SemaphoreType.DMA
    grad_hidden, summed = pl.pallas_call(
        kernel,
        out_shape=(
            jax.ShapeDtypeStruct((TOK, UN), BF),
            jax.ShapeDtypeStruct((HALF, 512), BF),
        ),
        in_specs=[vmem] * 4 + [hbm],
        out_specs=(vmem, vmem),
        scratch_shapes=[
            pltpu.VMEM((XY * TOK, UN), BF),
            pltpu.VMEM((512, XY * TOK), BF),
            pltpu.VMEM((ZN, COL, UN), F32),
            pltpu.VMEM((ZN, COL, UN), BF),
            pltpu.VMEM((ZN, 16, UN), BF),
            pltpu.VMEM((ZN, 16, UN), BF),
            pltpu.VMEM((ZN, 16, UN), BF),
            pltpu.VMEM((ZN, 16, UN), BF),
            pltpu.VMEM((512, HALF), BF),
            pltpu.VMEM((TOK, UN), BF),
            pltpu.VMEM((ZN, 16, UN), BF),
            pltpu.VMEM((ZN, 16, UN), BF),
            pltpu.VMEM((TOK, UN), BF),
            pltpu.VMEM((512, TOK), BF),
            pltpu.VMEM((UN, UN), BF),
            dma(()), dma((2,)), dma((2, 10, 2)), dma(()), dma((2, 8, 2)),
            dma(()), dma(()), dma(()), dma(()),
            dma(()), dma(()), dma(()), dma((3,)),
            dma(()), dma((3,)), dma((4,)), dma((4,)),
        ],
        compiler_params=pltpu.CompilerParams(
            collective_id=0, has_side_effects=True, vmem_limit_bytes=56 * 1024 * 1024
        ),
    )(gate_pre, up_pre, grad_rot, grad_out, table)
    core = lax.axis_index("dp") & 1
    rows = jnp.where(core == 1, summed[HALF - 832 :], summed[:832])
    levels = jnp.left_shift(jnp.int32(1), bits - 1) - 1
    clip_bound = clip_codes.astype(F32) * levels.astype(F32) / 65536.0
    inside = jnp.abs(latent_weight.astype(F32)) <= clip_bound[None, :]
    grad_weight = jnp.where(inside, rows, jnp.zeros((), BF))
    gate_vals, up_vals = gate_pre.astype(F32), up_pre.astype(F32)
    gh = grad_hidden.astype(F32)
    sg = jax.nn.sigmoid(gate_vals)
    grad_gate = (gh * up_vals * sg * (1.0 + gate_vals * (1.0 - sg))).astype(BF)
    grad_up = (gh * gate_vals * sg).astype(BF)
    return grad_gate, grad_up, grad_weight


def solution(mesh):
    both = P("dp", "tensor")
    return jax.shard_map(
        local,
        mesh=mesh,
        in_specs=(both, both, both, both, both, P("tensor"), P("tensor")),
        out_specs=(both, both, both),
        check_vma=False,
    )
```

```python
import jax
import jax.numpy as jnp
import numpy as np
from jax import lax
from jax.experimental import pallas as pl
from jax.experimental.pallas import tpu as pltpu
from jax.sharding import PartitionSpec as P

HAD = 1024
NBLK = 26
MESH = pl.DeviceIdType.MESH
BF = jnp.bfloat16
F32 = jnp.float32

ZN = 16
XY = 16
TOK = 128
UN = 1664
COL = 32
HALF = 896


def local_table():
    table = np.array([[1.0]])
    for _ in range(6):
        table = np.block([[table, table], [table, -table]])
    table = np.kron(table / 8.0, np.eye(NBLK)).astype(jnp.bfloat16)
    order = np.concatenate([np.arange(832 * c + a, 832 * c + b) for a, b in ROWS for c in range(2)])
    return np.stack([table, table[:, order]])


def hint(value, multiple):
    return pl.multiple_of(value, multiple)


CHUNKS = ((0, 768), (768, 512), (1280, 384))
ROWS = ((0, 384), (384, 640), (640, 832))
PIECES = (
    ((0, 0, 0, 384, 0), (1, 1, 384, 384, 0)),
    ((2, 0, 768, 256, 384), (3, 1, 1024, 256, 384)),
    ((4, 0, 1280, 256, 640), (5, 1, 1408, 256, 640)),
)


def far_first(t):
    half = (t + 1) >> 1
    return (8 + half * (1 - 2 * (t & 1))) & 15


def rotate16(src, dst, first, width):
    def tile(t, carry):
        lanes = pl.ds(hint(t * 128, 128), 128)
        vals = [src[j, :, lanes].astype(F32) for j in range(16)]
        for bit in range(4):
            step = 1 << bit
            for j in range(16):
                if not j & step:
                    low, high = vals[j], vals[j | step]
                    vals[j], vals[j | step] = low + high, low - high
        for j in range(16):
            dst[j, :, lanes] = (vals[j] * 0.25).astype(BF)
        return carry

    lax.fori_loop(first // 128, (first + width) // 128, tile, 0)


def kernel(
    gate, up, grot, gout, tables, gg, gu, gw_out,
    acts, outs, part, send, other, own, got, turned, landed, hid, fin, fturn, fback,
    bt, table, ordered, load_sem, load_sem2, a_s, a_r, ring_s, ring_r, f_s, f_r, fb_s, fb_r, b_s, b_r, e_s, e_r, g_s, g_r, z_s, z_r,
):
    i = lax.axis_index("dp")
    z = lax.axis_index("tensor")
    c = i & 1
    xy = i >> 1
    x, y = xy >> 2, xy & 3
    k_me = z >> 1
    active = (z & 1) == c

    def remote(src, dst, ssem, rsem, dp, zz):
        return pltpu.make_async_remote_copy(
            src_ref=src, dst_ref=dst, send_sem=ssem, recv_sem=rsem,
            device_id=(dp, zz), device_id_type=MESH,
        )

    load_table = pltpu.make_async_copy(tables.at[0], table, load_sem)
    load_ordered = pltpu.make_async_copy(tables.at[1], ordered, load_sem2)
    load_ordered.start()
    load_table.start()

    def taken(ref, sem):
        remote(ref, ref, load_sem, sem, i, z ^ 1).wait_recv()

    def gone(ref, sem):
        remote(ref, ref, sem, load_sem, i, z ^ 1).wait_send()

    barrier = pltpu.get_barrier_semaphore()

    def hail_z(off, carry):
        pl.semaphore_signal(barrier, inc=1, device_id=(i, (z + off) & 15), device_id_type=MESH)
        return carry

    def hail_xy(off, carry):
        pl.semaphore_signal(barrier, inc=1, device_id=((i + off) & 31, z), device_id_type=MESH)
        return carry

    lax.fori_loop(1, ZN, hail_z, 0)
    lax.fori_loop(1, 32, hail_xy, 0)

    pl.semaphore_wait(barrier, ZN - 1 + 31)

    def f_copy(k):
        rows = pl.ds(hint(16 * k, 16), 16)
        return remote(grot.at[rows, :], fin.at[z], f_s, f_r, i, 2 * k + c)

    def f_start(j, carry):
        half = (j + 1) >> 1
        k = (k_me + 4 + half * (1 - 2 * (j & 1))) & 7

        @pl.when(2 * k + c != z)
        def _():
            f_copy(k).start()

        return carry

    lax.fori_loop(0, 3, f_start, 0)

    for t in range(4):
        lanes = slice(128 * t, 128 * (t + 1))
        bt[lanes, :] = gout[:, lanes].astype(F32).T.astype(BF)

    def b_copy(off):
        peer = (xy + 7 * off) & 15
        return remote(
            bt.at[pl.ds(hint(COL * peer, COL), COL), :],
            outs.at[pl.ds(hint(COL * z, COL), COL), pl.ds(hint(TOK * xy, TOK), TOK)],
            b_s, b_r, 2 * peer + c, z,
        )

    def b_start(off, carry):
        b_copy(off).start()
        return carry

    lax.fori_loop(1, XY, b_start, 0)
    outs[pl.ds(hint(COL * z, COL), COL), pl.ds(hint(TOK * xy, TOK), TOK)] = bt[
        pl.ds(hint(COL * xy, COL), COL), :
    ]

    @pl.when(active)
    def _():
        fin[z] = grot[pl.ds(hint(16 * k_me, 16), 16), :]

    def make_hidden(t, carry):
        lanes = pl.ds(hint(t * 128, 128), 128)
        g = gate[:, lanes].astype(F32)
        u = up[:, lanes].astype(F32)
        hid[:, lanes] = (g * jax.nn.sigmoid(g) * u).astype(BF)
        return carry

    lax.fori_loop(0, UN // 128, make_hidden, 0)
    load_ordered.wait()
    mine = pl.ds(hint(TOK * xy, TOK), TOK)

    def turn_hidden(t, carry):
        lanes = pl.ds(hint(t * 256, 256), 256)
        acts[mine, lanes] = jnp.dot(hid[...], ordered[:, lanes], preferred_element_type=F32).astype(BF)
        return carry

    lax.fori_loop(0, UN // 256, turn_hidden, 0)
    acts[mine, UN - 128 :] = jnp.dot(
        hid[...], ordered[:, UN - 128 :], preferred_element_type=F32
    ).astype(BF)

    COLS = (0, -1, 1, 2)

    def chip(h, p, q):
        return 4 * (p & 3) + (q & 3) if h == 0 else 4 * (q & 3) + (p & 3)

    def spot(h):
        return (x, y) if h == 0 else (y, x)

    def a_rows(h, blk, part):
        if part is None:
            return acts.at[pl.ds(hint(TOK * blk + 64 * h, 64), 64), :]
        return acts.at[pl.ds(hint(TOK * blk + 64 * h + 32 * part, 32), 32), :]

    def a_send(h, first_axis, blk, part, d, sem):
        p, q = spot(h)
        hop = 1 - 2 * d
        peer = chip(h, p + hop, q) if first_axis else chip(h, p, q + hop)
        ref = a_rows(h, blk, part)
        remote(ref, ref, a_s.at[h], a_r.at[h, sem, d], 2 * peer + c, z).start()

    def a_take(h, rows, d, sem):
        taken(acts.at[pl.ds(0, rows), :], a_r.at[h, sem, d])

    def first_near(h, d):
        a_send(h, True, chip(h, *spot(h)), None, d, 0)

    def first_far(h, d):
        p, q = spot(h)
        a_send(h, True, chip(h, p - 1 + 2 * d, q), d, d, 1)

    def second_near(h, j, d):
        p, q = spot(h)
        a_send(h, False, chip(h, p + COLS[j], q), None, d, 2 + j)

    def second_far(h, j, d):
        p, q = spot(h)
        a_send(h, False, chip(h, p + COLS[j], q - 1 + 2 * d), d, d, 6 + j)

    both = [(h, d) for d in range(2) for h in range(2)]
    for h, d in both:
        first_near(h, d)
    for h, d in both:
        second_near(h, 0, d)

    def ring_copy(d, s, u):
        origin = (z + 16 - s if d == 0 else z + s) & 15
        ref = outs.at[pl.ds(hint(COL * origin + 16 * u, 16), 16), :]
        peer = (z + 1 if d == 0 else z + 15) & 15
        return remote(ref, ref, ring_s, ring_r.at[d, s, u], i, peer)

    def ring_wait(d, s, u):
        taken(outs.at[pl.ds(0, 16), :], ring_r.at[d, s, u])

    def ring_step(s):
        for u in range(2):
            for d in range(2):
                ring_wait(d, s - 1, u)
                if s < 7 or u == d:
                    ring_copy(d, s, u).start()

    taken(outs.at[pl.ds(0, COL), pl.ds(0, TOK * (XY - 1))], b_r)
    for u in range(2):
        for d in range(2):
            ring_copy(d, 0, u).start()

    f_start(3, 0)
    ring_step(1)
    for h, d in both:
        a_take(h, 64, d, 0)
        first_far(h, d)
    for h, d in both:
        second_near(h, 1, d)
    f_start(4, 0)
    ring_step(2)
    for h, d in both:
        a_take(h, 64, d, 2)
        second_far(h, 0, d)
    for h, d in both:
        second_near(h, 2, d)
    f_start(5, 0)
    ring_step(3)
    for h, d in both:
        a_take(h, 32, d, 1)
    for h, d in both:
        second_near(h, 3, d)
    f_start(6, 0)
    ring_step(4)
    for j in range(1, 4):
        for h, d in both:
            a_take(h, 64, d, 2 + j)
            second_far(h, j, d)
        if j == 1:
            f_start(7, 0)
        ring_step(4 + j)
    for d in range(2):
        ring_wait(d, 7, d)
    for j in range(4):
        for h, d in both:
            a_take(h, 32, d, 6 + j)

    def fb_copy(dest):
        return remote(
            fturn.at[dest], fback.at[pl.ds(hint(16 * k_me, 16), 16), :],
            fb_s, fb_r, i, dest,
        )

    @pl.when(active)
    def _():
        taken(fin.at[pl.ds(0, ZN - 1)], f_r)
        rotate16(fin, fturn, 0, UN)

        def fb_start(t, carry):
            fb_copy((z + far_first(t)) & 15).start()
            return carry

        lax.fori_loop(0, ZN - 1, fb_start, 0)
        fback[pl.ds(hint(16 * k_me, 16), 16), :] = fturn[z]

    def product(lanes, width):
        tile = jnp.dot(outs[...], acts[:, lanes], preferred_element_type=F32)
        tile = tile.reshape(ZN, COL, width)
        part[:, :, lanes] = tile
        send[:, :, lanes] = tile.astype(BF)

    def product_chunk(q):
        first, width = CHUNKS[q]

        def product_tile(t, carry):
            product(pl.ds(hint(first + t * 256, 128), 256), 256)
            return carry

        lax.fori_loop(0, width // 256, product_tile, 0)
        if width % 256:
            product(pl.ds(first + width - 128, 128), 128)

    def swap(q):
        lanes = pl.ds(*CHUNKS[q])
        return remote(
            send.at[:, pl.ds(hint(16 * (1 - c), 16), 16), lanes], other.at[:, :, lanes],
            e_s, e_r.at[q], i ^ 1, z,
        )

    def g_copy(q, dest):
        lanes = pl.ds(*CHUNKS[q])
        return remote(
            own.at[dest, :, lanes], got.at[z, :, lanes], g_s, g_r.at[q], i, dest
        )

    def share(q):
        lanes = pl.ds(*CHUNKS[q])
        taken(other.at[:, :, lanes], e_r.at[q])

        def add_send(t, carry):
            j = (z + far_first(t)) & 15
            own[j, :, lanes] = (
                part[j, pl.ds(hint(16 * c, 16), 16), lanes] + other[j, :, lanes].astype(F32)
            ).astype(BF)

            @pl.when(t < ZN - 1)
            def _():
                g_copy(q, j).start()

            return carry

        lax.fori_loop(0, ZN, add_send, 0)
        got[z, :, lanes] = own[z, :, lanes]

    product_chunk(0)
    swap(0).start()
    product_chunk(1)
    swap(1).start()
    share(0)
    product_chunk(2)
    swap(2).start()
    share(1)
    share(2)

    @pl.when(active)
    def _():
        taken(fback.at[pl.ds(0, TOK - 16), :], fb_r)

    @pl.when(jnp.logical_not(active))
    def _():
        taken(fback, fb_r)

    def finish(lanes):
        gh = jnp.dot(fback[...], table[:, lanes], preferred_element_type=F32)
        g = gate[:, lanes].astype(F32)
        u = up[:, lanes].astype(F32)
        sg = jax.nn.sigmoid(g)
        gg[:, lanes] = (gh * u * sg * (1.0 + g * (1.0 - sg))).astype(BF)
        gu[:, lanes] = (gh * g * sg).astype(BF)

    load_table.wait()

    def finish_tile(t, carry):
        finish(pl.ds(hint(t * 256, 256), 256))
        return carry

    lax.fori_loop(0, UN // 256, finish_tile, 0)
    finish(pl.ds(UN - 128, 128))

    def z_copy(piece, peer):
        p, core, first, width, at = piece
        return remote(
            turned.at[peer, :, pl.ds(first, width)],
            landed.at[pl.ds(hint(COL * xy + 16 * c, 16), 16), pl.ds(at, width)],
            z_s.at[p], z_r.at[p], 2 * peer + core, z,
        )

    def g_wait_chunk(q):
        lanes = pl.ds(*CHUNKS[q])

        taken(got.at[pl.ds(0, ZN - 1), :, lanes], g_r.at[q])

    def z_send(piece):
        p, core, first, width, at = piece

        def z_start(off, carry):
            z_copy(piece, (xy + 7 * off) & 15).start()
            return carry

        lax.fori_loop(1, XY, z_start, 0)

        @pl.when(c == core)
        def _():
            landed[pl.ds(hint(COL * xy + 16 * c, 16), 16), at : at + width] = turned[
                xy, :, first : first + width
            ]

        @pl.when(c != core)
        def _():
            z_copy(piece, xy).start()

    def z_take(piece):
        p, core, first, width, at = piece

        @pl.when(c == core)
        def _():
            taken(landed.at[pl.ds(0, 496), pl.ds(at, width)], z_r.at[p])

            def flip(t):
                return landed[:, at + 128 * t : at + 128 * (t + 1)].astype(F32).T.astype(BF)

            if width == 256 and at == 640:
                one, two = flip(0), flip(1)
                if core == 0:
                    gw_out[640:768, :] = one
                    gw_out[768:832, :] = two[:64]
                else:
                    gw_out[640:704, :] = one[64:]
                    gw_out[704:832, :] = two
            else:
                for t in range(width // 128):
                    gw_out[at + 128 * t : at + 128 * (t + 1), :] = flip(t)

    for q in range(3):
        g_wait_chunk(q)
        rotate16(got, turned, *CHUNKS[q])
        for piece in PIECES[q]:
            z_send(piece)
        if q:
            for piece in PIECES[q - 1]:
                z_take(piece)
    for piece in PIECES[2]:
        z_take(piece)

    for h in range(2):
        gone(acts.at[pl.ds(0, 64 * 15), :], a_s.at[h])
    gone(outs.at[pl.ds(0, COL * 15), :], ring_s)
    gone(outs.at[pl.ds(0, COL), pl.ds(0, TOK * (XY - 1))], b_s)

    @pl.when(active)
    def _():
        gone(grot.at[pl.ds(0, TOK - 16), :], f_s)
        gone(fturn.at[pl.ds(0, ZN - 1)], fb_s)

    @pl.when(jnp.logical_not(active))
    def _():
        gone(grot, f_s)

    gone(other, e_s)
    gone(own.at[pl.ds(0, ZN - 1)], g_s)
    for pieces in PIECES:
        for p, core, first, width, at in pieces:

            @pl.when(c == core)
            def _():
                gone(turned.at[pl.ds(0, XY - 1), :, pl.ds(first, width)], z_s.at[p])

            @pl.when(c != core)
            def _():
                gone(turned.at[:, :, pl.ds(first, width)], z_s.at[p])


def last(gg_in, gu_in, summed, latent, codes, bits, gg, gu, gw, sem):
    moves = [pltpu.make_async_copy(src, dst, sem.at[n]) for n, (src, dst) in enumerate(((gg_in, gg), (gu_in, gu)))]
    for move in moves:
        move.start()
    levels = jnp.left_shift(jnp.int32(1), bits[...] - 1) - 1
    limit = codes[...].astype(F32) * levels.astype(F32) / 65536.0

    def mask(t, carry):
        rows = pl.ds(hint(t * 64, 64), 64)
        inside = jnp.abs(latent[rows, :].astype(F32)) <= limit
        gw[rows, :] = jnp.where(inside, summed[rows, :].astype(F32), 0.0).astype(BF)
        return carry

    lax.fori_loop(0, 13, mask, 0)
    for move in moves:
        move.wait()


def local(gate_pre, up_pre, grad_rot, grad_out, latent_weight, clip_codes, bits):
    tables = jnp.asarray(local_table())
    vmem = pl.BlockSpec(memory_space=pltpu.VMEM)
    hbm = pl.BlockSpec(memory_space=pl.ANY)
    dma = pltpu.SemaphoreType.DMA
    grad_gate, grad_up, summed = pl.pallas_call(
        kernel,
        out_shape=(
            jax.ShapeDtypeStruct((TOK, UN), BF),
            jax.ShapeDtypeStruct((TOK, UN), BF),
            jax.ShapeDtypeStruct((832, 512), BF),
        ),
        in_specs=[vmem] * 4 + [hbm],
        out_specs=(vmem, vmem, vmem),
        scratch_shapes=[
            pltpu.VMEM((XY * TOK, UN), BF),
            pltpu.VMEM((512, XY * TOK), BF),
            pltpu.VMEM((ZN, COL, UN), F32),
            pltpu.VMEM((ZN, COL, UN), BF),
            pltpu.VMEM((ZN, 16, UN), BF),
            pltpu.VMEM((ZN, 16, UN), BF),
            pltpu.VMEM((ZN, 16, UN), BF),
            pltpu.VMEM((ZN, 16, UN), BF),
            pltpu.VMEM((512, HALF), BF),
            pltpu.VMEM((TOK, UN), BF),
            pltpu.VMEM((ZN, 16, UN), BF),
            pltpu.VMEM((ZN, 16, UN), BF),
            pltpu.VMEM((TOK, UN), BF),
            pltpu.VMEM((512, TOK), BF),
            pltpu.VMEM((UN, UN), BF),
            pltpu.VMEM((UN, UN), BF),
            dma(()), dma(()), dma((2,)), dma((2, 10, 2)), dma(()), dma((2, 8, 2)),
            dma(()), dma(()), dma(()), dma(()),
            dma(()), dma(()), dma(()), dma((3,)),
            dma(()), dma((3,)), dma((6,)), dma((6,)),
        ],
        compiler_params=pltpu.CompilerParams(
            collective_id=0, has_side_effects=True, vmem_limit_bytes=56 * 1024 * 1024
        ),
    )(gate_pre, up_pre, grad_rot, grad_out, tables)
    return pl.pallas_call(
        last,
        out_shape=(
            jax.ShapeDtypeStruct((TOK, UN), BF),
            jax.ShapeDtypeStruct((TOK, UN), BF),
            jax.ShapeDtypeStruct((832, 512), BF),
        ),
        in_specs=[hbm] * 2 + [vmem] * 4,
        out_specs=(hbm, hbm, vmem),
        scratch_shapes=[dma((2,))],
    )(grad_gate, grad_up, summed, latent_weight, clip_codes[None, :], bits[None, :])


def solution(mesh):
    both = P("dp", "tensor")
    return jax.shard_map(
        local,
        mesh=mesh,
        in_specs=(both, both, both, both, both, P("tensor"), P("tensor")),
        out_specs=(both, both, both),
        check_vma=False,
    )
```

```python
import jax
import jax.numpy as jnp
import numpy as np
from jax import lax
from jax.experimental import pallas as pl
from jax.experimental.pallas import tpu as pltpu
from jax.sharding import PartitionSpec as P

HAD = 1024
NBLK = 26
MESH = pl.DeviceIdType.MESH
BF = jnp.bfloat16
F32 = jnp.float32

ZN = 16
XY = 16
TOK = 128
UN = 1664
COL = 32
HALF = 896


def local_table():
    table = np.array([[1.0]])
    for _ in range(6):
        table = np.block([[table, table], [table, -table]])
    table = np.kron(table / 8.0, np.eye(NBLK)).astype(jnp.bfloat16)
    order = np.concatenate([np.arange(832 * c + a, 832 * c + b) for a, b in ROWS for c in range(2)])
    return np.stack([table, table[:, order]])


def hint(value, multiple):
    return pl.multiple_of(value, multiple)


CHUNKS = ((0, 768), (768, 512), (1280, 384))
ROWS = ((0, 384), (384, 640), (640, 832))
PIECES = (
    ((0, 0, 0, 384, 0), (1, 1, 384, 384, 0)),
    ((2, 0, 768, 256, 384), (3, 1, 1024, 256, 384)),
    ((4, 0, 1280, 256, 640), (5, 1, 1408, 256, 640)),
)


def far_first(t):
    half = (t + 1) >> 1
    return (8 + half * (1 - 2 * (t & 1))) & 15


def rotate16(src, dst, first, width):
    def tile(t, carry):
        lanes = pl.ds(hint(t * 128, 128), 128)
        vals = [src[j, :, lanes].astype(F32) for j in range(16)]
        for bit in range(4):
            step = 1 << bit
            for j in range(16):
                if not j & step:
                    low, high = vals[j], vals[j | step]
                    vals[j], vals[j | step] = low + high, low - high
        for j in range(16):
            dst[j, :, lanes] = (vals[j] * 0.25).astype(BF)
        return carry

    lax.fori_loop(first // 128, (first + width) // 128, tile, 0)


def kernel(
    gate, up, grot, gout, tables, gg, gu, gw_out,
    acts, outs, part, send, other, own, got, turned, landed, hid, fin, fturn, fback,
    bt, table, ordered, load_sem, load_sem2, a_s, a_r, ring_s, ring_r, f_s, f_r, fb_s, fb_r, b_s, b_r, e_s, e_r, g_s, g_r, z_s, z_r,
):
    i = lax.axis_index("dp")
    z = lax.axis_index("tensor")
    c = i & 1
    xy = i >> 1
    x, y = xy >> 2, xy & 3
    k_me = z >> 1
    active = (z & 1) == c

    def remote(src, dst, ssem, rsem, dp, zz):
        return pltpu.make_async_remote_copy(
            src_ref=src, dst_ref=dst, send_sem=ssem, recv_sem=rsem,
            device_id=(dp, zz), device_id_type=MESH,
        )

    def load(n, dst, sem):
        def load_rows(t, carry):
            rows = pl.ds(hint(t * 128, 128), 128)
            pltpu.make_async_copy(tables.at[n, rows, :], dst.at[rows, :], sem).start()
            return carry

        lax.fori_loop(0, UN // 128, load_rows, 0)

    load(1, ordered, load_sem2)

    def taken(ref, sem):
        remote(ref, ref, load_sem, sem, i, z ^ 1).wait_recv()

    def gone(ref, sem):
        remote(ref, ref, sem, load_sem, i, z ^ 1).wait_send()

    barrier = pltpu.get_barrier_semaphore()

    def hail_z(off, carry):
        pl.semaphore_signal(barrier, inc=1, device_id=(i, (z + off) & 15), device_id_type=MESH)
        return carry

    def hail_xy(off, carry):
        pl.semaphore_signal(barrier, inc=1, device_id=((i + off) & 31, z), device_id_type=MESH)
        return carry

    lax.fori_loop(1, ZN, hail_z, 0)
    lax.fori_loop(1, 32, hail_xy, 0)

    pl.semaphore_wait(barrier, ZN - 1 + 31)

    def f_copy(k):
        rows = pl.ds(hint(16 * k, 16), 16)
        return remote(grot.at[rows, :], fin.at[z], f_s, f_r, i, 2 * k + c)

    def f_start(j, carry):
        half = (j + 1) >> 1
        k = (k_me + 4 + half * (1 - 2 * (j & 1))) & 7

        @pl.when(2 * k + c != z)
        def _():
            f_copy(k).start()

        return carry

    lax.fori_loop(0, 3, f_start, 0)

    for t in range(4):
        lanes = slice(128 * t, 128 * (t + 1))
        bt[lanes, :] = gout[:, lanes].astype(F32).T.astype(BF)

    def b_copy(off):
        peer = (xy + 7 * off) & 15
        return remote(
            bt.at[pl.ds(hint(COL * peer, COL), COL), :],
            outs.at[pl.ds(hint(COL * z, COL), COL), pl.ds(hint(TOK * xy, TOK), TOK)],
            b_s, b_r, 2 * peer + c, z,
        )

    def b_start(off, carry):
        b_copy(off).start()
        return carry

    lax.fori_loop(1, XY, b_start, 0)
    outs[pl.ds(hint(COL * z, COL), COL), pl.ds(hint(TOK * xy, TOK), TOK)] = bt[
        pl.ds(hint(COL * xy, COL), COL), :
    ]

    @pl.when(active)
    def _():
        fin[z] = grot[pl.ds(hint(16 * k_me, 16), 16), :]

    def make_hidden(t, carry):
        lanes = pl.ds(hint(t * 128, 128), 128)
        g = gate[:, lanes].astype(F32)
        u = up[:, lanes].astype(F32)
        hid[:, lanes] = (g * jax.nn.sigmoid(g) * u).astype(BF)
        return carry

    lax.fori_loop(0, UN // 128, make_hidden, 0)
    pltpu.make_async_copy(tables.at[1], ordered, load_sem2).wait()
    mine = pl.ds(hint(TOK * xy, TOK), TOK)

    def turn_hidden(t, carry):
        lanes = pl.ds(hint(t * 256, 256), 256)
        acts[mine, lanes] = jnp.dot(hid[...], ordered[:, lanes], preferred_element_type=F32).astype(BF)
        return carry

    lax.fori_loop(0, UN // 256, turn_hidden, 0)
    acts[mine, UN - 128 :] = jnp.dot(
        hid[...], ordered[:, UN - 128 :], preferred_element_type=F32
    ).astype(BF)

    COLS = (0, -1, 1, 2)

    def chip(h, p, q):
        return 4 * (p & 3) + (q & 3) if h == 0 else 4 * (q & 3) + (p & 3)

    def spot(h):
        return (x, y) if h == 0 else (y, x)

    def a_rows(h, blk, part):
        if part is None:
            return acts.at[pl.ds(hint(TOK * blk + 64 * h, 64), 64), :]
        return acts.at[pl.ds(hint(TOK * blk + 64 * h + 32 * part, 32), 32), :]

    def a_send(h, first_axis, blk, part, d, sem):
        p, q = spot(h)
        hop = 1 - 2 * d
        peer = chip(h, p + hop, q) if first_axis else chip(h, p, q + hop)
        ref = a_rows(h, blk, part)
        remote(ref, ref, a_s.at[h], a_r.at[h, sem, d], 2 * peer + c, z).start()

    def a_take(h, rows, d, sem):
        taken(acts.at[pl.ds(0, rows), :], a_r.at[h, sem, d])

    def first_near(h, d):
        a_send(h, True, chip(h, *spot(h)), None, d, 0)

    def first_far(h, d):
        p, q = spot(h)
        a_send(h, True, chip(h, p - 1 + 2 * d, q), d, d, 1)

    def second_near(h, j, d):
        p, q = spot(h)
        a_send(h, False, chip(h, p + COLS[j], q), None, d, 2 + j)

    def second_far(h, j, d):
        p, q = spot(h)
        a_send(h, False, chip(h, p + COLS[j], q - 1 + 2 * d), d, d, 6 + j)

    both = [(h, d) for d in range(2) for h in range(2)]
    for h, d in both:
        first_near(h, d)
    for h, d in both:
        second_near(h, 0, d)

    load(0, table, load_sem)

    def ring_copy(d, s, u):
        origin = (z + 16 - s if d == 0 else z + s) & 15
        ref = outs.at[pl.ds(hint(COL * origin + 16 * u, 16), 16), :]
        peer = (z + 1 if d == 0 else z + 15) & 15
        return remote(ref, ref, ring_s, ring_r.at[d, s, u], i, peer)

    def ring_wait(d, s, u):
        taken(outs.at[pl.ds(0, 16), :], ring_r.at[d, s, u])

    def ring_step(s):
        for u in range(2):
            for d in range(2):
                ring_wait(d, s - 1, u)
                if s < 7 or u == d:
                    ring_copy(d, s, u).start()

    taken(outs.at[pl.ds(0, COL), pl.ds(0, TOK * (XY - 1))], b_r)
    for u in range(2):
        for d in range(2):
            ring_copy(d, 0, u).start()

    f_start(3, 0)
    ring_step(1)
    for h, d in both:
        a_take(h, 64, d, 0)
        first_far(h, d)
    for h, d in both:
        second_near(h, 1, d)
    f_start(4, 0)
    ring_step(2)
    for h, d in both:
        a_take(h, 64, d, 2)
        second_far(h, 0, d)
    for h, d in both:
        second_near(h, 2, d)
    f_start(5, 0)
    ring_step(3)
    for h, d in both:
        a_take(h, 32, d, 1)
    for h, d in both:
        second_near(h, 3, d)
    f_start(6, 0)
    ring_step(4)
    for j in range(1, 4):
        for h, d in both:
            a_take(h, 64, d, 2 + j)
            second_far(h, j, d)
        if j == 1:
            f_start(7, 0)
        ring_step(4 + j)
    def fb_copy(dest):
        return remote(
            fturn.at[dest], fback.at[pl.ds(hint(16 * k_me, 16), 16), :],
            fb_s, fb_r, i, dest,
        )

    @pl.when(active)
    def _():
        taken(fin.at[pl.ds(0, ZN - 1)], f_r)
        rotate16(fin, fturn, 0, UN)

        def fb_start(t, carry):
            fb_copy((z + far_first(t)) & 15).start()
            return carry

        lax.fori_loop(0, ZN - 1, fb_start, 0)
        fback[pl.ds(hint(16 * k_me, 16), 16), :] = fturn[z]

    for d in range(2):
        ring_wait(d, 7, d)
    for j in range(4):
        for h, d in both:
            a_take(h, 32, d, 6 + j)

    def product(lanes, width):
        tile = jnp.dot(outs[...], acts[:, lanes], preferred_element_type=F32)
        tile = tile.reshape(ZN, COL, width)
        part[:, :, lanes] = tile
        send[:, :, lanes] = tile.astype(BF)

    def product_chunk(q):
        first, width = CHUNKS[q]

        def product_tile(t, carry):
            product(pl.ds(hint(first + t * 256, 128), 256), 256)
            return carry

        lax.fori_loop(0, width // 256, product_tile, 0)
        if width % 256:
            product(pl.ds(first + width - 128, 128), 128)

    def swap(q):
        lanes = pl.ds(*CHUNKS[q])
        return remote(
            send.at[:, pl.ds(hint(16 * (1 - c), 16), 16), lanes], other.at[:, :, lanes],
            e_s, e_r.at[q], i ^ 1, z,
        )

    def g_copy(q, dest):
        lanes = pl.ds(*CHUNKS[q])
        return remote(
            own.at[dest, :, lanes], got.at[z, :, lanes], g_s, g_r.at[q], i, dest
        )

    def share(q):
        lanes = pl.ds(*CHUNKS[q])
        taken(other.at[:, :, lanes], e_r.at[q])

        def add_send(t, carry):
            j = (z + far_first(t)) & 15
            own[j, :, lanes] = (
                part[j, pl.ds(hint(16 * c, 16), 16), lanes] + other[j, :, lanes].astype(F32)
            ).astype(BF)

            @pl.when(t < ZN - 1)
            def _():
                g_copy(q, j).start()

            return carry

        lax.fori_loop(0, ZN, add_send, 0)
        got[z, :, lanes] = own[z, :, lanes]

    product_chunk(0)
    swap(0).start()
    product_chunk(1)
    swap(1).start()
    share(0)
    product_chunk(2)
    swap(2).start()
    share(1)
    share(2)

    @pl.when(active)
    def _():
        taken(fback.at[pl.ds(0, TOK - 16), :], fb_r)

    @pl.when(jnp.logical_not(active))
    def _():
        taken(fback, fb_r)

    def finish(lanes):
        gh = jnp.dot(fback[...], table[:, lanes], preferred_element_type=F32)
        g = gate[:, lanes].astype(F32)
        u = up[:, lanes].astype(F32)
        sg = jax.nn.sigmoid(g)
        gg[:, lanes] = (gh * u * sg * (1.0 + g * (1.0 - sg))).astype(BF)
        gu[:, lanes] = (gh * g * sg).astype(BF)

    pltpu.make_async_copy(tables.at[0], table, load_sem).wait()

    def finish_tile(t, carry):
        finish(pl.ds(hint(t * 256, 256), 256))
        return carry

    lax.fori_loop(0, UN // 256, finish_tile, 0)
    finish(pl.ds(UN - 128, 128))

    def z_copy(piece, peer):
        p, core, first, width, at = piece
        return remote(
            turned.at[peer, :, pl.ds(first, width)],
            landed.at[pl.ds(hint(COL * xy + 16 * c, 16), 16), pl.ds(at, width)],
            z_s.at[p], z_r.at[p], 2 * peer + core, z,
        )

    def g_wait_chunk(q):
        lanes = pl.ds(*CHUNKS[q])

        taken(got.at[pl.ds(0, ZN - 1), :, lanes], g_r.at[q])

    def z_send(piece):
        p, core, first, width, at = piece

        def z_start(off, carry):
            z_copy(piece, (xy + 7 * off) & 15).start()
            return carry

        lax.fori_loop(1, XY, z_start, 0)

        @pl.when(c == core)
        def _():
            landed[pl.ds(hint(COL * xy + 16 * c, 16), 16), at : at + width] = turned[
                xy, :, first : first + width
            ]

        @pl.when(c != core)
        def _():
            z_copy(piece, xy).start()

    def z_take(piece):
        p, core, first, width, at = piece

        @pl.when(c == core)
        def _():
            taken(landed.at[pl.ds(0, 496), pl.ds(at, width)], z_r.at[p])

            def flip(t):
                return landed[:, at + 128 * t : at + 128 * (t + 1)].astype(F32).T.astype(BF)

            if width == 256 and at == 640:
                one, two = flip(0), flip(1)
                if core == 0:
                    gw_out[640:768, :] = one
                    gw_out[768:832, :] = two[:64]
                else:
                    gw_out[640:704, :] = one[64:]
                    gw_out[704:832, :] = two
            else:
                for t in range(width // 128):
                    gw_out[at + 128 * t : at + 128 * (t + 1), :] = flip(t)

    for q in range(3):
        g_wait_chunk(q)
        rotate16(got, turned, *CHUNKS[q])
        for piece in PIECES[q]:
            z_send(piece)
        if q:
            for piece in PIECES[q - 1]:
                z_take(piece)
    for piece in PIECES[2]:
        z_take(piece)

    for h in range(2):
        gone(acts.at[pl.ds(0, 64 * 15), :], a_s.at[h])
    gone(outs.at[pl.ds(0, COL * 15), :], ring_s)
    gone(outs.at[pl.ds(0, COL), pl.ds(0, TOK * (XY - 1))], b_s)

    @pl.when(active)
    def _():
        gone(grot.at[pl.ds(0, TOK - 16), :], f_s)
        gone(fturn.at[pl.ds(0, ZN - 1)], fb_s)

    @pl.when(jnp.logical_not(active))
    def _():
        gone(grot, f_s)

    gone(other, e_s)
    gone(own.at[pl.ds(0, ZN - 1)], g_s)
    for pieces in PIECES:
        for p, core, first, width, at in pieces:

            @pl.when(c == core)
            def _():
                gone(turned.at[pl.ds(0, XY - 1), :, pl.ds(first, width)], z_s.at[p])

            @pl.when(c != core)
            def _():
                gone(turned.at[:, :, pl.ds(first, width)], z_s.at[p])


def last(gg_in, gu_in, summed, latent, codes, bits, gg, gu, gw):
    levels = jnp.left_shift(jnp.int32(1), bits[...] - 1) - 1
    limit = codes[...].astype(F32) * levels.astype(F32) / 65536.0

    def mask(t, carry):
        rows = pl.ds(hint(t * 64, 64), 64)
        inside = jnp.abs(latent[rows, :].astype(F32)) <= limit
        gw[rows, :] = jnp.where(inside, summed[rows, :].astype(F32), 0.0).astype(BF)
        return carry

    lax.fori_loop(0, 13, mask, 0)
    gg[...] = gg_in[...]
    gu[...] = gu_in[...]


def local(gate_pre, up_pre, grad_rot, grad_out, latent_weight, clip_codes, bits):
    tables = jnp.asarray(local_table())
    vmem = pl.BlockSpec(memory_space=pltpu.VMEM)
    hbm = pl.BlockSpec(memory_space=pl.ANY)
    dma = pltpu.SemaphoreType.DMA
    grad_gate, grad_up, summed = pl.pallas_call(
        kernel,
        out_shape=(
            jax.ShapeDtypeStruct((TOK, UN), BF),
            jax.ShapeDtypeStruct((TOK, UN), BF),
            jax.ShapeDtypeStruct((832, 512), BF),
        ),
        in_specs=[vmem] * 4 + [hbm],
        out_specs=(vmem, vmem, vmem),
        scratch_shapes=[
            pltpu.VMEM((XY * TOK, UN), BF),
            pltpu.VMEM((512, XY * TOK), BF),
            pltpu.VMEM((ZN, COL, UN), F32),
            pltpu.VMEM((ZN, COL, UN), BF),
            pltpu.VMEM((ZN, 16, UN), BF),
            pltpu.VMEM((ZN, 16, UN), BF),
            pltpu.VMEM((ZN, 16, UN), BF),
            pltpu.VMEM((ZN, 16, UN), BF),
            pltpu.VMEM((512, HALF), BF),
            pltpu.VMEM((TOK, UN), BF),
            pltpu.VMEM((ZN, 16, UN), BF),
            pltpu.VMEM((ZN, 16, UN), BF),
            pltpu.VMEM((TOK, UN), BF),
            pltpu.VMEM((512, TOK), BF),
            pltpu.VMEM((UN, UN), BF),
            pltpu.VMEM((UN, UN), BF),
            dma(()), dma(()), dma((2,)), dma((2, 10, 2)), dma(()), dma((2, 8, 2)),
            dma(()), dma(()), dma(()), dma(()),
            dma(()), dma(()), dma(()), dma((3,)),
            dma(()), dma((3,)), dma((6,)), dma((6,)),
        ],
        compiler_params=pltpu.CompilerParams(
            collective_id=0, has_side_effects=True, vmem_limit_bytes=56 * 1024 * 1024
        ),
    )(gate_pre, up_pre, grad_rot, grad_out, tables)
    return pl.pallas_call(
        last,
        out_shape=(
            jax.ShapeDtypeStruct((TOK, UN), BF),
            jax.ShapeDtypeStruct((TOK, UN), BF),
            jax.ShapeDtypeStruct((832, 512), BF),
        ),
        in_specs=[vmem] * 6,
        out_specs=(vmem, vmem, vmem),
    )(grad_gate, grad_up, summed, latent_weight, clip_codes[None, :], bits[None, :])


def solution(mesh):
    both = P("dp", "tensor")
    return jax.shard_map(
        local,
        mesh=mesh,
        in_specs=(both, both, both, both, both, P("tensor"), P("tensor")),
        out_specs=(both, both, both),
        check_vma=False,
    )
```

```python
import jax
import jax.numpy as jnp
import numpy as np
from jax import lax
from jax.experimental import pallas as pl
from jax.experimental.pallas import tpu as pltpu
from jax.sharding import PartitionSpec as P

HAD = 1024
NBLK = 26
MESH = pl.DeviceIdType.MESH
BF = jnp.bfloat16
F32 = jnp.float32

ZN = 16
XY = 16
TOK = 128
UN = 1664
COL = 32
HALF = 896


def local_table():
    table = np.array([[1.0]])
    for _ in range(6):
        table = np.block([[table, table], [table, -table]])
    table = np.kron(table / 8.0, np.eye(NBLK)).astype(jnp.bfloat16)
    order = np.concatenate([np.arange(832 * c + a, 832 * c + b) for a, b in ROWS for c in range(2)])
    return np.stack([table, table[:, order]])


def hint(value, multiple):
    return pl.multiple_of(value, multiple)


CHUNKS = ((0, 768), (768, 512), (1280, 384))
ROWS = ((0, 384), (384, 640), (640, 832))
PIECES = (
    ((0, 0, 0, 384, 0), (1, 1, 384, 384, 0)),
    ((2, 0, 768, 256, 384), (3, 1, 1024, 256, 384)),
    ((4, 0, 1280, 256, 640), (5, 1, 1408, 256, 640)),
)


def far_first(t):
    half = (t + 1) >> 1
    return (8 + half * (1 - 2 * (t & 1))) & 15


def rotate16(src, dst, first, width):
    def tile(t, carry):
        lanes = pl.ds(hint(t * 128, 128), 128)
        vals = [src[j, :, lanes].astype(F32) for j in range(16)]
        for bit in range(4):
            step = 1 << bit
            for j in range(16):
                if not j & step:
                    low, high = vals[j], vals[j | step]
                    vals[j], vals[j | step] = low + high, low - high
        for j in range(16):
            dst[j, :, lanes] = (vals[j] * 0.25).astype(BF)
        return carry

    lax.fori_loop(first // 128, (first + width) // 128, tile, 0)


def kernel(
    gate, up, grot, gout, tables, gg, gu, gw_out,
    acts, outs, part, send, other, own, got, turned, landed, hid, fin, fturn, fback,
    bt, table, ordered, load_sem, load_sem2, a_s, a_r, ring_s, ring_r, f_s, f_r, fb_s, fb_r, b_s, b_r, e_s, e_r, g_s, g_r, z_s, z_r,
):
    i = lax.axis_index("dp")
    z = lax.axis_index("tensor")
    c = i & 1
    xy = i >> 1
    x, y = xy >> 2, xy & 3
    k_me = z >> 1
    active = (z & 1) == c

    def remote(src, dst, ssem, rsem, dp, zz):
        return pltpu.make_async_remote_copy(
            src_ref=src, dst_ref=dst, send_sem=ssem, recv_sem=rsem,
            device_id=(dp, zz), device_id_type=MESH,
        )

    def load(n, dst, sem):
        def load_rows(t, carry):
            rows = pl.ds(hint(t * 128, 128), 128)
            pltpu.make_async_copy(tables.at[n, rows, :], dst.at[rows, :], sem).start()
            return carry

        lax.fori_loop(0, UN // 128, load_rows, 0)

    load(1, ordered, load_sem2)

    def taken(ref, sem):
        remote(ref, ref, load_sem, sem, i, z ^ 1).wait_recv()

    def gone(ref, sem):
        remote(ref, ref, sem, load_sem, i, z ^ 1).wait_send()

    barrier = pltpu.get_barrier_semaphore()

    def hail_z(off, carry):
        pl.semaphore_signal(barrier, inc=1, device_id=(i, (z + off) & 15), device_id_type=MESH)
        return carry

    def hail_xy(off, carry):
        pl.semaphore_signal(barrier, inc=1, device_id=((i + off) & 31, z), device_id_type=MESH)
        return carry

    lax.fori_loop(1, ZN, hail_z, 0)
    lax.fori_loop(1, 32, hail_xy, 0)

    pl.semaphore_wait(barrier, ZN - 1 + 31)

    def f_copy(k):
        rows = pl.ds(hint(16 * k, 16), 16)
        return remote(grot.at[rows, :], fin.at[z], f_s, f_r, i, 2 * k + c)

    def f_start(j, carry):
        half = (j + 1) >> 1
        k = (k_me + 4 + half * (1 - 2 * (j & 1))) & 7

        @pl.when(2 * k + c != z)
        def _():
            f_copy(k).start()

        return carry

    lax.fori_loop(0, 3, f_start, 0)

    for t in range(4):
        lanes = slice(128 * t, 128 * (t + 1))
        bt[lanes, :] = gout[:, lanes].astype(F32).T.astype(BF)

    def b_copy(off):
        peer = (xy + 7 * off) & 15
        return remote(
            bt.at[pl.ds(hint(COL * peer, COL), COL), :],
            outs.at[pl.ds(hint(COL * z, COL), COL), pl.ds(hint(TOK * xy, TOK), TOK)],
            b_s, b_r, 2 * peer + c, z,
        )

    def b_start(off, carry):
        b_copy(off).start()
        return carry

    lax.fori_loop(1, XY, b_start, 0)
    outs[pl.ds(hint(COL * z, COL), COL), pl.ds(hint(TOK * xy, TOK), TOK)] = bt[
        pl.ds(hint(COL * xy, COL), COL), :
    ]

    @pl.when(active)
    def _():
        fin[z] = grot[pl.ds(hint(16 * k_me, 16), 16), :]

    def make_hidden(t, carry):
        lanes = pl.ds(hint(t * 128, 128), 128)
        g = gate[:, lanes].astype(F32)
        u = up[:, lanes].astype(F32)
        hid[:, lanes] = (g * jax.nn.sigmoid(g) * u).astype(BF)
        return carry

    lax.fori_loop(0, UN // 128, make_hidden, 0)
    pltpu.make_async_copy(tables.at[1], ordered, load_sem2).wait()
    mine = pl.ds(hint(TOK * xy, TOK), TOK)

    def turn_hidden(t, carry):
        lanes = pl.ds(hint(t * 256, 256), 256)
        acts[mine, lanes] = jnp.dot(hid[...], ordered[:, lanes], preferred_element_type=F32).astype(BF)
        return carry

    lax.fori_loop(0, UN // 256, turn_hidden, 0)
    acts[mine, UN - 128 :] = jnp.dot(
        hid[...], ordered[:, UN - 128 :], preferred_element_type=F32
    ).astype(BF)

    COLS = (0, -1, 1, 2)

    def chip(h, p, q):
        return 4 * (p & 3) + (q & 3) if h == 0 else 4 * (q & 3) + (p & 3)

    def spot(h):
        return (x, y) if h == 0 else (y, x)

    def a_rows(h, blk, part):
        if part is None:
            return acts.at[pl.ds(hint(TOK * blk + 64 * h, 64), 64), :]
        return acts.at[pl.ds(hint(TOK * blk + 64 * h + 32 * part, 32), 32), :]

    def a_send(h, first_axis, blk, part, d, sem):
        p, q = spot(h)
        hop = 1 - 2 * d
        peer = chip(h, p + hop, q) if first_axis else chip(h, p, q + hop)
        ref = a_rows(h, blk, part)
        remote(ref, ref, a_s.at[h], a_r.at[h, sem, d], 2 * peer + c, z).start()

    def a_take(h, rows, d, sem):
        taken(acts.at[pl.ds(0, rows), :], a_r.at[h, sem, d])

    def first_near(h, d):
        a_send(h, True, chip(h, *spot(h)), None, d, 0)

    def first_far(h, d):
        p, q = spot(h)
        a_send(h, True, chip(h, p - 1 + 2 * d, q), d, d, 1)

    def second_near(h, j, d):
        p, q = spot(h)
        a_send(h, False, chip(h, p + COLS[j], q), None, d, 2 + j)

    def second_far(h, j, d):
        p, q = spot(h)
        a_send(h, False, chip(h, p + COLS[j], q - 1 + 2 * d), d, d, 6 + j)

    load(0, table, load_sem)

    def ring_copy(d, s, u):
        origin = (z + 16 - s if d == 0 else z + s) & 15
        ref = outs.at[pl.ds(hint(COL * origin + 16 * u, 16), 16), :]
        peer = (z + 1 if d == 0 else z + 15) & 15
        return remote(ref, ref, ring_s, ring_r.at[d, s, u], i, peer)

    def ring_wait(d, s, u):
        taken(outs.at[pl.ds(0, 16), :], ring_r.at[d, s, u])

    def ring_step(s):
        for u in range(2):
            for d in range(2):
                ring_wait(d, s - 1, u)
                if s < 7 or u == d:
                    ring_copy(d, s, u).start()

    taken(outs.at[pl.ds(0, COL), pl.ds(0, TOK * (XY - 1))], b_r)
    for u in range(2):
        for d in range(2):
            ring_copy(d, 0, u).start()

    both = [(h, d) for d in range(2) for h in range(2)]
    for h, d in both:
        first_near(h, d)
    for h, d in both:
        second_near(h, 0, d)

    f_start(3, 0)
    ring_step(1)
    for h, d in both:
        a_take(h, 64, d, 0)
        first_far(h, d)
    for h, d in both:
        second_near(h, 1, d)
    f_start(4, 0)
    ring_step(2)
    for h, d in both:
        a_take(h, 64, d, 2)
        second_far(h, 0, d)
    for h, d in both:
        second_near(h, 2, d)
    f_start(5, 0)
    ring_step(3)
    for h, d in both:
        a_take(h, 32, d, 1)
    for h, d in both:
        second_near(h, 3, d)
    f_start(6, 0)
    ring_step(4)
    for j in range(1, 4):
        for h, d in both:
            a_take(h, 64, d, 2 + j)
            second_far(h, j, d)
        if j == 1:
            f_start(7, 0)
        ring_step(4 + j)
    def fb_copy(dest):
        return remote(
            fturn.at[dest], fback.at[pl.ds(hint(16 * k_me, 16), 16), :],
            fb_s, fb_r, i, dest,
        )

    def send_back(first, last_one):
        @pl.when(active)
        def _():
            def fb_start(t, carry):
                fb_copy((z + far_first(t)) & 15).start()
                return carry

            lax.fori_loop(first, last_one, fb_start, 0)

    @pl.when(active)
    def _():
        taken(fin.at[pl.ds(0, ZN - 1)], f_r)
        rotate16(fin, fturn, 0, UN)
        fback[pl.ds(hint(16 * k_me, 16), 16), :] = fturn[z]

    send_back(0, 5)

    for d in range(2):
        ring_wait(d, 7, d)
    for j in range(4):
        for h, d in both:
            a_take(h, 32, d, 6 + j)

    def product(lanes, width):
        tile = jnp.dot(outs[...], acts[:, lanes], preferred_element_type=F32)
        tile = tile.reshape(ZN, COL, width)
        part[:, :, lanes] = tile
        send[:, :, lanes] = tile.astype(BF)

    def product_chunk(q):
        first, width = CHUNKS[q]

        def product_tile(t, carry):
            product(pl.ds(hint(first + t * 256, 128), 256), 256)
            return carry

        lax.fori_loop(0, width // 256, product_tile, 0)
        if width % 256:
            product(pl.ds(first + width - 128, 128), 128)

    def swap(q):
        lanes = pl.ds(*CHUNKS[q])
        return remote(
            send.at[:, pl.ds(hint(16 * (1 - c), 16), 16), lanes], other.at[:, :, lanes],
            e_s, e_r.at[q], i ^ 1, z,
        )

    def g_copy(q, dest):
        lanes = pl.ds(*CHUNKS[q])
        return remote(
            own.at[dest, :, lanes], got.at[z, :, lanes], g_s, g_r.at[q], i, dest
        )

    def share(q):
        lanes = pl.ds(*CHUNKS[q])
        taken(other.at[:, :, lanes], e_r.at[q])

        def add_send(t, carry):
            j = (z + far_first(t)) & 15
            own[j, :, lanes] = (
                part[j, pl.ds(hint(16 * c, 16), 16), lanes] + other[j, :, lanes].astype(F32)
            ).astype(BF)

            @pl.when(t < ZN - 1)
            def _():
                g_copy(q, j).start()

            return carry

        lax.fori_loop(0, ZN, add_send, 0)
        got[z, :, lanes] = own[z, :, lanes]

    product_chunk(0)
    swap(0).start()
    send_back(5, ZN - 1)
    product_chunk(1)
    swap(1).start()
    share(0)
    product_chunk(2)
    swap(2).start()
    share(1)
    share(2)

    @pl.when(active)
    def _():
        taken(fback.at[pl.ds(0, TOK - 16), :], fb_r)

    @pl.when(jnp.logical_not(active))
    def _():
        taken(fback, fb_r)

    def finish(lanes):
        gh = jnp.dot(fback[...], table[:, lanes], preferred_element_type=F32)
        g = gate[:, lanes].astype(F32)
        u = up[:, lanes].astype(F32)
        sg = jax.nn.sigmoid(g)
        gg[:, lanes] = (gh * u * sg * (1.0 + g * (1.0 - sg))).astype(BF)
        gu[:, lanes] = (gh * g * sg).astype(BF)

    pltpu.make_async_copy(tables.at[0], table, load_sem).wait()

    def finish_tile(t, carry):
        finish(pl.ds(hint(t * 256, 256), 256))
        return carry

    lax.fori_loop(0, UN // 256, finish_tile, 0)
    finish(pl.ds(UN - 128, 128))

    def z_copy(piece, peer):
        p, core, first, width, at = piece
        return remote(
            turned.at[peer, :, pl.ds(first, width)],
            landed.at[pl.ds(hint(COL * xy + 16 * c, 16), 16), pl.ds(at, width)],
            z_s.at[p], z_r.at[p], 2 * peer + core, z,
        )

    def g_wait_chunk(q):
        lanes = pl.ds(*CHUNKS[q])

        taken(got.at[pl.ds(0, ZN - 1), :, lanes], g_r.at[q])

    def z_send(piece):
        p, core, first, width, at = piece

        def z_start(off, carry):
            z_copy(piece, (xy + 7 * off) & 15).start()
            return carry

        lax.fori_loop(1, XY, z_start, 0)

        @pl.when(c == core)
        def _():
            landed[pl.ds(hint(COL * xy + 16 * c, 16), 16), at : at + width] = turned[
                xy, :, first : first + width
            ]

        @pl.when(c != core)
        def _():
            z_copy(piece, xy).start()

    def z_take(piece):
        p, core, first, width, at = piece

        @pl.when(c == core)
        def _():
            taken(landed.at[pl.ds(0, 496), pl.ds(at, width)], z_r.at[p])

            def flip(t):
                return landed[:, at + 128 * t : at + 128 * (t + 1)].astype(F32).T.astype(BF)

            if width == 256 and at == 640:
                one, two = flip(0), flip(1)
                if core == 0:
                    gw_out[640:768, :] = one
                    gw_out[768:832, :] = two[:64]
                else:
                    gw_out[640:704, :] = one[64:]
                    gw_out[704:832, :] = two
            else:
                for t in range(width // 128):
                    gw_out[at + 128 * t : at + 128 * (t + 1), :] = flip(t)

    for q in range(3):
        g_wait_chunk(q)
        rotate16(got, turned, *CHUNKS[q])
        for piece in PIECES[q]:
            z_send(piece)
        if q:
            for piece in PIECES[q - 1]:
                z_take(piece)
    for piece in PIECES[2]:
        z_take(piece)

    for h in range(2):
        gone(acts.at[pl.ds(0, 64 * 15), :], a_s.at[h])
    gone(outs.at[pl.ds(0, COL * 15), :], ring_s)
    gone(outs.at[pl.ds(0, COL), pl.ds(0, TOK * (XY - 1))], b_s)

    @pl.when(active)
    def _():
        gone(grot.at[pl.ds(0, TOK - 16), :], f_s)
        gone(fturn.at[pl.ds(0, ZN - 1)], fb_s)

    @pl.when(jnp.logical_not(active))
    def _():
        gone(grot, f_s)

    gone(other, e_s)
    gone(own.at[pl.ds(0, ZN - 1)], g_s)
    for pieces in PIECES:
        for p, core, first, width, at in pieces:

            @pl.when(c == core)
            def _():
                gone(turned.at[pl.ds(0, XY - 1), :, pl.ds(first, width)], z_s.at[p])

            @pl.when(c != core)
            def _():
                gone(turned.at[:, :, pl.ds(first, width)], z_s.at[p])


def last(gg_in, gu_in, summed, latent, codes, bits, gg, gu, gw):
    levels = jnp.left_shift(jnp.int32(1), bits[...] - 1) - 1
    limit = codes[...].astype(F32) * levels.astype(F32) / 65536.0

    def mask(t, carry):
        rows = pl.ds(hint(t * 64, 64), 64)
        inside = jnp.abs(latent[rows, :].astype(F32)) <= limit
        gw[rows, :] = jnp.where(inside, summed[rows, :].astype(F32), 0.0).astype(BF)
        return carry

    lax.fori_loop(0, 13, mask, 0)
    gg[...] = gg_in[...]
    gu[...] = gu_in[...]


def local(gate_pre, up_pre, grad_rot, grad_out, latent_weight, clip_codes, bits):
    tables = jnp.asarray(local_table())
    vmem = pl.BlockSpec(memory_space=pltpu.VMEM)
    hbm = pl.BlockSpec(memory_space=pl.ANY)
    dma = pltpu.SemaphoreType.DMA
    grad_gate, grad_up, summed = pl.pallas_call(
        kernel,
        out_shape=(
            jax.ShapeDtypeStruct((TOK, UN), BF),
            jax.ShapeDtypeStruct((TOK, UN), BF),
            jax.ShapeDtypeStruct((832, 512), BF),
        ),
        in_specs=[vmem] * 4 + [hbm],
        out_specs=(vmem, vmem, vmem),
        scratch_shapes=[
            pltpu.VMEM((XY * TOK, UN), BF),
            pltpu.VMEM((512, XY * TOK), BF),
            pltpu.VMEM((ZN, COL, UN), F32),
            pltpu.VMEM((ZN, COL, UN), BF),
            pltpu.VMEM((ZN, 16, UN), BF),
            pltpu.VMEM((ZN, 16, UN), BF),
            pltpu.VMEM((ZN, 16, UN), BF),
            pltpu.VMEM((ZN, 16, UN), BF),
            pltpu.VMEM((512, HALF), BF),
            pltpu.VMEM((TOK, UN), BF),
            pltpu.VMEM((ZN, 16, UN), BF),
            pltpu.VMEM((ZN, 16, UN), BF),
            pltpu.VMEM((TOK, UN), BF),
            pltpu.VMEM((512, TOK), BF),
            pltpu.VMEM((UN, UN), BF),
            pltpu.VMEM((UN, UN), BF),
            dma(()), dma(()), dma((2,)), dma((2, 10, 2)), dma(()), dma((2, 8, 2)),
            dma(()), dma(()), dma(()), dma(()),
            dma(()), dma(()), dma(()), dma((3,)),
            dma(()), dma((3,)), dma((6,)), dma((6,)),
        ],
        compiler_params=pltpu.CompilerParams(
            collective_id=0, has_side_effects=True, vmem_limit_bytes=56 * 1024 * 1024
        ),
    )(gate_pre, up_pre, grad_rot, grad_out, tables)
    return pl.pallas_call(
        last,
        out_shape=(
            jax.ShapeDtypeStruct((TOK, UN), BF),
            jax.ShapeDtypeStruct((TOK, UN), BF),
            jax.ShapeDtypeStruct((832, 512), BF),
        ),
        in_specs=[vmem] * 6,
        out_specs=(vmem, vmem, vmem),
    )(grad_gate, grad_up, summed, latent_weight, clip_codes[None, :], bits[None, :])


def solution(mesh):
    both = P("dp", "tensor")
    return jax.shard_map(
        local,
        mesh=mesh,
        in_specs=(both, both, both, both, both, P("tensor"), P("tensor")),
        out_specs=(both, both, both),
        check_vma=False,
    )
```

```python
import jax
import jax.numpy as jnp
import numpy as np
from jax import lax
from jax.experimental import pallas as pl
from jax.experimental.pallas import tpu as pltpu
from jax.sharding import PartitionSpec as P

HAD = 1024
NBLK = 26
MESH = pl.DeviceIdType.MESH
BF = jnp.bfloat16
F32 = jnp.float32

ZN = 16
XY = 16
TOK = 128
UN = 1664
COL = 32
HALF = 896


def local_table():
    table = np.array([[1.0]])
    for _ in range(6):
        table = np.block([[table, table], [table, -table]])
    table = np.kron(table / 8.0, np.eye(NBLK)).astype(jnp.bfloat16)
    order = np.concatenate([np.arange(832 * c + a, 832 * c + b) for a, b in ROWS for c in range(2)])
    return np.stack([table, table[:, order]])


def hint(value, multiple):
    return pl.multiple_of(value, multiple)


CHUNKS = ((0, 768), (768, 512), (1280, 384))
ROWS = ((0, 384), (384, 640), (640, 832))
PIECES = (
    ((0, 0, 0, 384, 0), (1, 1, 384, 384, 0)),
    ((2, 0, 768, 256, 384), (3, 1, 1024, 256, 384)),
    ((4, 0, 1280, 256, 640), (5, 1, 1408, 256, 640)),
)


def far_first(t):
    half = (t + 1) >> 1
    return (8 + half * (1 - 2 * (t & 1))) & 15


def rotate16(src, dst, first, width):
    def tile(t, carry):
        lanes = pl.ds(hint(t * 128, 128), 128)
        vals = [src[j, :, lanes].astype(F32) for j in range(16)]
        for bit in range(4):
            step = 1 << bit
            for j in range(16):
                if not j & step:
                    low, high = vals[j], vals[j | step]
                    vals[j], vals[j | step] = low + high, low - high
        for j in range(16):
            dst[j, :, lanes] = (vals[j] * 0.25).astype(BF)
        return carry

    lax.fori_loop(first // 128, (first + width) // 128, tile, 0)


def kernel(
    gate, up, grot, gout, tables, gg, gu, gw_out,
    acts, outs, part, send, other, own, got, turned, landed, hid, fin, fturn, fback,
    bt, table, ordered, load_sem, load_sem2, a_s, a_r, ring_s, ring_r, f_s, f_r, fb_s, fb_r, b_s, b_r, e_s, e_r, g_s, g_r, z_s, z_r,
):
    i = lax.axis_index("dp")
    z = lax.axis_index("tensor")
    c = i & 1
    xy = i >> 1
    x, y = xy >> 2, xy & 3
    k_me = z >> 1
    active = (z & 1) == c

    def remote(src, dst, ssem, rsem, dp, zz):
        return pltpu.make_async_remote_copy(
            src_ref=src, dst_ref=dst, send_sem=ssem, recv_sem=rsem,
            device_id=(dp, zz), device_id_type=MESH,
        )

    def load(n, dst, sem):
        def load_rows(t, carry):
            rows = pl.ds(hint(t * 128, 128), 128)
            pltpu.make_async_copy(tables.at[n, rows, :], dst.at[rows, :], sem).start()
            return carry

        lax.fori_loop(0, UN // 128, load_rows, 0)

    load(1, ordered, load_sem2)

    def taken(ref, sem):
        remote(ref, ref, load_sem, sem, i, z ^ 1).wait_recv()

    def gone(ref, sem):
        remote(ref, ref, sem, load_sem, i, z ^ 1).wait_send()

    barrier = pltpu.get_barrier_semaphore()

    def hail_z(off, carry):
        pl.semaphore_signal(barrier, inc=1, device_id=(i, (z + off) & 15), device_id_type=MESH)
        return carry

    def hail_xy(off, carry):
        pl.semaphore_signal(barrier, inc=1, device_id=((i + off) & 31, z), device_id_type=MESH)
        return carry

    lax.fori_loop(1, ZN, hail_z, 0)
    lax.fori_loop(1, 32, hail_xy, 0)

    pl.semaphore_wait(barrier, ZN - 1 + 31)

    def f_copy(k):
        rows = pl.ds(hint(16 * k, 16), 16)
        return remote(grot.at[rows, :], fin.at[z], f_s, f_r, i, 2 * k + c)

    def f_start(j, carry):
        half = (j + 1) >> 1
        k = (k_me + 4 + half * (1 - 2 * (j & 1))) & 7

        @pl.when(2 * k + c != z)
        def _():
            f_copy(k).start()

        return carry

    lax.fori_loop(0, 4, f_start, 0)

    for t in range(4):
        lanes = slice(128 * t, 128 * (t + 1))
        bt[lanes, :] = gout[:, lanes].astype(F32).T.astype(BF)

    def b_copy(off):
        peer = (xy + 7 * off) & 15
        return remote(
            bt.at[pl.ds(hint(COL * peer, COL), COL), :],
            outs.at[pl.ds(hint(COL * z, COL), COL), pl.ds(hint(TOK * xy, TOK), TOK)],
            b_s, b_r, 2 * peer + c, z,
        )

    def b_start(off, carry):
        b_copy(off).start()
        return carry

    lax.fori_loop(1, XY, b_start, 0)
    outs[pl.ds(hint(COL * z, COL), COL), pl.ds(hint(TOK * xy, TOK), TOK)] = bt[
        pl.ds(hint(COL * xy, COL), COL), :
    ]

    @pl.when(active)
    def _():
        fin[z] = grot[pl.ds(hint(16 * k_me, 16), 16), :]

    def make_hidden(t, carry):
        lanes = pl.ds(hint(t * 128, 128), 128)
        g = gate[:, lanes].astype(F32)
        u = up[:, lanes].astype(F32)
        hid[:, lanes] = (g * jax.nn.sigmoid(g) * u).astype(BF)
        return carry

    lax.fori_loop(0, UN // 128, make_hidden, 0)
    pltpu.make_async_copy(tables.at[1], ordered, load_sem2).wait()
    mine = pl.ds(hint(TOK * xy, TOK), TOK)

    def turn_hidden(t, carry):
        lanes = pl.ds(hint(t * 256, 256), 256)
        acts[mine, lanes] = jnp.dot(hid[...], ordered[:, lanes], preferred_element_type=F32).astype(BF)
        return carry

    lax.fori_loop(0, UN // 256, turn_hidden, 0)
    acts[mine, UN - 128 :] = jnp.dot(
        hid[...], ordered[:, UN - 128 :], preferred_element_type=F32
    ).astype(BF)

    COLS = (0, -1, 1, 2)

    def chip(h, p, q):
        return 4 * (p & 3) + (q & 3) if h == 0 else 4 * (q & 3) + (p & 3)

    def spot(h):
        return (x, y) if h == 0 else (y, x)

    def a_rows(h, blk, part):
        if part is None:
            return acts.at[pl.ds(hint(TOK * blk + 64 * h, 64), 64), :]
        return acts.at[pl.ds(hint(TOK * blk + 64 * h + 32 * part, 32), 32), :]

    def a_send(h, first_axis, blk, part, d, sem):
        p, q = spot(h)
        hop = 1 - 2 * d
        peer = chip(h, p + hop, q) if first_axis else chip(h, p, q + hop)
        ref = a_rows(h, blk, part)
        remote(ref, ref, a_s.at[h], a_r.at[h, sem, d], 2 * peer + c, z).start()

    def a_take(h, rows, d, sem):
        taken(acts.at[pl.ds(0, rows), :], a_r.at[h, sem, d])

    def first_near(h, d):
        a_send(h, True, chip(h, *spot(h)), None, d, 0)

    def first_far(h, d):
        p, q = spot(h)
        a_send(h, True, chip(h, p - 1 + 2 * d, q), d, d, 1)

    def second_near(h, j, d):
        p, q = spot(h)
        a_send(h, False, chip(h, p + COLS[j], q), None, d, 2 + j)

    def second_far(h, j, d):
        p, q = spot(h)
        a_send(h, False, chip(h, p + COLS[j], q - 1 + 2 * d), d, d, 6 + j)

    both = [(h, d) for d in range(2) for h in range(2)]
    for h, d in both:
        first_near(h, d)
    for h, d in both:
        second_near(h, 0, d)

    load(0, table, load_sem)

    def ring_copy(d, s, u):
        origin = (z + 16 - s if d == 0 else z + s) & 15
        ref = outs.at[pl.ds(hint(COL * origin + 16 * u, 16), 16), :]
        peer = (z + 1 if d == 0 else z + 15) & 15
        return remote(ref, ref, ring_s, ring_r.at[d, s, u], i, peer)

    def ring_wait(d, s, u):
        taken(outs.at[pl.ds(0, 16), :], ring_r.at[d, s, u])

    def ring_step(s):
        for u in range(2):
            for d in range(2):
                ring_wait(d, s - 1, u)
                if s < 7 or u == d:
                    ring_copy(d, s, u).start()

    taken(outs.at[pl.ds(0, COL), pl.ds(0, TOK * (XY - 1))], b_r)
    for u in range(2):
        for d in range(2):
            ring_copy(d, 0, u).start()

    f_start(4, 0)
    ring_step(1)
    for h, d in both:
        a_take(h, 64, d, 0)
        first_far(h, d)
    for h, d in both:
        second_near(h, 1, d)
    f_start(5, 0)
    ring_step(2)
    for h, d in both:
        a_take(h, 64, d, 2)
        second_far(h, 0, d)
    for h, d in both:
        second_near(h, 2, d)
    f_start(6, 0)
    ring_step(3)
    for h, d in both:
        a_take(h, 32, d, 1)
    for h, d in both:
        second_near(h, 3, d)
    f_start(7, 0)
    ring_step(4)
    for j in range(1, 3):
        for h, d in both:
            a_take(h, 64, d, 2 + j)
            second_far(h, j, d)
        ring_step(4 + j)

    def fb_copy(dest):
        return remote(
            fturn.at[dest], fback.at[pl.ds(hint(16 * k_me, 16), 16), :],
            fb_s, fb_r, i, dest,
        )

    @pl.when(active)
    def _():
        taken(fin.at[pl.ds(0, ZN - 1)], f_r)
        rotate16(fin, fturn, 0, UN)

        def fb_start(t, carry):
            fb_copy((z + far_first(t)) & 15).start()
            return carry

        lax.fori_loop(0, ZN - 1, fb_start, 0)
        fback[pl.ds(hint(16 * k_me, 16), 16), :] = fturn[z]

    for h, d in both:
        a_take(h, 64, d, 5)
        second_far(h, 3, d)
    ring_step(7)
    for d in range(2):
        ring_wait(d, 7, d)
    for j in range(4):
        for h, d in both:
            a_take(h, 32, d, 6 + j)

    def product(lanes, width):
        tile = jnp.dot(outs[...], acts[:, lanes], preferred_element_type=F32)
        tile = tile.reshape(ZN, COL, width)
        part[:, :, lanes] = tile
        send[:, :, lanes] = tile.astype(BF)

    def product_chunk(q):
        first, width = CHUNKS[q]

        def product_tile(t, carry):
            product(pl.ds(hint(first + t * 256, 128), 256), 256)
            return carry

        lax.fori_loop(0, width // 256, product_tile, 0)
        if width % 256:
            product(pl.ds(first + width - 128, 128), 128)

    def swap(q):
        lanes = pl.ds(*CHUNKS[q])
        return remote(
            send.at[:, pl.ds(hint(16 * (1 - c), 16), 16), lanes], other.at[:, :, lanes],
            e_s, e_r.at[q], i ^ 1, z,
        )

    def g_copy(q, dest):
        lanes = pl.ds(*CHUNKS[q])
        return remote(
            own.at[dest, :, lanes], got.at[z, :, lanes], g_s, g_r.at[q], i, dest
        )

    def share(q):
        lanes = pl.ds(*CHUNKS[q])
        taken(other.at[:, :, lanes], e_r.at[q])

        def add_send(t, carry):
            j = (z + far_first(t)) & 15
            own[j, :, lanes] = (
                part[j, pl.ds(hint(16 * c, 16), 16), lanes] + other[j, :, lanes].astype(F32)
            ).astype(BF)

            @pl.when(t < ZN - 1)
            def _():
                g_copy(q, j).start()

            return carry

        lax.fori_loop(0, ZN, add_send, 0)
        got[z, :, lanes] = own[z, :, lanes]

    product_chunk(0)
    swap(0).start()
    product_chunk(1)
    swap(1).start()
    share(0)
    product_chunk(2)
    swap(2).start()
    share(1)
    share(2)

    @pl.when(active)
    def _():
        taken(fback.at[pl.ds(0, TOK - 16), :], fb_r)

    @pl.when(jnp.logical_not(active))
    def _():
        taken(fback, fb_r)

    def finish(lanes):
        gh = jnp.dot(fback[...], table[:, lanes], preferred_element_type=F32)
        g = gate[:, lanes].astype(F32)
        u = up[:, lanes].astype(F32)
        sg = jax.nn.sigmoid(g)
        gg[:, lanes] = (gh * u * sg * (1.0 + g * (1.0 - sg))).astype(BF)
        gu[:, lanes] = (gh * g * sg).astype(BF)

    pltpu.make_async_copy(tables.at[0], table, load_sem).wait()

    def finish_tile(t, carry):
        finish(pl.ds(hint(t * 256, 256), 256))
        return carry

    lax.fori_loop(0, UN // 256, finish_tile, 0)
    finish(pl.ds(UN - 128, 128))

    def z_copy(piece, peer):
        p, core, first, width, at = piece
        return remote(
            turned.at[peer, :, pl.ds(first, width)],
            landed.at[pl.ds(hint(COL * xy + 16 * c, 16), 16), pl.ds(at, width)],
            z_s.at[p], z_r.at[p], 2 * peer + core, z,
        )

    def g_wait_chunk(q):
        lanes = pl.ds(*CHUNKS[q])

        taken(got.at[pl.ds(0, ZN - 1), :, lanes], g_r.at[q])

    def z_send(piece):
        p, core, first, width, at = piece

        def z_start(off, carry):
            z_copy(piece, (xy + 7 * off) & 15).start()
            return carry

        lax.fori_loop(1, XY, z_start, 0)

        @pl.when(c == core)
        def _():
            landed[pl.ds(hint(COL * xy + 16 * c, 16), 16), at : at + width] = turned[
                xy, :, first : first + width
            ]

        @pl.when(c != core)
        def _():
            z_copy(piece, xy).start()

    def z_take(piece):
        p, core, first, width, at = piece

        @pl.when(c == core)
        def _():
            taken(landed.at[pl.ds(0, 496), pl.ds(at, width)], z_r.at[p])

            def flip(t):
                return landed[:, at + 128 * t : at + 128 * (t + 1)].astype(F32).T.astype(BF)

            if width == 256 and at == 640:
                one, two = flip(0), flip(1)
                if core == 0:
                    gw_out[640:768, :] = one
                    gw_out[768:832, :] = two[:64]
                else:
                    gw_out[640:704, :] = one[64:]
                    gw_out[704:832, :] = two
            else:
                for t in range(width // 128):
                    gw_out[at + 128 * t : at + 128 * (t + 1), :] = flip(t)

    for q in range(3):
        g_wait_chunk(q)
        rotate16(got, turned, *CHUNKS[q])
        for piece in PIECES[q]:
            z_send(piece)
        if q:
            for piece in PIECES[q - 1]:
                z_take(piece)
    for piece in PIECES[2]:
        z_take(piece)

    for h in range(2):
        gone(acts.at[pl.ds(0, 64 * 15), :], a_s.at[h])
    gone(outs.at[pl.ds(0, COL * 15), :], ring_s)
    gone(outs.at[pl.ds(0, COL), pl.ds(0, TOK * (XY - 1))], b_s)

    @pl.when(active)
    def _():
        gone(grot.at[pl.ds(0, TOK - 16), :], f_s)
        gone(fturn.at[pl.ds(0, ZN - 1)], fb_s)

    @pl.when(jnp.logical_not(active))
    def _():
        gone(grot, f_s)

    gone(other, e_s)
    gone(own.at[pl.ds(0, ZN - 1)], g_s)
    for pieces in PIECES:
        for p, core, first, width, at in pieces:

            @pl.when(c == core)
            def _():
                gone(turned.at[pl.ds(0, XY - 1), :, pl.ds(first, width)], z_s.at[p])

            @pl.when(c != core)
            def _():
                gone(turned.at[:, :, pl.ds(first, width)], z_s.at[p])


def last(gg_in, gu_in, summed, latent, codes, bits, gg, gu, gw):
    levels = jnp.left_shift(jnp.int32(1), bits[...] - 1) - 1
    limit = codes[...].astype(F32) * levels.astype(F32) / 65536.0

    def mask(t, carry):
        rows = pl.ds(hint(t * 64, 64), 64)
        inside = jnp.abs(latent[rows, :].astype(F32)) <= limit
        gw[rows, :] = jnp.where(inside, summed[rows, :].astype(F32), 0.0).astype(BF)
        return carry

    lax.fori_loop(0, 13, mask, 0)
    gg[...] = gg_in[...]
    gu[...] = gu_in[...]


def local(gate_pre, up_pre, grad_rot, grad_out, latent_weight, clip_codes, bits):
    tables = jnp.asarray(local_table())
    vmem = pl.BlockSpec(memory_space=pltpu.VMEM)
    hbm = pl.BlockSpec(memory_space=pl.ANY)
    dma = pltpu.SemaphoreType.DMA
    grad_gate, grad_up, summed = pl.pallas_call(
        kernel,
        out_shape=(
            jax.ShapeDtypeStruct((TOK, UN), BF),
            jax.ShapeDtypeStruct((TOK, UN), BF),
            jax.ShapeDtypeStruct((832, 512), BF),
        ),
        in_specs=[vmem] * 4 + [hbm],
        out_specs=(vmem, vmem, vmem),
        scratch_shapes=[
            pltpu.VMEM((XY * TOK, UN), BF),
            pltpu.VMEM((512, XY * TOK), BF),
            pltpu.VMEM((ZN, COL, UN), F32),
            pltpu.VMEM((ZN, COL, UN), BF),
            pltpu.VMEM((ZN, 16, UN), BF),
            pltpu.VMEM((ZN, 16, UN), BF),
            pltpu.VMEM((ZN, 16, UN), BF),
            pltpu.VMEM((ZN, 16, UN), BF),
            pltpu.VMEM((512, HALF), BF),
            pltpu.VMEM((TOK, UN), BF),
            pltpu.VMEM((ZN, 16, UN), BF),
            pltpu.VMEM((ZN, 16, UN), BF),
            pltpu.VMEM((TOK, UN), BF),
            pltpu.VMEM((512, TOK), BF),
            pltpu.VMEM((UN, UN), BF),
            pltpu.VMEM((UN, UN), BF),
            dma(()), dma(()), dma((2,)), dma((2, 10, 2)), dma(()), dma((2, 8, 2)),
            dma(()), dma(()), dma(()), dma(()),
            dma(()), dma(()), dma(()), dma((3,)),
            dma(()), dma((3,)), dma((6,)), dma((6,)),
        ],
        compiler_params=pltpu.CompilerParams(
            collective_id=0, has_side_effects=True, vmem_limit_bytes=56 * 1024 * 1024
        ),
    )(gate_pre, up_pre, grad_rot, grad_out, tables)
    return pl.pallas_call(
        last,
        out_shape=(
            jax.ShapeDtypeStruct((TOK, UN), BF),
            jax.ShapeDtypeStruct((TOK, UN), BF),
            jax.ShapeDtypeStruct((832, 512), BF),
        ),
        in_specs=[vmem] * 6,
        out_specs=(vmem, vmem, vmem),
    )(grad_gate, grad_up, summed, latent_weight, clip_codes[None, :], bits[None, :])


def solution(mesh):
    both = P("dp", "tensor")
    return jax.shard_map(
        local,
        mesh=mesh,
        in_specs=(both, both, both, both, both, P("tensor"), P("tensor")),
        out_specs=(both, both, both),
        check_vma=False,
    )
```

```python
import jax
import jax.numpy as jnp
import numpy as np
from jax import lax
from jax.experimental import pallas as pl
from jax.experimental.pallas import tpu as pltpu
from jax.sharding import PartitionSpec as P

HAD = 1024
NBLK = 26
MESH = pl.DeviceIdType.MESH
BF = jnp.bfloat16
F32 = jnp.float32

ZN = 16
XY = 16
TOK = 128
UN = 1664
COL = 32
HALF = 896


def local_table():
    table = np.array([[1.0]])
    for _ in range(6):
        table = np.block([[table, table], [table, -table]])
    table = np.kron(table / 8.0, np.eye(NBLK)).astype(jnp.bfloat16)
    order = np.concatenate([np.arange(832 * c + a, 832 * c + b) for a, b in ROWS for c in range(2)])
    return np.stack([table, table[:, order]])


def hint(value, multiple):
    return pl.multiple_of(value, multiple)


CHUNKS = ((0, 768), (768, 768), (1536, 128))
ROWS = ((0, 384), (384, 768), (768, 832))
PIECES = (
    ((0, 0, 0, 384, 0), (1, 1, 384, 384, 0)),
    ((2, 0, 768, 384, 384), (3, 1, 1152, 384, 384)),
    ((4, 0, 1536, 128, 768), (5, 1, 1536, 128, 768)),
)


def far_first(t):
    half = (t + 1) >> 1
    return (8 + half * (1 - 2 * (t & 1))) & 15


def rotate16(src, dst, first, width):
    def tile(t, carry):
        lanes = pl.ds(hint(t * 128, 128), 128)
        vals = [src[j, :, lanes].astype(F32) for j in range(16)]
        for bit in range(4):
            step = 1 << bit
            for j in range(16):
                if not j & step:
                    low, high = vals[j], vals[j | step]
                    vals[j], vals[j | step] = low + high, low - high
        for j in range(16):
            dst[j, :, lanes] = (vals[j] * 0.25).astype(BF)
        return carry

    lax.fori_loop(first // 128, (first + width) // 128, tile, 0)


def kernel(
    gate, up, grot, gout, tables, gg, gu, gw_out,
    acts, outs, part, send, other, own, got, turned, landed, hid, fin, fturn, fback,
    bt, table, ordered, load_sem, load_sem2, a_s, a_r, ring_s, ring_r, f_s, f_r, fb_s, fb_r, b_s, b_r, e_s, e_r, g_s, g_r, z_s, z_r,
):
    i = lax.axis_index("dp")
    z = lax.axis_index("tensor")
    c = i & 1
    xy = i >> 1
    x, y = xy >> 2, xy & 3
    k_me = z >> 1
    active = (z & 1) == c

    def remote(src, dst, ssem, rsem, dp, zz):
        return pltpu.make_async_remote_copy(
            src_ref=src, dst_ref=dst, send_sem=ssem, recv_sem=rsem,
            device_id=(dp, zz), device_id_type=MESH,
        )

    def load(n, dst, sem):
        def load_rows(t, carry):
            rows = pl.ds(hint(t * 128, 128), 128)
            pltpu.make_async_copy(tables.at[n, rows, :], dst.at[rows, :], sem).start()
            return carry

        lax.fori_loop(0, UN // 128, load_rows, 0)

    load(1, ordered, load_sem2)

    def taken(ref, sem):
        remote(ref, ref, load_sem, sem, i, z ^ 1).wait_recv()

    def gone(ref, sem):
        remote(ref, ref, sem, load_sem, i, z ^ 1).wait_send()

    barrier = pltpu.get_barrier_semaphore()

    def hail_z(off, carry):
        pl.semaphore_signal(barrier, inc=1, device_id=(i, (z + off) & 15), device_id_type=MESH)
        return carry

    def hail_xy(off, carry):
        pl.semaphore_signal(barrier, inc=1, device_id=((i + off) & 31, z), device_id_type=MESH)
        return carry

    lax.fori_loop(1, ZN, hail_z, 0)
    lax.fori_loop(1, 32, hail_xy, 0)

    pl.semaphore_wait(barrier, ZN - 1 + 31)

    def f_copy(k):
        rows = pl.ds(hint(16 * k, 16), 16)
        return remote(grot.at[rows, :], fin.at[z], f_s, f_r, i, 2 * k + c)

    def f_start(j, carry):
        half = (j + 1) >> 1
        k = (k_me + 4 + half * (1 - 2 * (j & 1))) & 7

        @pl.when(2 * k + c != z)
        def _():
            f_copy(k).start()

        return carry

    lax.fori_loop(0, 3, f_start, 0)

    for t in range(4):
        lanes = slice(128 * t, 128 * (t + 1))
        bt[lanes, :] = gout[:, lanes].astype(F32).T.astype(BF)

    def b_copy(off):
        peer = (xy + 7 * off) & 15
        return remote(
            bt.at[pl.ds(hint(COL * peer, COL), COL), :],
            outs.at[pl.ds(hint(COL * z, COL), COL), pl.ds(hint(TOK * xy, TOK), TOK)],
            b_s, b_r, 2 * peer + c, z,
        )

    def b_start(off, carry):
        b_copy(off).start()
        return carry

    lax.fori_loop(1, XY, b_start, 0)
    outs[pl.ds(hint(COL * z, COL), COL), pl.ds(hint(TOK * xy, TOK), TOK)] = bt[
        pl.ds(hint(COL * xy, COL), COL), :
    ]

    @pl.when(active)
    def _():
        fin[z] = grot[pl.ds(hint(16 * k_me, 16), 16), :]

    def make_hidden(t, carry):
        lanes = pl.ds(hint(t * 128, 128), 128)
        g = gate[:, lanes].astype(F32)
        u = up[:, lanes].astype(F32)
        hid[:, lanes] = (g * jax.nn.sigmoid(g) * u).astype(BF)
        return carry

    lax.fori_loop(0, UN // 128, make_hidden, 0)
    pltpu.make_async_copy(tables.at[1], ordered, load_sem2).wait()
    mine = pl.ds(hint(TOK * xy, TOK), TOK)

    def turn_hidden(t, carry):
        lanes = pl.ds(hint(t * 256, 256), 256)
        acts[mine, lanes] = jnp.dot(hid[...], ordered[:, lanes], preferred_element_type=F32).astype(BF)
        return carry

    lax.fori_loop(0, UN // 256, turn_hidden, 0)
    acts[mine, UN - 128 :] = jnp.dot(
        hid[...], ordered[:, UN - 128 :], preferred_element_type=F32
    ).astype(BF)

    COLS = (0, -1, 1, 2)

    def chip(h, p, q):
        return 4 * (p & 3) + (q & 3) if h == 0 else 4 * (q & 3) + (p & 3)

    def spot(h):
        return (x, y) if h == 0 else (y, x)

    def a_rows(h, blk, part):
        if part is None:
            return acts.at[pl.ds(hint(TOK * blk + 64 * h, 64), 64), :]
        return acts.at[pl.ds(hint(TOK * blk + 64 * h + 32 * part, 32), 32), :]

    def a_send(h, first_axis, blk, part, d, sem):
        p, q = spot(h)
        hop = 1 - 2 * d
        peer = chip(h, p + hop, q) if first_axis else chip(h, p, q + hop)
        ref = a_rows(h, blk, part)
        remote(ref, ref, a_s.at[h], a_r.at[h, sem, d], 2 * peer + c, z).start()

    def a_take(h, rows, d, sem):
        taken(acts.at[pl.ds(0, rows), :], a_r.at[h, sem, d])

    def first_near(h, d):
        a_send(h, True, chip(h, *spot(h)), None, d, 0)

    def first_far(h, d):
        p, q = spot(h)
        a_send(h, True, chip(h, p - 1 + 2 * d, q), d, d, 1)

    def second_near(h, j, d):
        p, q = spot(h)
        a_send(h, False, chip(h, p + COLS[j], q), None, d, 2 + j)

    def second_far(h, j, d):
        p, q = spot(h)
        a_send(h, False, chip(h, p + COLS[j], q - 1 + 2 * d), d, d, 6 + j)

    both = [(h, d) for d in range(2) for h in range(2)]
    for h, d in both:
        first_near(h, d)
    for h, d in both:
        second_near(h, 0, d)

    load(0, table, load_sem)

    def ring_copy(d, s, u):
        origin = (z + 16 - s if d == 0 else z + s) & 15
        ref = outs.at[pl.ds(hint(COL * origin + 16 * u, 16), 16), :]
        peer = (z + 1 if d == 0 else z + 15) & 15
        return remote(ref, ref, ring_s, ring_r.at[d, s, u], i, peer)

    def ring_wait(d, s, u):
        taken(outs.at[pl.ds(0, 16), :], ring_r.at[d, s, u])

    def ring_step(s):
        for u in range(2):
            for d in range(2):
                ring_wait(d, s - 1, u)
                if s < 7 or u == d:
                    ring_copy(d, s, u).start()

    taken(outs.at[pl.ds(0, COL), pl.ds(0, TOK * (XY - 1))], b_r)
    for u in range(2):
        for d in range(2):
            ring_copy(d, 0, u).start()

    f_start(3, 0)
    ring_step(1)
    for h, d in both:
        a_take(h, 64, d, 0)
        first_far(h, d)
    for h, d in both:
        second_near(h, 1, d)
    f_start(4, 0)
    ring_step(2)
    for h, d in both:
        a_take(h, 64, d, 2)
        second_far(h, 0, d)
    for h, d in both:
        second_near(h, 2, d)
    f_start(5, 0)
    ring_step(3)
    for h, d in both:
        a_take(h, 32, d, 1)
    for h, d in both:
        second_near(h, 3, d)
    f_start(6, 0)
    ring_step(4)
    for j in range(1, 4):
        for h, d in both:
            a_take(h, 64, d, 2 + j)
            second_far(h, j, d)
        if j == 1:
            f_start(7, 0)
        ring_step(4 + j)
    def fb_copy(dest):
        return remote(
            fturn.at[dest], fback.at[pl.ds(hint(16 * k_me, 16), 16), :],
            fb_s, fb_r, i, dest,
        )

    @pl.when(active)
    def _():
        taken(fin.at[pl.ds(0, ZN - 1)], f_r)
        rotate16(fin, fturn, 0, UN)

        def fb_start(t, carry):
            fb_copy((z + far_first(t)) & 15).start()
            return carry

        lax.fori_loop(0, ZN - 1, fb_start, 0)
        fback[pl.ds(hint(16 * k_me, 16), 16), :] = fturn[z]

    for d in range(2):
        ring_wait(d, 7, d)
    for j in range(4):
        for h, d in both:
            a_take(h, 32, d, 6 + j)

    def product(lanes, width):
        tile = jnp.dot(outs[...], acts[:, lanes], preferred_element_type=F32)
        tile = tile.reshape(ZN, COL, width)
        part[:, :, lanes] = tile
        send[:, :, lanes] = tile.astype(BF)

    def product_chunk(q):
        first, width = CHUNKS[q]

        def product_tile(t, carry):
            product(pl.ds(hint(first + t * 256, 128), 256), 256)
            return carry

        lax.fori_loop(0, width // 256, product_tile, 0)
        if width % 256:
            product(pl.ds(first + width - 128, 128), 128)

    def swap(q):
        lanes = pl.ds(*CHUNKS[q])
        return remote(
            send.at[:, pl.ds(hint(16 * (1 - c), 16), 16), lanes], other.at[:, :, lanes],
            e_s, e_r.at[q], i ^ 1, z,
        )

    def g_copy(q, dest):
        lanes = pl.ds(*CHUNKS[q])
        return remote(
            own.at[dest, :, lanes], got.at[z, :, lanes], g_s, g_r.at[q], i, dest
        )

    def share(q):
        lanes = pl.ds(*CHUNKS[q])
        taken(other.at[:, :, lanes], e_r.at[q])

        def add_send(t, carry):
            j = (z + far_first(t)) & 15
            own[j, :, lanes] = (
                part[j, pl.ds(hint(16 * c, 16), 16), lanes] + other[j, :, lanes].astype(F32)
            ).astype(BF)

            @pl.when(t < ZN - 1)
            def _():
                g_copy(q, j).start()

            return carry

        lax.fori_loop(0, ZN, add_send, 0)
        got[z, :, lanes] = own[z, :, lanes]

    product_chunk(0)
    swap(0).start()
    product_chunk(1)
    swap(1).start()
    share(0)
    product_chunk(2)
    swap(2).start()
    share(1)
    share(2)

    @pl.when(active)
    def _():
        taken(fback.at[pl.ds(0, TOK - 16), :], fb_r)

    @pl.when(jnp.logical_not(active))
    def _():
        taken(fback, fb_r)

    def finish(lanes):
        gh = jnp.dot(fback[...], table[:, lanes], preferred_element_type=F32)
        g = gate[:, lanes].astype(F32)
        u = up[:, lanes].astype(F32)
        sg = jax.nn.sigmoid(g)
        gg[:, lanes] = (gh * u * sg * (1.0 + g * (1.0 - sg))).astype(BF)
        gu[:, lanes] = (gh * g * sg).astype(BF)

    pltpu.make_async_copy(tables.at[0], table, load_sem).wait()

    def finish_tile(t, carry):
        finish(pl.ds(hint(t * 256, 256), 256))
        return carry

    lax.fori_loop(0, UN // 256, finish_tile, 0)
    finish(pl.ds(UN - 128, 128))

    def z_copy(piece, peer):
        p, core, first, width, at = piece
        return remote(
            turned.at[peer, :, pl.ds(first, width)],
            landed.at[pl.ds(hint(COL * xy + 16 * c, 16), 16), pl.ds(at, width)],
            z_s.at[p], z_r.at[p], 2 * peer + core, z,
        )

    def g_wait_chunk(q):
        lanes = pl.ds(*CHUNKS[q])

        taken(got.at[pl.ds(0, ZN - 1), :, lanes], g_r.at[q])

    def z_send(piece):
        p, core, first, width, at = piece

        def z_start(off, carry):
            z_copy(piece, (xy + 7 * off) & 15).start()
            return carry

        lax.fori_loop(1, XY, z_start, 0)

        @pl.when(c == core)
        def _():
            landed[pl.ds(hint(COL * xy + 16 * c, 16), 16), at : at + width] = turned[
                xy, :, first : first + width
            ]

        @pl.when(c != core)
        def _():
            z_copy(piece, xy).start()

    def z_take(piece):
        p, core, first, width, at = piece

        @pl.when(c == core)
        def _():
            taken(landed.at[pl.ds(0, 496), pl.ds(at, width)], z_r.at[p])

            def flip(t):
                return landed[:, at + 128 * t : at + 128 * (t + 1)].astype(F32).T.astype(BF)

            if at == 768:
                gw_out[768:832, :] = flip(0)[64 * core : 64 * core + 64]
            else:
                for t in range(width // 128):
                    gw_out[at + 128 * t : at + 128 * (t + 1), :] = flip(t)

    for q in range(3):
        g_wait_chunk(q)
        rotate16(got, turned, *CHUNKS[q])
        for piece in PIECES[q]:
            z_send(piece)
        if q:
            for piece in PIECES[q - 1]:
                z_take(piece)
    for piece in PIECES[2]:
        z_take(piece)

    for h in range(2):
        gone(acts.at[pl.ds(0, 64 * 15), :], a_s.at[h])
    gone(outs.at[pl.ds(0, COL * 15), :], ring_s)
    gone(outs.at[pl.ds(0, COL), pl.ds(0, TOK * (XY - 1))], b_s)

    @pl.when(active)
    def _():
        gone(grot.at[pl.ds(0, TOK - 16), :], f_s)
        gone(fturn.at[pl.ds(0, ZN - 1)], fb_s)

    @pl.when(jnp.logical_not(active))
    def _():
        gone(grot, f_s)

    gone(other, e_s)
    gone(own.at[pl.ds(0, ZN - 1)], g_s)
    for pieces in PIECES:
        for p, core, first, width, at in pieces:

            @pl.when(c == core)
            def _():
                gone(turned.at[pl.ds(0, XY - 1), :, pl.ds(first, width)], z_s.at[p])

            @pl.when(c != core)
            def _():
                gone(turned.at[:, :, pl.ds(first, width)], z_s.at[p])


def last(gg_in, gu_in, summed, latent, codes, bits, gg, gu, gw):
    levels = jnp.left_shift(jnp.int32(1), bits[...] - 1) - 1
    limit = codes[...].astype(F32) * levels.astype(F32) / 65536.0

    def mask(t, carry):
        rows = pl.ds(hint(t * 64, 64), 64)
        inside = jnp.abs(latent[rows, :].astype(F32)) <= limit
        gw[rows, :] = jnp.where(inside, summed[rows, :].astype(F32), 0.0).astype(BF)
        return carry

    lax.fori_loop(0, 13, mask, 0)
    gg[...] = gg_in[...]
    gu[...] = gu_in[...]


def local(gate_pre, up_pre, grad_rot, grad_out, latent_weight, clip_codes, bits):
    tables = jnp.asarray(local_table())
    vmem = pl.BlockSpec(memory_space=pltpu.VMEM)
    hbm = pl.BlockSpec(memory_space=pl.ANY)
    dma = pltpu.SemaphoreType.DMA
    grad_gate, grad_up, summed = pl.pallas_call(
        kernel,
        out_shape=(
            jax.ShapeDtypeStruct((TOK, UN), BF),
            jax.ShapeDtypeStruct((TOK, UN), BF),
            jax.ShapeDtypeStruct((832, 512), BF),
        ),
        in_specs=[vmem] * 4 + [hbm],
        out_specs=(vmem, vmem, vmem),
        scratch_shapes=[
            pltpu.VMEM((XY * TOK, UN), BF),
            pltpu.VMEM((512, XY * TOK), BF),
            pltpu.VMEM((ZN, COL, UN), F32),
            pltpu.VMEM((ZN, COL, UN), BF),
            pltpu.VMEM((ZN, 16, UN), BF),
            pltpu.VMEM((ZN, 16, UN), BF),
            pltpu.VMEM((ZN, 16, UN), BF),
            pltpu.VMEM((ZN, 16, UN), BF),
            pltpu.VMEM((512, HALF), BF),
            pltpu.VMEM((TOK, UN), BF),
            pltpu.VMEM((ZN, 16, UN), BF),
            pltpu.VMEM((ZN, 16, UN), BF),
            pltpu.VMEM((TOK, UN), BF),
            pltpu.VMEM((512, TOK), BF),
            pltpu.VMEM((UN, UN), BF),
            pltpu.VMEM((UN, UN), BF),
            dma(()), dma(()), dma((2,)), dma((2, 10, 2)), dma(()), dma((2, 8, 2)),
            dma(()), dma(()), dma(()), dma(()),
            dma(()), dma(()), dma(()), dma((3,)),
            dma(()), dma((3,)), dma((6,)), dma((6,)),
        ],
        compiler_params=pltpu.CompilerParams(
            collective_id=0, has_side_effects=True, vmem_limit_bytes=56 * 1024 * 1024
        ),
    )(gate_pre, up_pre, grad_rot, grad_out, tables)
    return pl.pallas_call(
        last,
        out_shape=(
            jax.ShapeDtypeStruct((TOK, UN), BF),
            jax.ShapeDtypeStruct((TOK, UN), BF),
            jax.ShapeDtypeStruct((832, 512), BF),
        ),
        in_specs=[vmem] * 6,
        out_specs=(vmem, vmem, vmem),
    )(grad_gate, grad_up, summed, latent_weight, clip_codes[None, :], bits[None, :])


def solution(mesh):
    both = P("dp", "tensor")
    return jax.shard_map(
        local,
        mesh=mesh,
        in_specs=(both, both, both, both, both, P("tensor"), P("tensor")),
        out_specs=(both, both, both),
        check_vma=False,
    )
```
